128 devices in a mesh: fsdp: 64 (over y, z_lo, x, core), tp: 2 (over z_hi).
Axes of the slice: x: 4, y: 4, z: 4 (z_hi: 2, z_lo: 2; z = z_hi * 2 + z_lo), core: 2. Of those that a mesh axis runs over, the one named last changes fastest.
Arguments:
- x_in: bfloat16 [16384, 1024], P(('fsdp', 'tp')), may hold values from -6 to 6
- cotangent: bfloat16 [16384, 1024], P(('fsdp', 'tp')), may hold values from -6 to 6
- seq_lengths: int32 [64, 4], P('fsdp'), may hold values from 1 to 253, as said below
- gain_in: bfloat16 [2, 1024], replicated, may hold values from 0.5 to 1.5
- w_zx: bfloat16 [2, 1024, 2, 2048], P(None, 'fsdp', None, 'tp'), may hold values from -0.1875 to 0.1875
- w_bc: bfloat16 [2, 1024, 256], P(None, 'fsdp'), may hold values from -0.1875 to 0.1875
- w_dt: bfloat16 [2, 1024, 32], P(None, 'fsdp', 'tp'), may hold values from -0.1875 to 0.1875
- conv_x: bfloat16 [2, 4, 2048], P(None, None, 'tp'), may hold values from -0.5 to 0.5
- conv_bc: bfloat16 [2, 4, 256], replicated, may hold values from -0.5 to 0.5
- bias_x: bfloat16 [2, 2048], P(None, 'tp'), may hold values from -0.5 to 0.5
- bias_bc: bfloat16 [2, 256], replicated, may hold values from -0.5 to 0.5
- dt_bias: bfloat16 [2, 32], P(None, 'tp'), may hold values from -6 to -2
- a_log: bfloat16 [2, 32], P(None, 'tp'), may hold values from 0 to 2.5
- skip: bfloat16 [2, 32], P(None, 'tp'), may hold values from 0.5 to 1.5
- gain_gate: bfloat16 [2, 2048], P(None, 'tp'), may hold values from 0.5 to 1.5
- w_out: bfloat16 [2, 2048, 1024], P(None, 'tp', 'fsdp'), may hold values from -0.125 to 0.125
Outputs:
- act_out: bfloat16 [16384, 1024], P(('fsdp', 'tp'))
- grad_in: float32 [16384, 1024], P(('fsdp', 'tp'))
- grad_gain_in: float32 [2, 1024], replicated
- grad_w_zx: float32 [2, 1024, 2, 2048], P(None, 'fsdp', None, 'tp')
- grad_w_bc: float32 [2, 1024, 256], P(None, 'fsdp')
- grad_w_dt: float32 [2, 1024, 32], P(None, 'fsdp', 'tp')
- grad_conv_x: float32 [2, 4, 2048], P(None, None, 'tp')
- grad_conv_bc: float32 [2, 4, 256], replicated
- grad_bias_x: float32 [2, 2048], P(None, 'tp')
- grad_bias_bc: float32 [2, 256], replicated
- grad_dt_bias: float32 [2, 32], P(None, 'tp')
- grad_a_log: float32 [2, 32], P(None, 'tp')
- grad_skip: float32 [2, 32], P(None, 'tp')
- grad_gain_gate: float32 [2, 2048], P(None, 'tp')
- grad_w_out: float32 [2, 2048, 1024], P(None, 'tp', 'fsdp')
The draws below stay inside these ranges and needn't reach their ends.
Inputs may be any that keep to these rules, and one draw needn't show every extreme that they name: `seq_lengths`: row g lists the lengths of the 4 sequences packed in order from the first row of group g; rows after their sum are padding. Every row sums to 192 or more and some row sums to 256; in every row one sequence holds both rows 127 and 128.
All inputs are finite; a program needn't handle non-finite values.
Results may differ from the reference program's by a relative error of at most 0.03.
Values may be sent and summed in bfloat16 or wider, within the bound.
A program may use at most 192 MiB of HBM per device.

```python
import jax
import jax.numpy as jnp
from jax import lax

D = 1024
HEADS = 32
STATE = 128
CONV = 4
SPAN = 256
SEQS = 4
LAYERS = 2
INNER = 2048
GRP_TOK = 256
TOKENS = 16384
N_FSDP = 64


def draw_seq_lengths(key, part):
    key = jax.random.fold_in(key, 11)
    half = GRP_TOK // 2
    keys = jax.random.split(key, 5)
    slack = jax.random.randint(keys[0], (N_FSDP,), 0, half // 2 + 1)
    full_group = jax.random.randint(keys[1], (), 0, N_FSDP)
    is_full = jnp.arange(N_FSDP) == full_group
    slack = jnp.where(is_full, 0, slack)
    filled = GRP_TOK - slack
    first_cut = jax.random.randint(keys[2], (N_FSDP,), 1, half - half // 4)
    second_cut = half + jax.random.randint(keys[3], (N_FSDP,), 1, half // 4 + 1)
    third_cut = second_cut + jax.random.randint(keys[4], (N_FSDP,), 1, filled - second_cut)
    first_cut = jnp.where(is_full, 1, first_cut)
    second_cut = jnp.where(is_full, GRP_TOK - 2, second_cut)
    third_cut = jnp.where(is_full, GRP_TOK - 1, third_cut)
    lengths = jnp.stack([first_cut, second_cut - first_cut, third_cut - second_cut, filled - third_cut], axis=1)
    return lengths.astype(jnp.int32)


def steps_of(key, dims, pieces, smallest, high):
    factor_of, own = 1.0, jax.random.fold_in(key, 6)
    for dim, parts in pieces:
        draws = jnp.exp(jax.random.uniform(jax.random.fold_in(own, dim), (parts,), jnp.float32, smallest / len(pieces), high / len(pieces)))
        factor_of = factor_of * jnp.repeat(draws, dims[dim] // parts).reshape([-1 if axis == dim else 1 for axis in range(len(dims))])
    return factor_of


def normal_values(stream_key, dims, spread, reach, shards=(), kind=jnp.bfloat16):
    level = steps_of(stream_key, dims, shards, -0.22, 0.18) if shards else 1.0
    entries = jax.random.normal(stream_key, dims, jnp.float32) * spread * level
    return jnp.minimum(jnp.maximum(entries, -reach), reach).astype(kind)


def setup_inputs(seed: int = 0) -> dict:
    key_of = jax.random.split(jax.random.key(seed), 17)
    return {
        "x_in": normal_values(key_of[0], (TOKENS, D), 1.0, 6.0, ((0, 128),)),
        "cotangent": normal_values(key_of[1], (TOKENS, D), 1.0, 6.0, ((0, 128),)),
        "seq_lengths": draw_seq_lengths(jax.random.fold_in(key_of[16], 71), 0),
        "gain_in": jnp.clip(1.0 + 0.1 * jax.random.normal(key_of[3], (LAYERS, D), jnp.float32), 0.5, 1.5).astype(jnp.bfloat16),
        "w_zx": normal_values(key_of[4], (LAYERS, D, 2, INNER), D ** -0.5, 0.1875, ((1, 64), (3, 2))),
        "w_bc": normal_values(key_of[5], (LAYERS, D, 2 * STATE), D ** -0.5, 0.1875, ((1, 64),)),
        "w_dt": normal_values(key_of[6], (LAYERS, D, HEADS), D ** -0.5, 0.1875, ((1, 64), (2, 2))),
        "conv_x": jnp.clip(jax.random.uniform(key_of[7], (LAYERS, CONV, INNER), jnp.float32, -0.5, 0.5) * steps_of(key_of[7], (LAYERS, CONV, INNER), ((2, 2),), -0.4, 0.0), -0.5, 0.5).astype(jnp.bfloat16),
        "conv_bc": jnp.clip(jax.random.uniform(key_of[8], (LAYERS, CONV, 2 * STATE), jnp.float32, -0.5, 0.5), -0.5, 0.5).astype(jnp.bfloat16),
        "bias_x": jnp.clip(jax.random.uniform(key_of[9], (LAYERS, INNER), jnp.float32, -0.5, 0.5) * steps_of(key_of[9], (LAYERS, INNER), ((1, 2),), -0.4, 0.0), -0.5, 0.5).astype(jnp.bfloat16),
        "bias_bc": jnp.clip(jax.random.uniform(key_of[10], (LAYERS, 2 * STATE), jnp.float32, -0.5, 0.5), -0.5, 0.5).astype(jnp.bfloat16),
        "dt_bias": jnp.clip(-6.0 + 4.0 * jax.random.uniform(key_of[11], (LAYERS, HEADS), jnp.float32) ** steps_of(key_of[11], (LAYERS, HEADS), ((1, 2),), -0.2, 0.2), -6.0, -2.0).astype(jnp.bfloat16),
        "a_log": jnp.clip(2.5 * jax.random.uniform(key_of[12], (LAYERS, HEADS), jnp.float32) ** steps_of(key_of[12], (LAYERS, HEADS), ((1, 2),), -0.2, 0.2), 0.0, 2.5).astype(jnp.bfloat16),
        "skip": jnp.clip(0.5 + 1.0 * jax.random.uniform(key_of[13], (LAYERS, HEADS), jnp.float32) ** steps_of(key_of[13], (LAYERS, HEADS), ((1, 2),), -0.2, 0.2), 0.5, 1.5).astype(jnp.bfloat16),
        "gain_gate": jnp.clip(1.0 + 0.1 * jax.random.normal(key_of[14], (LAYERS, INNER), jnp.float32), 0.5, 1.5).astype(jnp.bfloat16),
        "w_out": normal_values(key_of[15], (LAYERS, INNER, D), INNER ** -0.5, 0.125, ((1, 2), (2, 64))),
    }


EPS = 1e-05

@jax.custom_vjp
def low(v):
    return lax.optimization_barrier(v.astype(jnp.bfloat16)).astype(jnp.float32)

@jax.custom_vjp
def low_back(v):
    return v

def low_keep(v):
    return (low(v), None)

def low_pass(kept, grad):
    return (grad,)

def back_keep(v):
    return (v, None)

def back_low(kept, grad):
    return (low(grad),)
low.defvjp(low_keep, low_pass)
low_back.defvjp(back_keep, back_low)

def segment_rows(lengths, row_count):
    positions = jnp.arange(row_count, dtype=jnp.int32)
    bounds = jnp.cumsum(lengths).astype(jnp.int32)
    return lax.optimization_barrier(jnp.sum((positions[:, None] >= bounds[None, :]).astype(jnp.int32), axis=1)).astype(jnp.int32)

def conv_mix(signal, weight, bias, segment_ids):
    row_count, channel_count = signal.shape
    tap_count = weight.shape[0]
    summed = bias[None, :] + weight[tap_count - 1][None, :] * signal
    for offset in range(1, tap_count):
        earlier = jnp.concatenate([jnp.zeros((offset, channel_count), signal.dtype), signal[:row_count - offset]], axis=0)
        earlier_ids = jnp.concatenate([jnp.full((offset,), -1, jnp.int32), segment_ids[:row_count - offset]])
        same_seq = (earlier_ids == segment_ids).astype(signal.dtype)
        summed = summed + weight[tap_count - 1 - offset][None, :] * earlier * same_seq[:, None]
    return jax.nn.silu(summed)

def ssd_scan(values, steps, rates, b_mat, c_mat, skip_gain, segment_ids):
    row_count, head_count, head_width = values.shape
    state_width = b_mat.shape[1]
    block_count = row_count // SPAN
    lower = (jnp.arange(SPAN)[:, None] >= jnp.arange(SPAN)[None, :]).astype(values.dtype)
    highest = lax.Precision.HIGHEST

    def one_block(carry, block):
        state, last_segment = carry
        block_values, block_steps, block_b, block_c, block_ids = block
        log_steps = block_steps * rates[None, :]
        cumulative = jnp.dot(lower, log_steps, precision=highest)
        same_seq = (block_ids[:, None] == block_ids[None, :]) & (lower > 0)
        gaps = cumulative[:, None, :] - cumulative[None, :, :]
        decays = jnp.where(same_seq[:, :, None], jnp.exp(jnp.where(same_seq[:, :, None], gaps, 0.0)), 0.0)
        scores = jnp.dot(block_c, block_b.T, precision=highest)
        weights = scores[:, :, None] * decays * block_steps[None, :, :]
        inside = jnp.einsum('tsh,shp->thp', weights, block_values, precision=highest)
        carried = (block_ids == last_segment).astype(values.dtype)
        from_state = jnp.einsum('tn,hpn->thp', block_c, state, precision=highest) * (carried[:, None] * jnp.exp(cumulative))[:, :, None]
        final_segment = block_ids[SPAN - 1]
        in_final = (block_ids == final_segment)[:, None]
        tails = jnp.where(in_final, jnp.exp(jnp.where(in_final, cumulative[SPAN - 1][None, :] - cumulative, 0.0)), 0.0) * block_steps
        keeping = (last_segment == final_segment).astype(values.dtype)
        new_state = keeping * jnp.exp(cumulative[SPAN - 1])[:, None, None] * state + jnp.einsum('sh,shp,sn->hpn', tails, block_values, block_b, precision=highest)
        output = inside + from_state + skip_gain[None, :, None] * block_values
        return ((new_state, final_segment), output)
    blocks = (values.reshape(block_count, SPAN, head_count, head_width), steps.reshape(block_count, SPAN, head_count), b_mat.reshape(block_count, SPAN, state_width), c_mat.reshape(block_count, SPAN, state_width), segment_ids.reshape(block_count, SPAN))
    initial = (jnp.zeros((head_count, head_width, state_width), values.dtype), jnp.array(-1, jnp.int32))
    unused, outputs = lax.scan(jax.checkpoint(one_block), initial, blocks)
    return outputs.reshape(row_count, head_count, head_width)

def mixer_layer(hidden, segment_ids, live, params):
    gain_norm, wzx, wbc, wdt, taps_x, taps_bc, shift_x, shift_bc, step_bias, log_rate, skip_gain, gain_inner, wout = params
    highest = lax.Precision.HIGHEST
    row_count = hidden.shape[0]
    inner_width = wzx.shape[2]
    head_count = step_bias.shape[0]
    scale = lax.rsqrt(lax.optimization_barrier(jnp.mean(hidden * hidden, axis=1)) + EPS)
    normed = low(hidden * scale[:, None] * gain_norm[None, :])
    proj_zx = low_back(low(jnp.dot(normed, wzx.reshape(wzx.shape[0], 2 * inner_width), precision=highest)))
    proj_bc = low_back(low(jnp.dot(normed, wbc, precision=highest)))
    proj_dt = low_back(low(jnp.dot(normed, wdt, precision=highest)))
    gate_pre = proj_zx[:, :inner_width]
    signal = jnp.concatenate([proj_zx[:, inner_width:], proj_bc], axis=1)
    activated = conv_mix(signal, jnp.concatenate([taps_x, taps_bc], axis=1), jnp.concatenate([shift_x, shift_bc]), segment_ids)
    values = low(activated[:, :inner_width])
    b_mat = low(activated[:, inner_width:inner_width + STATE])
    c_mat = low(activated[:, inner_width + STATE:])
    steps = jax.nn.softplus(proj_dt + step_bias[None, :])
    ssd_out = ssd_scan(values.reshape(row_count, head_count, -1), steps, -jnp.exp(log_rate), b_mat, c_mat, skip_gain, segment_ids)
    gated = ssd_out.reshape(row_count, inner_width) * jax.nn.silu(gate_pre)
    gate_scale = lax.rsqrt(lax.optimization_barrier(jnp.mean(gated * gated, axis=1)) + EPS)
    normed_gate = low(gated * gate_scale[:, None] * gain_inner[None, :])
    mixed = low_back(jnp.dot(normed_gate, wout, precision=highest))
    return hidden + live[:, None] * mixed

def reference(x_in, cotangent, seq_lengths, gain_in, w_zx, w_bc, w_dt, conv_x, conv_bc, bias_x, bias_bc, dt_bias, a_log, skip, gain_gate, w_out):
    group_total = seq_lengths.shape[0]
    group_rows = x_in.shape[0] // group_total
    float_params = (gain_in.astype(jnp.float32), w_zx.astype(jnp.float32), w_bc.astype(jnp.float32), w_dt.astype(jnp.float32), conv_x.astype(jnp.float32), conv_bc.astype(jnp.float32), bias_x.astype(jnp.float32), bias_bc.astype(jnp.float32), dt_bias.astype(jnp.float32), a_log.astype(jnp.float32), skip.astype(jnp.float32), gain_gate.astype(jnp.float32), w_out.astype(jnp.float32))

    def forward(activations, *params):

        def per_group(group):
            hidden, lengths = group
            segment_ids = segment_rows(lengths, group_rows)
            live = (segment_ids < SEQS).astype(jnp.float32)
            for layer_index in range(LAYERS):
                hidden = mixer_layer(hidden, segment_ids, live, tuple((param[layer_index] for param in params)))
            return hidden
        grouped = activations.reshape(group_total, group_rows, activations.shape[1])
        return lax.map(jax.checkpoint(per_group), (grouped, seq_lengths)).reshape(activations.shape)
    outputs, backward = jax.vjp(forward, x_in.astype(jnp.float32), *float_params)
    grads = backward(cotangent.astype(jnp.float32))
    return (outputs.astype(jnp.bfloat16), grads[0], grads[1], grads[2], grads[3], grads[4], grads[5], grads[6], grads[7], grads[8], grads[9], grads[10], grads[11], grads[12], grads[13])
```

```python
import functools

import jax
import jax.numpy as jnp
from jax import lax
from jax.experimental import pallas as pl
from jax.experimental.pallas import tpu as pltpu
from jax.sharding import PartitionSpec as P

MESH = pl.DeviceIdType.MESH

SPAN = 256
SEQS = 4
INNER = 2048


EPS = 1e-05


def joined_along(parts, dim):
    shape = list(parts.shape[1:])
    shape[dim] *= parts.shape[0]
    return jnp.moveaxis(parts, 0, dim).reshape(shape)


def copy_for_each(shard, axis):
    length = lax.axis_size(axis)
    return lax.all_to_all(
        jnp.broadcast_to(shard[None], (length, *shard.shape)), axis, 0, 0, tiled=True
    )


def gather_directly(shard, axis, dim):
    return joined_along(copy_for_each(shard, axis), dim)


def taken_together(shard, axis):
    return copy_for_each(shard, axis).astype(jnp.float32).sum(axis=0)


def in_blocks(shard, dim, length):
    shape = shard.shape
    parts = shard.reshape(*shape[:dim], length, shape[dim] // length, *shape[dim + 1 :])
    return jnp.moveaxis(parts, dim, 0)


def sent_and_summed(shard, axis, dim):
    parts = in_blocks(shard, dim, lax.axis_size(axis))
    arrived = lax.all_to_all(parts, axis, split_axis=0, concat_axis=0, tiled=True)
    return arrived.astype(jnp.float32).sum(axis=0)


def place():
    index = lax.axis_index("fsdp")
    return index // 16, (index // 8) % 2, (index // 2) % 4, index % 2


def index_of(y, z, x, c):
    return ((y * 2 + z) * 4 + x) * 2 + c


PLANE_ZX = [(dz, dx) for dz in range(2) for dx in range(4) if (dz, dx) != (0, 0)]
PLANE_YZ = [(dy, dz) for dy in range(4) for dz in range(2) if (dy, dz) != (0, 0)]


def peers_of():
    y, z, x, c = place()
    found = [index_of(y, (z + dz) % 2, (x + dx) % 4, c) for dz, dx in PLANE_ZX]
    found += [index_of((y + dy) % 4, (z + dz) % 2, x, c) for dy, dz in PLANE_YZ if dy != 0]
    found.append(index_of(y, z, x, 1 - c))
    return found


def greet_all(with_tp):
    barrier = pltpu.get_barrier_semaphore()
    peers = peers_of()
    for peer in peers:
        pl.semaphore_signal(barrier, inc=1, device_id={"fsdp": peer}, device_id_type=MESH)
    count = len(peers)
    if with_tp:
        other = 1 - lax.axis_index("tp")
        pl.semaphore_signal(barrier, inc=1, device_id={"tp": other}, device_id_type=MESH)
        count += 1
    pl.semaphore_wait(barrier, count)


def send(src, dst, sems, slot, **where):
    copy = pltpu.make_async_remote_copy(
        src_ref=src,
        dst_ref=dst,
        send_sem=sems.at[0, slot],
        recv_sem=sems.at[1, slot],
        device_id=where,
        device_id_type=MESH,
    )
    copy.start()
    return copy


GATHER_COPIES = 28


class Gather:
    def __init__(self, whole, sems, first, half, end):
        self.whole, self.sems = whole, sems
        self.cols = (pl.ds(first, half - first), pl.ds(half, end - half))
        self.started = []

    def plane(self):
        y, z, x, c = place()
        cols_a, cols_b = self.cols
        self.first = []
        for slot, (dz, dx) in enumerate(PLANE_ZX):
            ref = self.whole.at[y, z, x, c, :, cols_a]
            self.first.append(
                send(ref, ref, self.sems, slot, fsdp=index_of(y, (z + dz) % 2, (x + dx) % 4, c))
            )
        for slot, (dy, dz) in enumerate(PLANE_YZ):
            ref = self.whole.at[y, z, x, c, :, cols_b]
            self.first.append(
                send(ref, ref, self.sems, 7 + slot, fsdp=index_of((y + dy) % 4, (z + dz) % 2, x, c))
            )

    def line(self):
        y, z, x, c = place()
        cols_a, cols_b = self.cols
        for copy in self.first:
            copy.wait_recv()
        self.second = []
        for step in range(1, 4):
            ref = self.whole.at[y, :, :, c, :, cols_a]
            self.second.append(
                send(ref, ref, self.sems, 14 + step - 1, fsdp=index_of((y + step) % 4, z, x, c))
            )
            ref = self.whole.at[:, :, x, c, :, cols_b]
            self.second.append(
                send(ref, ref, self.sems, 17 + step - 1, fsdp=index_of(y, z, (x + step) % 4, c))
            )
        self.third = []
        self.hand_over(0)

    def hand_over(self, step):
        y, z, x, c = place()
        cols_a, cols_b = self.cols
        ref = self.whole.at[(y - step + 4) % 4, :, :, c, :, cols_a]
        self.third.append(send(ref, ref, self.sems, 20 + step, fsdp=index_of(y, z, x, 1 - c)))
        ref = self.whole.at[:, :, (x - step + 4) % 4, c, :, cols_b]
        self.third.append(send(ref, ref, self.sems, 24 + step, fsdp=index_of(y, z, x, 1 - c)))

    def core(self):
        for step in (1, 3, 2):
            self.second[2 * (step - 1)].wait_recv()
            self.second[2 * (step - 1) + 1].wait_recv()
            self.hand_over(step)

    def finish(self):
        for copy in self.third:
            copy.wait_recv()
        for copy in self.first + self.second + self.third:
            copy.wait_send()


REDUCE_COPIES = 21


class Reduce:
    def __init__(self, grad, from_core, from_line_a, from_line_b, from_plane_a, from_plane_b, sems, half, end):
        self.grad, self.from_core, self.sems = grad, from_core, sems
        self.line_a, self.line_b = from_line_a, from_line_b
        self.plane_a, self.plane_b = from_plane_a, from_plane_b
        self.cols = (pl.ds(0, half), pl.ds(half, end - half))

    def core(self):
        y, z, x, c = place()
        self.copies = [
            send(
                self.grad.at[:, :, :, 1 - c],
                self.from_core,
                self.sems,
                0,
                fsdp=index_of(y, z, x, 1 - c),
            )
        ]

    def line(self):
        y, z, x, c = place()
        cols_a, cols_b = self.cols
        self.copies[0].wait_recv()

        @pl.loop(0, 32)
        def _(block):
            iy, iz, ix = block // 8, (block // 4) % 2, block % 4
            mine = self.grad[iy, iz, ix, c].astype(jnp.float32)
            theirs = self.from_core[iy, iz, ix].astype(jnp.float32)
            self.from_core[iy, iz, ix] = (mine + theirs).astype(jnp.bfloat16)

        self.second = []
        for step in range(1, 4):
            to = (y + step) % 4
            self.second.append(
                send(
                    self.from_core.at[to, :, :, :, cols_a],
                    self.line_a.at[step - 1],
                    self.sems,
                    step,
                    fsdp=index_of(to, z, x, c),
                )
            )
            to = (x + step) % 4
            self.second.append(
                send(
                    self.from_core.at[:, :, to, :, cols_b],
                    self.line_b.at[step - 1],
                    self.sems,
                    3 + step,
                    fsdp=index_of(y, z, to, c),
                )
            )

    def plane(self):
        y, z, x, c = place()
        cols_a, cols_b = self.cols
        for copy in self.second:
            copy.wait_recv()

        @pl.loop(0, 8)
        def _(block):
            iz, ix = block // 4, block % 4
            total = self.from_core[y, iz, ix, :, cols_a].astype(jnp.float32)
            for step in range(3):
                total = total + self.line_a[step, iz, ix].astype(jnp.float32)
            self.line_a[0, iz, ix] = total.astype(jnp.bfloat16)
            iy, iz = block // 2, block % 2
            total = self.from_core[iy, iz, x, :, cols_b].astype(jnp.float32)
            for step in range(3):
                total = total + self.line_b[step, iy, iz].astype(jnp.float32)
            self.line_b[0, iy, iz] = total.astype(jnp.bfloat16)

        self.third = []
        for slot, (dz, dx) in enumerate(PLANE_ZX):
            tz, tx = (z + dz) % 2, (x + dx) % 4
            self.third.append(
                send(
                    self.line_a.at[0, tz, tx],
                    self.plane_a.at[slot],
                    self.sems,
                    7 + slot,
                    fsdp=index_of(y, tz, tx, c),
                )
            )
        for slot, (dy, dz) in enumerate(PLANE_YZ):
            ty, tz = (y + dy) % 4, (z + dz) % 2
            self.third.append(
                send(
                    self.line_b.at[0, ty, tz],
                    self.plane_b.at[slot],
                    self.sems,
                    14 + slot,
                    fsdp=index_of(ty, tz, x, c),
                )
            )

    def finish(self, out):
        y, z, x, c = place()
        cols_a, cols_b = self.cols
        for copy in self.third:
            copy.wait_recv()
        total = self.line_a[0, z, x].astype(jnp.float32)
        for slot in range(7):
            total = total + self.plane_a[slot].astype(jnp.float32)
        out[:, cols_a] = total
        total = self.line_b[0, y, z].astype(jnp.float32)
        for slot in range(7):
            total = total + self.plane_b[slot].astype(jnp.float32)
        out[:, cols_b] = total
        for copy in self.copies + self.second + self.third:
            copy.wait_send()

ZX, PAIR, DT, OUT = 2048, 256, 128, 1024
COLS = ZX + PAIR + DT + OUT
IN_COLS = ZX + PAIR + DT


def gather_kernel(own, out, sems, local_sem):
    y, z, x, c = place()
    keep = pltpu.make_async_copy(own, out.at[y, z, x, c], local_sem)
    keep.start()
    greet_all(False)
    keep.wait()
    width = out.shape[-1]
    job = Gather(out, sems, 0, width // 2, width)
    job.plane()
    job.line()
    job.core()
    job.finish()


def gather_rows(own):
    return pl.pallas_call(
        gather_kernel,
        out_shape=jax.ShapeDtypeStruct((4, 2, 4, 2, *own.shape), own.dtype),
        in_specs=[pl.BlockSpec(memory_space=pltpu.VMEM)],
        out_specs=pl.BlockSpec(memory_space=pltpu.VMEM),
        scratch_shapes=[pltpu.SemaphoreType.DMA((2, GATHER_COPIES)), pltpu.SemaphoreType.DMA],
        compiler_params=pltpu.CompilerParams(
            collective_id=0, has_side_effects=True, vmem_limit_bytes=40 << 20
        ),
        name="gather_rows",
    )(own)


def reduce_kernel(grad, out, from_core, line_a, line_b, plane_a, plane_b, sems):
    greet_all(False)
    width = grad.shape[-1]
    job = Reduce(grad, from_core, line_a, line_b, plane_a, plane_b, sems, width // 2, width)
    job.core()
    job.line()
    job.plane()
    job.finish(out)


def reduce_rows(grad):
    rows, width = grad.shape[-2:]
    half = width // 2
    return pl.pallas_call(
        reduce_kernel,
        out_shape=jax.ShapeDtypeStruct((rows, width), jnp.float32),
        in_specs=[pl.BlockSpec(memory_space=pltpu.VMEM)],
        out_specs=pl.BlockSpec(memory_space=pltpu.VMEM),
        scratch_shapes=[
            pltpu.VMEM((4, 2, 4, rows, width), jnp.bfloat16),
            pltpu.VMEM((3, 2, 4, rows, half), jnp.bfloat16),
            pltpu.VMEM((3, 4, 2, rows, width - half), jnp.bfloat16),
            pltpu.VMEM((7, rows, half), jnp.bfloat16),
            pltpu.VMEM((7, rows, width - half), jnp.bfloat16),
            pltpu.SemaphoreType.DMA((2, REDUCE_COPIES)),
        ],
        compiler_params=pltpu.CompilerParams(
            collective_id=1, has_side_effects=True, vmem_limit_bytes=40 << 20
        ),
        name="reduce_rows",
    )(grad)


def segment_rows(lengths, row_count):
    positions = jnp.arange(row_count, dtype=jnp.int32)
    bounds = jnp.cumsum(lengths)
    return jnp.sum((positions[:, None] >= bounds[None, :]).astype(jnp.int32), axis=1)


def conv_mix(signal, weight, bias, segment_ids):
    row_count, channel_count = signal.shape
    tap_count = weight.shape[0]
    summed = bias[None, :] + weight[tap_count - 1][None, :] * signal
    for offset in range(1, tap_count):
        earlier = jnp.concatenate(
            [jnp.zeros((offset, channel_count), signal.dtype), signal[: row_count - offset]], axis=0
        )
        earlier_ids = jnp.concatenate(
            [jnp.full((offset,), -1, jnp.int32), segment_ids[: row_count - offset]]
        )
        same_seq = (earlier_ids == segment_ids).astype(signal.dtype)
        summed = summed + weight[tap_count - 1 - offset][None, :] * earlier * same_seq[:, None]
    return jax.nn.silu(summed)


def ssd_scan(values, steps, rates, b_mat, c_mat, skip_gain, segment_ids):
    row_count, head_count, head_width = values.shape
    state_width = b_mat.shape[1]
    block_count = row_count // SPAN
    lower = (jnp.arange(SPAN)[:, None] >= jnp.arange(SPAN)[None, :]).astype(values.dtype)
    highest = lax.Precision.HIGHEST

    def one_block(carry, block):
        state, last_segment = carry
        block_values, block_steps, block_b, block_c, block_ids = block
        log_steps = block_steps * rates[None, :]
        cumulative = jnp.dot(lower, log_steps, precision=highest)
        same_seq = (block_ids[:, None] == block_ids[None, :]) & (lower > 0)
        gaps = cumulative[:, None, :] - cumulative[None, :, :]
        decays = jnp.where(
            same_seq[:, :, None], jnp.exp(jnp.where(same_seq[:, :, None], gaps, 0.0)), 0.0
        )
        scores = jnp.dot(block_c, block_b.T, precision=highest)
        weights = scores[:, :, None] * decays * block_steps[None, :, :]
        inside = jnp.einsum("tsh,shp->thp", weights, block_values, precision=highest)
        carried = (block_ids == last_segment).astype(values.dtype)
        from_state = (
            jnp.einsum("tn,hpn->thp", block_c, state, precision=highest)
            * (carried[:, None] * jnp.exp(cumulative))[:, :, None]
        )
        final_segment = block_ids[SPAN - 1]
        in_final = (block_ids == final_segment)[:, None]
        tails = (
            jnp.where(
                in_final,
                jnp.exp(jnp.where(in_final, cumulative[SPAN - 1][None, :] - cumulative, 0.0)),
                0.0,
            )
            * block_steps
        )
        keeping = (last_segment == final_segment).astype(values.dtype)
        new_state = keeping * jnp.exp(cumulative[SPAN - 1])[:, None, None] * state + jnp.einsum(
            "sh,shp,sn->hpn", tails, block_values, block_b, precision=highest
        )
        output = inside + from_state + skip_gain[None, :, None] * block_values
        return ((new_state, final_segment), output)

    blocks = (
        values.reshape(block_count, SPAN, head_count, head_width),
        steps.reshape(block_count, SPAN, head_count),
        b_mat.reshape(block_count, SPAN, state_width),
        c_mat.reshape(block_count, SPAN, state_width),
        segment_ids.reshape(block_count, SPAN),
    )
    initial = (
        jnp.zeros((head_count, head_width, state_width), values.dtype),
        jnp.array(-1, jnp.int32),
    )
    unused, outputs = lax.scan(jax.checkpoint(one_block), initial, blocks)
    return outputs.reshape(row_count, head_count, head_width)


def term_builder(entries):
    pieces_out = []
    contract_rows = (((0,), (0,)), ((), ()))
    for gathered_rows, d_proj_all, cot_rows, normed_rows in entries:
        pieces_out.append(
            lax.dot_general(
                gathered_rows, d_proj_all, contract_rows, preferred_element_type=jnp.float32
            )
        )
        pieces_out.append(
            lax.dot_general(
                cot_rows, normed_rows, contract_rows, preferred_element_type=jnp.float32
            )
        )
    return jnp.concatenate(pieces_out, axis=1)


def shards(
    x_in,
    cotangent,
    seq_lengths,
    gain_in,
    w_zx,
    w_bc,
    w_dt,
    conv_x,
    conv_bc,
    bias_x,
    bias_bc,
    dt_bias,
    a_log,
    skip,
    gain_gate,
    w_out,
):
    f32 = jnp.float32
    bf16 = jnp.bfloat16
    own_count = x_in.shape[0]
    model_width = x_in.shape[1]
    tp_count = lax.axis_size("tp")
    tp_place = lax.axis_index("tp")
    group_count = own_count * tp_count
    row_start = tp_place * own_count
    layer_count = w_zx.shape[0]
    local_rows = w_zx.shape[1]
    local_inner = w_zx.shape[3]
    local_heads = dt_bias.shape[1]
    head_width = local_inner // local_heads
    pair_width = w_bc.shape[2]
    state_width = pair_width // 2
    segment_ids = segment_rows(seq_lengths[0], group_count)
    live_group = (segment_ids < SEQS).astype(f32)
    live_own = lax.dynamic_slice_in_dim(live_group, row_start, own_count, 0)
    positions = jnp.arange(group_count, dtype=jnp.int32)
    own_flags = ((positions >= row_start) & (positions < row_start + own_count)).astype(f32)

    def widen(part):
        full_shape = part.shape[:-1] + (part.shape[-1] * tp_count,)
        return lax.dynamic_update_slice_in_dim(
            jnp.zeros(full_shape, f32), part, tp_place * part.shape[-1], part.ndim - 1
        )

    def conv_apply(signal_in, weight_in, bias_in):
        return conv_mix(signal_in, weight_in, bias_in, segment_ids)

    def ssd_apply(values_in, raw_in, bias_in, log_in, skip_in, b_in, c_in):
        steps = jax.nn.softplus(raw_in + bias_in[None, :])
        result = ssd_scan(
            values_in.reshape(group_count, local_heads, head_width),
            steps,
            -jnp.exp(log_in),
            b_in,
            c_in,
            skip_in,
            segment_ids,
        )
        return result.reshape(group_count, local_inner)

    hidden = x_in.astype(f32)
    saved = []
    packed = jnp.concatenate(
        [
            w_zx.reshape(layer_count, local_rows, 2 * local_inner),
            w_bc,
            jnp.pad(w_dt, ((0, 0), (0, 0), (0, DT - local_heads))),
            jnp.swapaxes(w_out, 1, 2),
        ],
        axis=2,
    )
    packed = jnp.moveaxis(packed, 0, 1).reshape(local_rows, layer_count * COLS)
    whole = gather_rows(packed).reshape(model_width, layer_count, COLS)
    for layer_index in range(layer_count):
        gain_norm = gain_in[layer_index].astype(f32)
        scale = lax.rsqrt(jnp.mean(hidden * hidden, axis=1) + EPS)
        normed_own = (hidden * scale[:, None] * gain_norm[None, :]).astype(bf16)
        gathered = lax.all_gather(normed_own, "tp", axis=0, tiled=True)

        def add_rows(totals, pieces, first_row, gathered=gathered):
            piece_zx, piece_bc, piece_dt = pieces
            count = piece_zx.shape[0]
            return (
                jnp.dot(
                    gathered, piece_zx.reshape(count, 2 * local_inner), preferred_element_type=f32
                ),
                jnp.dot(gathered, piece_bc, preferred_element_type=f32),
                jnp.dot(gathered, piece_dt, preferred_element_type=f32),
            )

        starting = (
            jnp.zeros((group_count, 2 * local_inner), f32),
            jnp.zeros((group_count, pair_width), f32),
            jnp.zeros((group_count, local_heads), f32),
        )
        proj_zx, proj_bc, proj_dt = add_rows(
            starting,
            (
                whole[:, layer_index, :ZX].reshape(model_width, 2, local_inner),
                whole[:, layer_index, ZX : ZX + PAIR],
                whole[:, layer_index, ZX + PAIR : ZX + PAIR + local_heads],
            ),
            jnp.int32(0),
        )
        proj_zx = proj_zx.astype(bf16)
        proj_bc = proj_bc.astype(bf16)
        proj_dt = proj_dt.astype(bf16)
        gate_pre = proj_zx[:, :local_inner].astype(f32)
        signal = jnp.concatenate([proj_zx[:, local_inner:], proj_bc], axis=1).astype(f32)
        conv_weight = jnp.concatenate([conv_x[layer_index], conv_bc[layer_index]], axis=1).astype(
            f32
        )
        conv_bias = jnp.concatenate([bias_x[layer_index], bias_bc[layer_index]]).astype(f32)
        activated, conv_back = jax.vjp(conv_apply, signal, conv_weight, conv_bias)
        rounded = lax.optimization_barrier(activated.astype(bf16)).astype(f32)
        values = rounded[:, :local_inner]
        b_mat = rounded[:, local_inner : local_inner + state_width]
        c_mat = rounded[:, local_inner + state_width :]
        ssd_out, ssd_back = jax.vjp(
            ssd_apply,
            values,
            proj_dt.astype(f32),
            dt_bias[layer_index].astype(f32),
            a_log[layer_index].astype(f32),
            skip[layer_index].astype(f32),
            b_mat,
            c_mat,
        )
        gated = ssd_out * jax.nn.silu(gate_pre)
        squares = lax.psum(jnp.sum(gated * gated, axis=1), "tp")
        gate_scale = lax.rsqrt(squares / INNER + EPS)
        gain_inner = gain_gate[layer_index].astype(f32)
        normed_gate = (gated * gate_scale[:, None] * gain_inner[None, :]).astype(bf16)

        def project_cols(weight_piece, first_row, normed_gate=normed_gate):
            return jnp.dot(normed_gate, weight_piece, preferred_element_type=f32)

        partial_mix = project_cols(whole[:, layer_index, IN_COLS:].T, jnp.int32(0))
        mixed_own = lax.psum_scatter(partial_mix, "tp", scatter_dimension=0, tiled=True)
        saved.append(
            (
                hidden,
                scale,
                gathered,
                conv_back,
                ssd_back,
                ssd_out,
                gate_pre,
                gated,
                gate_scale,
                normed_gate,
            )
        )
        hidden = hidden + live_own[:, None] * mixed_own
    act_out = hidden.astype(bf16)
    grad_hidden = cotangent.astype(f32)
    weight_sums = [None] * layer_count
    small_terms = [None] * layer_count
    kept_terms = [None] * layer_count
    contract_cols = (((1,), (1,)), ((), ()))
    for layer_index in reversed(range(layer_count)):
        (
            hidden_in,
            scale,
            gathered,
            conv_back,
            ssd_back,
            ssd_out,
            gate_pre,
            gated,
            gate_scale,
            normed_gate,
        ) = saved[layer_index]
        cot_own = (live_own[:, None] * grad_hidden).astype(bf16)
        cot_all = lax.all_gather(cot_own, "tp", axis=0, tiled=True)

        def add_back(totals, weight_piece, first_row, cot_all=cot_all):
            count = weight_piece.shape[1]
            return lax.dot_general(cot_all, weight_piece, contract_cols, preferred_element_type=f32)

        d_normed_gate = add_back(
            jnp.zeros((group_count, local_inner), f32),
            whole[:, layer_index, IN_COLS:].T,
            jnp.int32(0),
        )
        gain_inner = gain_gate[layer_index].astype(f32)
        weighted_gate = d_normed_gate * gain_inner[None, :]
        d_gain_gate = jnp.sum(d_normed_gate * gated * gate_scale[:, None], axis=0)
        inner_dot = lax.psum(jnp.sum(weighted_gate * gated, axis=1), "tp")
        d_gated = (
            gate_scale[:, None] * weighted_gate
            - gated * (gate_scale * gate_scale * gate_scale * inner_dot / INNER)[:, None]
        )
        sigmoid_gate = jax.nn.sigmoid(gate_pre)
        d_ssd_out = d_gated * jax.nn.silu(gate_pre)
        d_gate_pre = d_gated * ssd_out * sigmoid_gate * (1.0 + gate_pre * (1.0 - sigmoid_gate))
        d_values, d_raw, d_dt_bias, d_a_log, d_skip, d_b_mat, d_c_mat = ssd_back(d_ssd_out)
        d_signal, d_conv_weight, d_conv_bias = conv_back(
            jnp.concatenate([d_values, d_b_mat, d_c_mat], axis=1)
        )
        d_pair = taken_together(d_signal[:, local_inner:].astype(jnp.bfloat16), "tp").astype(
            jnp.float32
        )
        d_proj_zx = jnp.concatenate([d_gate_pre, d_signal[:, :local_inner]], axis=1).astype(bf16)
        d_proj_bc = d_pair.astype(bf16)
        d_proj_dt = d_raw.astype(bf16)
        d_pair_own = d_proj_bc * own_flags[:, None].astype(bf16)

        def back_cols(
            pieces, first_row, d_proj_zx=d_proj_zx, d_pair_own=d_pair_own, d_proj_dt=d_proj_dt
        ):
            piece_zx, piece_bc, piece_dt = pieces
            count = piece_zx.shape[0]
            return (
                lax.dot_general(
                    d_proj_zx,
                    piece_zx.reshape(count, 2 * local_inner),
                    contract_cols,
                    preferred_element_type=f32,
                )
                + lax.dot_general(d_pair_own, piece_bc, contract_cols, preferred_element_type=f32)
                + lax.dot_general(d_proj_dt, piece_dt, contract_cols, preferred_element_type=f32)
            )

        d_normed_part = back_cols(
            (
                whole[:, layer_index, :ZX].reshape(model_width, 2, local_inner),
                whole[:, layer_index, ZX : ZX + PAIR],
                whole[:, layer_index, ZX + PAIR : ZX + PAIR + local_heads],
            ),
            jnp.int32(0),
        )
        d_normed = sent_and_summed(d_normed_part.astype(jnp.bfloat16), "tp", 0)
        gain_norm = gain_in[layer_index].astype(f32)
        weighted_norm = d_normed * gain_norm[None, :]
        d_gain_norm = jnp.sum(d_normed * hidden_in * scale[:, None], axis=0)
        grad_hidden = (
            grad_hidden
            + scale[:, None] * weighted_norm
            - hidden_in
            * (scale * scale * scale * jnp.sum(weighted_norm * hidden_in, axis=1) / model_width)[
                :, None
            ]
        )
        kept_terms[layer_index] = (
            gathered,
            jnp.concatenate(
                [d_proj_zx, d_proj_bc, jnp.pad(d_proj_dt, ((0, 0), (0, DT - local_heads)))], axis=1
            ),
            cot_all,
            normed_gate,
        )
        small_terms[layer_index] = (
            d_gain_norm,
            widen(d_conv_weight[:, :local_inner]),
            d_conv_weight[:, local_inner:],
            widen(d_conv_bias[:local_inner]),
            d_conv_bias[local_inner:],
            widen(jnp.stack([d_dt_bias, d_a_log, d_skip])),
            widen(d_gain_gate),
        )
    terms = term_builder(kept_terms).astype(bf16)
    joined = reduce_rows(terms.reshape(4, 2, 4, 2, local_rows, layer_count * COLS))
    block_width = joined.shape[1] // layer_count
    weight_sums = [
        joined[:, layer_index * block_width : (layer_index + 1) * block_width]
        for layer_index in range(layer_count)
    ]
    zx_end = 2 * local_inner
    bc_end = zx_end + pair_width
    dt_end = bc_end + DT
    grad_w_zx = jnp.stack(
        [block[:, :zx_end].reshape(local_rows, 2, local_inner) for block in weight_sums]
    )
    grad_w_bc = jnp.stack([block[:, zx_end:bc_end] for block in weight_sums])
    grad_w_dt = jnp.stack([block[:, bc_end : bc_end + local_heads] for block in weight_sums])
    grad_w_out = jnp.stack([block[:, dt_end:].T for block in weight_sums])
    gains_all = jnp.stack([entry[0] for entry in small_terms])
    taps_x_all = jnp.stack([entry[1] for entry in small_terms])
    taps_bc_all = jnp.stack([entry[2] for entry in small_terms])
    shift_x_all = jnp.stack([entry[3] for entry in small_terms])
    shift_bc_all = jnp.stack([entry[4] for entry in small_terms])
    heads_all = jnp.stack([entry[5] for entry in small_terms])
    gate_all = jnp.stack([entry[6] for entry in small_terms])
    summed_small = lax.psum(
        (gains_all, taps_x_all, taps_bc_all, shift_x_all, shift_bc_all, heads_all, gate_all),
        ("fsdp", "tp"),
    )
    grad_gain_in = summed_small[0]
    grad_conv_x = lax.dynamic_slice_in_dim(summed_small[1], tp_place * local_inner, local_inner, 2)
    grad_conv_bc = summed_small[2]
    grad_bias_x = lax.dynamic_slice_in_dim(summed_small[3], tp_place * local_inner, local_inner, 1)
    grad_bias_bc = summed_small[4]
    heads_own = lax.dynamic_slice_in_dim(summed_small[5], tp_place * local_heads, local_heads, 2)
    grad_gain_gate = lax.dynamic_slice_in_dim(
        summed_small[6], tp_place * local_inner, local_inner, 1
    )
    return (
        act_out,
        grad_hidden,
        grad_gain_in,
        grad_w_zx,
        grad_w_bc,
        grad_w_dt,
        grad_conv_x,
        grad_conv_bc,
        grad_bias_x,
        grad_bias_bc,
        heads_own[:, 0],
        heads_own[:, 1],
        heads_own[:, 2],
        grad_gain_gate,
        grad_w_out,
    )


def solution(mesh):
    placed = (
        P(("fsdp", "tp"), None),
        P(("fsdp", "tp"), None),
        P("fsdp", None),
        P(),
        P(None, "fsdp", None, "tp"),
        P(None, "fsdp", None),
        P(None, "fsdp", "tp"),
        P(None, None, "tp"),
        P(),
        P(None, "tp"),
        P(),
        P(None, "tp"),
        P(None, "tp"),
        P(None, "tp"),
        P(None, "tp"),
        P(None, "tp", "fsdp"),
    )
    return jax.shard_map(
        shards,
        mesh=mesh,
        in_specs=placed,
        out_specs=(
            P(("fsdp", "tp"), None),
            P(("fsdp", "tp"), None),
            P(),
            P(None, "fsdp", None, "tp"),
            P(None, "fsdp", None),
            P(None, "fsdp", "tp"),
            P(None, None, "tp"),
            P(),
            P(None, "tp"),
            P(),
            P(None, "tp"),
            P(None, "tp"),
            P(None, "tp"),
            P(None, "tp"),
            P(None, "tp", "fsdp"),
        ),
        check_vma=False,
    )
```

```python
import jax
import jax.numpy as jnp
from jax import lax
from jax.experimental import pallas as pl
from jax.experimental.pallas import tpu as pltpu
from jax.sharding import PartitionSpec as P

MESH = pl.DeviceIdType.MESH
INNER = 2048
EPS = 1e-05


def place():
    index = lax.axis_index("fsdp")
    return index // 16, (index // 8) % 2, (index // 2) % 4, index % 2


def index_of(y, z, x, c):
    return ((y * 2 + z) * 4 + x) * 2 + c


PLANE_ZX = [(dz, dx) for dz in range(2) for dx in range(4) if (dz, dx) != (0, 0)]
PLANE_YZ = [(dy, dz) for dy in range(4) for dz in range(2) if (dy, dz) != (0, 0)]


def peers_of():
    y, z, x, c = place()
    found = [index_of(y, (z + dz) % 2, (x + dx) % 4, c) for dz, dx in PLANE_ZX]
    found += [index_of((y + dy) % 4, (z + dz) % 2, x, c) for dy, dz in PLANE_YZ if dy != 0]
    found.append(index_of(y, z, x, 1 - c))
    return found


def greet_all(with_tp):
    barrier = pltpu.get_barrier_semaphore()
    peers = peers_of()
    for peer in peers:
        pl.semaphore_signal(barrier, inc=1, device_id={"fsdp": peer}, device_id_type=MESH)
    count = len(peers)
    if with_tp:
        other = 1 - lax.axis_index("tp")
        pl.semaphore_signal(barrier, inc=1, device_id={"tp": other}, device_id_type=MESH)
        count += 1
    pl.semaphore_wait(barrier, count)


def send(src, dst, sems, slot, **where):
    copy = pltpu.make_async_remote_copy(
        src_ref=src,
        dst_ref=dst,
        send_sem=sems.at[0, slot],
        recv_sem=sems.at[1, slot],
        device_id=where,
        device_id_type=MESH,
    )
    copy.start()
    return copy


GATHER_COPIES = 28


class Gather:
    def __init__(self, whole, sems, first, half, end):
        self.whole, self.sems = whole, sems
        self.cols = (pl.ds(first, half - first), pl.ds(half, end - half))
        self.started = []

    def plane(self):
        y, z, x, c = place()
        cols_a, cols_b = self.cols
        self.first = []
        for slot, (dz, dx) in enumerate(PLANE_ZX):
            ref = self.whole.at[y, z, x, c, :, cols_a]
            self.first.append(
                send(ref, ref, self.sems, slot, fsdp=index_of(y, (z + dz) % 2, (x + dx) % 4, c))
            )
        for slot, (dy, dz) in enumerate(PLANE_YZ):
            ref = self.whole.at[y, z, x, c, :, cols_b]
            self.first.append(
                send(ref, ref, self.sems, 7 + slot, fsdp=index_of((y + dy) % 4, (z + dz) % 2, x, c))
            )

    def line(self):
        y, z, x, c = place()
        cols_a, cols_b = self.cols
        for copy in self.first:
            copy.wait_recv()
        self.second = []
        for step in range(1, 4):
            ref = self.whole.at[y, :, :, c, :, cols_a]
            self.second.append(
                send(ref, ref, self.sems, 14 + step - 1, fsdp=index_of((y + step) % 4, z, x, c))
            )
            ref = self.whole.at[:, :, x, c, :, cols_b]
            self.second.append(
                send(ref, ref, self.sems, 17 + step - 1, fsdp=index_of(y, z, (x + step) % 4, c))
            )
        self.third = []
        self.hand_over(0)

    def hand_over(self, step):
        y, z, x, c = place()
        cols_a, cols_b = self.cols
        ref = self.whole.at[(y - step + 4) % 4, :, :, c, :, cols_a]
        self.third.append(send(ref, ref, self.sems, 20 + step, fsdp=index_of(y, z, x, 1 - c)))
        ref = self.whole.at[:, :, (x - step + 4) % 4, c, :, cols_b]
        self.third.append(send(ref, ref, self.sems, 24 + step, fsdp=index_of(y, z, x, 1 - c)))

    def core(self):
        for step in (1, 3, 2):
            self.second[2 * (step - 1)].wait_recv()
            self.second[2 * (step - 1) + 1].wait_recv()
            self.hand_over(step)

    def finish(self):
        for copy in self.third:
            copy.wait_recv()
        for copy in self.first + self.second + self.third:
            copy.wait_send()


REDUCE_COPIES = 21


class Reduce:
    def __init__(self, grad, from_core, from_line_a, from_line_b, from_plane_a, from_plane_b, sems, half, end):
        self.grad, self.from_core, self.sems = grad, from_core, sems
        self.line_a, self.line_b = from_line_a, from_line_b
        self.plane_a, self.plane_b = from_plane_a, from_plane_b
        self.cols = (pl.ds(0, half), pl.ds(half, end - half))

    def core(self):
        y, z, x, c = place()
        self.copies = [
            send(
                self.grad.at[:, :, :, 1 - c],
                self.from_core,
                self.sems,
                0,
                fsdp=index_of(y, z, x, 1 - c),
            )
        ]

    def line(self):
        y, z, x, c = place()
        cols_a, cols_b = self.cols
        self.copies[0].wait_recv()

        @pl.loop(0, 32)
        def _(block):
            iy, iz, ix = block // 8, (block // 4) % 2, block % 4
            mine = self.grad[iy, iz, ix, c].astype(jnp.float32)
            theirs = self.from_core[iy, iz, ix].astype(jnp.float32)
            self.from_core[iy, iz, ix] = (mine + theirs).astype(jnp.bfloat16)

        self.second = []
        for step in range(1, 4):
            to = (y + step) % 4
            self.second.append(
                send(
                    self.from_core.at[to, :, :, :, cols_a],
                    self.line_a.at[step - 1],
                    self.sems,
                    step,
                    fsdp=index_of(to, z, x, c),
                )
            )
            to = (x + step) % 4
            self.second.append(
                send(
                    self.from_core.at[:, :, to, :, cols_b],
                    self.line_b.at[step - 1],
                    self.sems,
                    3 + step,
                    fsdp=index_of(y, z, to, c),
                )
            )

    def plane(self):
        y, z, x, c = place()
        cols_a, cols_b = self.cols
        for copy in self.second:
            copy.wait_recv()

        @pl.loop(0, 8)
        def _(block):
            iz, ix = block // 4, block % 4
            total = self.from_core[y, iz, ix, :, cols_a].astype(jnp.float32)
            for step in range(3):
                total = total + self.line_a[step, iz, ix].astype(jnp.float32)
            self.line_a[0, iz, ix] = total.astype(jnp.bfloat16)
            iy, iz = block // 2, block % 2
            total = self.from_core[iy, iz, x, :, cols_b].astype(jnp.float32)
            for step in range(3):
                total = total + self.line_b[step, iy, iz].astype(jnp.float32)
            self.line_b[0, iy, iz] = total.astype(jnp.bfloat16)

        self.third = []
        for slot, (dz, dx) in enumerate(PLANE_ZX):
            tz, tx = (z + dz) % 2, (x + dx) % 4
            self.third.append(
                send(
                    self.line_a.at[0, tz, tx],
                    self.plane_a.at[slot],
                    self.sems,
                    7 + slot,
                    fsdp=index_of(y, tz, tx, c),
                )
            )
        for slot, (dy, dz) in enumerate(PLANE_YZ):
            ty, tz = (y + dy) % 4, (z + dz) % 2
            self.third.append(
                send(
                    self.line_b.at[0, ty, tz],
                    self.plane_b.at[slot],
                    self.sems,
                    14 + slot,
                    fsdp=index_of(ty, tz, x, c),
                )
            )

    def finish(self, out):
        y, z, x, c = place()
        cols_a, cols_b = self.cols
        for copy in self.third:
            copy.wait_recv()
        total = self.line_a[0, z, x].astype(jnp.float32)
        for slot in range(7):
            total = total + self.plane_a[slot].astype(jnp.float32)
        out[:, cols_a] = total
        total = self.line_b[0, y, z].astype(jnp.float32)
        for slot in range(7):
            total = total + self.plane_b[slot].astype(jnp.float32)
        out[:, cols_b] = total
        for copy in self.copies + self.second + self.third:
            copy.wait_send()


ROWS, WIDTH, INNER_OWN, STATE, HEADS_OWN = 256, 1024, 1024, 128, 16
ZX, PAIR, DT, OUT = 2048, 256, 128, 1024
IN_COLS = ZX + PAIR + DT
COLS = IN_COLS + OUT
SIGNAL = INNER_OWN + PAIR
F32, BF16 = jnp.float32, jnp.bfloat16
NN = (((1,), (0,)), ((), ()))
NT = (((1,), (1,)), ((), ()))
TN = (((0,), (0,)), ((), ()))


def dot(a, b, dims=NN):
    return lax.dot_general(a, b, dims, preferred_element_type=F32)


def exact_dot(a, b, dims=NN):
    return lax.dot_general(
        a, b, dims, preferred_element_type=F32, precision=lax.Precision.HIGHEST
    )


def tile(index, width):
    return pl.ds(pl.multiple_of(index * width, width), width)


def twice(part):
    return jnp.concatenate([part, part], axis=1)


def column(part, head):
    lane = lax.broadcasted_iota(jnp.int32, part.shape, 1)
    return jnp.sum(jnp.where(lane == head, part, 0.0), axis=1, keepdims=True)


def body(
    x_ref, cot_ref, own_ref, lens_ref, vec_ref, conv_ref, head_ref,
    act_ref, gin_ref, gw_ref, small_ref,
    wz0, wo0, w1, hid, norm_t, proj, vals, ssd, ngate, steps, cums, cums_t, scales, gscales, sig_dt,
    xs, cots, normed, cot_b, cot_t, grad, du, dact, dproj, scores, dscores, mask, same, live, acc, dcum, dstep,
    mixs, mixr, row_s, row_r, smalls, slots, bc_s, bc_r,
    core1, la1, lb1, pa1, pb1, core0, la0, lb0, pa0, pb0, coreo, lao, lbo, pao, pbo,
    gsem, rsem, tsem, ssem, lsem,
):
    y, z, x, c = place()
    t = lax.axis_index("tp")
    other = 1 - t
    own_rows = pl.ds(pl.multiple_of(t * 128, 128), 128)
    peer_rows = pl.ds(pl.multiple_of(other * 128, 128), 128)

    def wz(layer, cols):
        ref = wz0 if layer == 0 else w1
        return ref.at[:, :, :, :, :, cols]

    def load_cols(ref, cols):
        part = ref[:, :, :, :, :, cols]
        return part.reshape(WIDTH, part.shape[-1])

    def store_cols(ref, cols, part):
        ref[:, :, :, :, :, cols] = part.astype(BF16).reshape(4, 2, 4, 2, 16, part.shape[-1])

    z_ref = (wz0, w1)
    o_ref = (wo0, w1)
    o_first = (0, IN_COLS)

    keeps = [
        pltpu.make_async_copy(own_ref.at[0, :, pl.ds(0, IN_COLS)], wz0.at[y, z, x, c], lsem.at[0]),
        pltpu.make_async_copy(own_ref.at[0, :, pl.ds(IN_COLS, OUT)], wo0.at[y, z, x, c], lsem.at[1]),
        pltpu.make_async_copy(own_ref.at[1], w1.at[y, z, x, c], lsem.at[2]),
    ]
    for keep in keeps:
        keep.start()
    greet_all(True)
    for keep in keeps:
        keep.wait()
    gather_z0 = Gather(wz0, gsem.at[0], 0, 1280, IN_COLS)
    gather_o0 = Gather(wo0, gsem.at[1], 0, 512, OUT)
    gather_1 = Gather(w1, gsem.at[2], 0, 1792, COLS)
    gather_z0.plane()
    send_x = send(x_ref, xs.at[own_rows], tsem, 0, tp=other)
    send_cot = send(cot_ref, cots.at[own_rows], tsem, 1, tp=other)
    xs[own_rows, :] = x_ref[...]
    cots[own_rows, :] = cot_ref[...]

    bounds = [lens_ref[0, 0]]
    for j in range(1, 4):
        bounds.append(bounds[-1] + lens_ref[0, j])

    def ids_at(pos):
        total = jnp.zeros(pos.shape, jnp.int32)
        for bound in bounds:
            total = total + (pos >= bound).astype(jnp.int32)
        return total

    pos = lax.broadcasted_iota(jnp.int32, (ROWS, 128), 0)
    ids = ids_at(pos)
    live[...] = (ids < 4).astype(F32)
    for back in range(1, 4):
        same[back - 1] = ((ids == ids_at(pos - back)) & (pos >= back)).astype(F32)
    at = lax.broadcasted_iota(jnp.int32, (ROWS, ROWS), 0)
    src = lax.broadcasted_iota(jnp.int32, (ROWS, ROWS), 1)
    mask[...] = jnp.where((ids_at(at) == ids_at(src)) & (src <= at), 0.0, -1e30)
    smalls[...] = jnp.zeros_like(smalls)

    def spread_rows(part):
        return jnp.broadcast_to(part[0:1, :], (128, ROWS)).T

    def send_rows(which):
        total = jnp.sum(acc[...], axis=1, keepdims=True)
        row_s[which] = jnp.broadcast_to(total, (ROWS, 128)).T[:8, :]
        return send(row_s.at[which], row_r.at[which], tsem, 2 + which, tp=other)

    def norm_layer(layer):
        @pl.loop(0, 4)
        def _(step):
            rows = tile(step, 64)
            part = hid[layer, rows, :]
            scale = lax.rsqrt(jnp.mean(part * part, axis=1, keepdims=True) + EPS)
            scales[layer, rows, :] = jnp.broadcast_to(scale, (64, 128))
            normed[rows, :] = (part * scale * vec_ref[layer, 0:1, :]).astype(BF16)

    def transposed(from_ref, to_ref):
        @pl.loop(0, 8)
        def _(step):
            cols = tile(step, 128)
            to_ref[cols, :] = from_ref[:, cols].astype(F32).T.astype(BF16)

    def conv_pre(layer, signal, cols):
        pre = conv_ref[layer, 4:5, cols] + conv_ref[layer, 3:4, cols] * signal
        shifted = []
        for back in range(1, 4):
            earlier = pltpu.roll(signal, back, 0) * twice(same[back - 1])
            shifted.append(earlier)
            pre = pre + conv_ref[layer, 3 - back : 4 - back, cols] * earlier
        return pre, shifted

    def shift_cols(step):
        return pl.ds(pl.multiple_of(INNER_OWN + step * 256, 256), 256)

    def forward_in(layer):
        norm_layer(layer)

        @pl.loop(0, 9)
        def _(step):
            cols = tile(step, 256)
            proj[layer, :, cols] = dot(normed[...], load_cols(z_ref[layer], cols)).astype(BF16)

        raw = dot(normed[...], load_cols(z_ref[layer], pl.ds(ZX + PAIR, DT)))
        raw = raw.astype(BF16).astype(F32) + head_ref[layer, 0:1, :]
        sig_dt[layer] = jax.nn.sigmoid(raw)
        step_sizes = jnp.maximum(raw, 0.0) + jnp.log1p(jnp.exp(-jnp.abs(raw)))
        steps[layer] = step_sizes
        rate = -jnp.exp(head_ref[layer, 1:2, :])
        lower = (src <= at).astype(F32)
        summed = exact_dot(lower, step_sizes * rate)
        cums[layer] = summed
        cums_t[layer] = summed.T

    def forward_conv(layer):
        @pl.loop(0, 5)
        def _(step):
            signal = proj[layer, :, shift_cols(step)].astype(F32)
            pre, unused = conv_pre(layer, signal, tile(step, 256))
            vals[layer, :, tile(step, 256)] = (pre * jax.nn.sigmoid(pre)).astype(BF16)

    def set_scores(layer):
        b_mat = vals[layer, :, pl.ds(INNER_OWN, STATE)]
        c_mat = vals[layer, :, pl.ds(INNER_OWN + STATE, STATE)]
        scores[...] = dot(c_mat, b_mat, NT)

    def decays(layer, head):
        return jnp.exp(
            column(cums[layer], head) - cums_t[layer, pl.ds(head, 1), :] + mask[...]
        )

    def forward_ssd(layer):
        set_scores(layer)
        acc[...] = jnp.zeros_like(acc)

        @pl.loop(0, 8)
        def _(step):
            cols = tile(step, 128)
            values = vals[layer, :, cols].astype(F32)
            upper = lax.broadcasted_iota(jnp.int32, (ROWS, 128), 1) >= 64
            total = vec_ref[layer, 2:3, cols] * values
            for half in range(2):
                head = 2 * step + half
                weights = (scores[...] * decays(layer, head)).astype(BF16)
                scaled = values * column(steps[layer], head)
                scaled = jnp.where(upper == (half == 1), scaled, 0.0).astype(BF16)
                total = total + dot(weights, scaled)
            ssd[layer, :, cols] = total
            gate = proj[layer, :, cols].astype(F32)
            gated = total * gate * jax.nn.sigmoid(gate)
            acc[...] += gated * gated
            ngate[:, cols] = (gated * vec_ref[layer, 1:2, cols]).astype(BF16)

    def mix_copy(which, step, rows):
        ref_s = mixs.at[which, rows, tile(step, 256)]
        ref_r = mixr.at[which, rows, tile(step, 256)]
        return pltpu.make_async_remote_copy(
            src_ref=ref_s,
            dst_ref=ref_r,
            send_sem=tsem.at[0, 8 + 4 * which + step],
            recv_sem=tsem.at[1, 8 + 4 * which + step],
            device_id={"tp": other},
            device_id_type=MESH,
        )

    def wait_mix(which, rows):
        @pl.loop(0, 4)
        def _(step):
            copy = mix_copy(which, step, rows)
            copy.wait_recv()
            copy.wait_send()

    def forward_out(layer, rows):
        ref, first = o_ref[layer], o_first[layer]

        @pl.loop(0, 4)
        def _(step):
            weight = ref[step, :, :, :, :, pl.ds(first, OUT)].reshape(256, OUT)
            mixs[layer, :, tile(step, 256)] = dot(ngate[...], weight, NT).astype(BF16)
            mix_copy(layer, step, rows).start()

    def take_gate_scale(layer, copy):
        copy.wait_recv()
        total = row_s[layer] + row_r[layer]
        gscales[layer] = spread_rows(lax.rsqrt(total / INNER + EPS))

    def mixed_rows(layer, rows):
        part = mixs[layer, rows, :].astype(F32) + mixr[layer, rows, :].astype(F32)
        return part * (gscales[layer, rows, 0:1] * live[rows, 0:1])

    gather_z0.line()
    send_x.wait_recv()

    @pl.loop(0, 4)
    def _(step):
        rows = tile(step, 64)
        hid[0, rows, :] = xs[rows, :].astype(F32)

    gather_z0.core()
    gather_o0.plane()
    gather_1.plane()
    gather_z0.finish()
    forward_in(0)
    gather_o0.line()
    transposed(normed, norm_t.at[0])
    forward_conv(0)
    gather_o0.core()
    gather_1.line()
    forward_ssd(0)
    squares_0 = send_rows(0)
    gather_o0.finish()
    forward_out(0, pl.ds(0, ROWS))
    gather_1.core()
    take_gate_scale(0, squares_0)
    wait_mix(0, pl.ds(0, ROWS))

    @pl.loop(0, 4)
    def _(step):
        rows = tile(step, 64)
        hid[1, rows, :] = hid[0, rows, :] + mixed_rows(0, rows)

    gather_1.finish()
    forward_in(1)
    transposed(normed, norm_t.at[1])
    forward_conv(1)
    forward_ssd(1)
    squares_1 = send_rows(1)
    forward_out(1, peer_rows)
    send_cot.wait_recv()

    @pl.loop(0, 4)
    def _(step):
        rows = tile(step, 64)
        grad[rows, :] = cots[rows, :].astype(F32)

    take_gate_scale(1, squares_1)

    def backward_gate(layer):
        @pl.loop(0, 4)
        def _(step):
            rows = tile(step, 64)
            cot_b[rows, :] = (live[rows, 0:1] * grad[rows, :]).astype(BF16)

        transposed(cot_b, cot_t)
        acc[...] = jnp.zeros_like(acc)

        @pl.loop(0, 4)
        def _(step):
            cols = tile(step, 256)
            first = pl.ds(pl.multiple_of(o_first[layer] + step * 256, 128), 256)
            d_normed_gate = dot(cot_b[...], load_cols(o_ref[layer], first))
            gate = proj[layer, :, cols].astype(F32)
            gated = ssd[layer, :, cols] * gate * jax.nn.sigmoid(gate)
            normal = gated * twice(gscales[layer])
            gain = vec_ref[layer, 1:2, cols]
            ngate[:, cols] = (normal * gain).astype(BF16)
            smalls[layer, 1:2, cols] = jnp.sum(d_normed_gate * normal, axis=0, keepdims=True)
            weighted = d_normed_gate * gain
            du[:, cols] = weighted
            inner = weighted * gated
            acc[...] += inner[:, :128] + inner[:, 128:]

    def backward_wo(layer):
        ref, first = o_ref[layer], o_first[layer]

        @pl.loop(0, 4)
        def _(step):
            part = dot(cot_t[tile(step, 256), :], ngate[...]).astype(BF16)
            ref[step, :, :, :, :, pl.ds(first, OUT)] = part.reshape(2, 4, 2, 16, OUT)

    def backward_ssd(layer, copy, which):
        copy.wait_recv()
        inner = spread_rows(row_s[which] + row_r[which])
        gs = gscales[layer]
        acc[...] = gs * gs * gs * inner / INNER
        set_scores(layer)
        dscores[...] = jnp.zeros_like(dscores)
        dcum[...] = jnp.zeros_like(dcum)
        dstep[...] = jnp.zeros_like(dstep)

        @pl.loop(0, 8)
        def _(step):
            cols = tile(step, 128)
            lane = lax.broadcasted_iota(jnp.int32, (ROWS, 128), 1)
            upper = lane >= 64
            gate = proj[layer, :, cols].astype(F32)
            out = ssd[layer, :, cols]
            sigmoid = jax.nn.sigmoid(gate)
            silu = gate * sigmoid
            d_gated = gscales[layer] * du[:, cols] - out * silu * acc[...]
            d_out = d_gated * silu
            dproj[:, cols] = (d_gated * out * sigmoid * (1.0 + gate * (1.0 - sigmoid))).astype(BF16)
            values = vals[layer, :, cols].astype(F32)
            size = jnp.where(
                upper, column(steps[layer], 2 * step + 1), column(steps[layer], 2 * step)
            )
            scaled = (values * size).astype(BF16)
            back = jnp.zeros((ROWS, 128), F32)
            for half in range(2):
                head = 2 * step + half
                decay = decays(layer, head)
                weights = (scores[...] * decay).astype(BF16)
                d_half = jnp.where(upper == (half == 1), d_out, 0.0).astype(BF16)
                dscores[...] += dot(d_half, scaled, NT) * decay
                back = back + dot(weights, d_half, TN)
            skip = vec_ref[layer, 2:3, cols]
            dact[:, cols] = skip * d_out + size * back
            smalls[layer, 2:3, cols] = jnp.sum(d_out * values, axis=0, keepdims=True)
            inside = out - skip * values
            turn = d_out.astype(BF16).astype(F32) * inside - scaled.astype(F32) * back
            size_turn = values * back
            for half in range(2):
                head = 2 * step + half
                mine = upper == (half == 1)
                dcum[...] += jnp.where(
                    lane == head,
                    jnp.sum(jnp.where(mine, turn, 0.0), axis=1, keepdims=True),
                    0.0,
                )
                dstep[...] += jnp.where(
                    lane == head,
                    jnp.sum(jnp.where(mine, size_turn, 0.0), axis=1, keepdims=True),
                    0.0,
                )

        rate = -jnp.exp(head_ref[layer, 1:2, :])
        later = (src >= at).astype(F32)
        d_log = exact_dot(later, dcum[...])
        d_raw = (dstep[...] + rate * d_log) * sig_dt[layer]
        smalls[layer, 9:10, pl.ds(256, 128)] = jnp.sum(d_raw, axis=0, keepdims=True)
        smalls[layer, 9:10, pl.ds(384, 128)] = rate * jnp.sum(
            steps[layer] * d_log, axis=0, keepdims=True
        )
        dproj[:, pl.ds(ZX + PAIR, DT)] = d_raw.astype(BF16)
        d_scores = dscores[...].astype(BF16)
        b_mat = vals[layer, :, pl.ds(INNER_OWN, STATE)]
        c_mat = vals[layer, :, pl.ds(INNER_OWN + STATE, STATE)]
        dact[:, pl.ds(INNER_OWN, STATE)] = dot(d_scores, c_mat, TN)
        dact[:, pl.ds(INNER_OWN + STATE, STATE)] = dot(d_scores, b_mat)

    def backward_conv(layer):
        def one(signal_cols, cols):
            signal = proj[layer, :, signal_cols].astype(F32)
            pre, shifted = conv_pre(layer, signal, cols)
            sigmoid = jax.nn.sigmoid(pre)
            d_pre = dact[:, cols] * sigmoid * (1.0 + pre * (1.0 - sigmoid))
            d_signal = conv_ref[layer, 3:4, cols] * d_pre
            d_taps = [jnp.sum(d_pre * signal, axis=0, keepdims=True)]
            for back in range(1, 4):
                d_signal = d_signal + conv_ref[layer, 3 - back : 4 - back, cols] * pltpu.roll(
                    d_pre * twice(same[back - 1]), ROWS - back, 0
                )
                d_taps.append(jnp.sum(d_pre * shifted[back - 1], axis=0, keepdims=True))
            dproj[:, signal_cols] = d_signal.astype(BF16)
            return jnp.sum(d_pre, axis=0, keepdims=True), d_taps

        @pl.loop(0, 4)
        def _(step):
            cols = tile(step, 256)
            d_bias, d_taps = one(shift_cols(step), cols)
            smalls[layer, 3:4, cols] = d_bias
            for back in range(4):
                smalls[layer, 7 - back : 8 - back, cols] = d_taps[back]

        d_bias, d_taps = one(pl.ds(ZX, PAIR), pl.ds(INNER_OWN, PAIR))
        smalls[layer, 9:10, pl.ds(0, PAIR)] = d_bias
        for back in range(4):
            smalls[layer, 8:9, pl.ds((3 - back) * PAIR, PAIR)] = d_taps[back]

    def backward_in(layer, which, rows):
        ref = z_ref[layer]

        @pl.loop(0, 4)
        def _(step):
            cols = tile(step, 256)
            weight = ref[step, :, :, :, :, pl.ds(0, IN_COLS)].reshape(256, IN_COLS)
            part = dot(dproj[...], weight, NT)
            mixs[which, :, cols] = part.astype(BF16)
            mix_copy(which, step, rows).start()
            smalls[layer, 0:1, cols] = jnp.sum(
                part * hid[layer, :, cols] * twice(scales[layer]), axis=0, keepdims=True
            )

    def backward_wz(layer):
        @pl.loop(0, 9)
        def _(step):
            cols = tile(step, 256)
            store_cols(z_ref[layer], cols, dot(norm_t[layer], dproj[:, cols]))

        cols = pl.ds(ZX + PAIR, DT)
        store_cols(z_ref[layer], cols, dot(norm_t[layer], dproj[:, cols]))

    def next_grad(layer, which, rows):
        part = mixs[which, rows, :].astype(F32) + mixr[which, rows, :].astype(F32)
        part = part * vec_ref[layer, 0:1, :]
        before = hid[layer, rows, :]
        scale = scales[layer, rows, 0:1]
        inner = jnp.sum(part * before, axis=1, keepdims=True)
        return grad[rows, :] + scale * part - before * (scale * scale * scale * inner / WIDTH)

    class Smalls:
        def __init__(self, layer):
            self.layer = layer
            self.copies = []

        def start(self, first, count, mine, where, base):
            layer = self.layer
            slots[layer, first + mine] = smalls[layer]
            ref = slots.at[layer, first + mine]
            for step in range(1, count):
                self.copies.append(send(ref, ref, ssem.at[layer], base + step - 1, **where(step)))
            self.pending = self.copies[len(self.copies) - count + 1 :]

        def take(self, first, count):
            layer = self.layer
            for copy in self.pending:
                copy.wait_recv()
            total = slots[layer, first]
            for step in range(1, count):
                total = total + slots[layer, first + step]
            smalls[layer] = total

        def core(self):
            self.start(0, 2, c, lambda step: {"fsdp": index_of(y, z, x, 1 - c)}, 0)

        def along_x(self):
            self.take(0, 2)
            self.start(2, 4, x, lambda step: {"fsdp": index_of(y, z, (x + step) % 4, c)}, 1)

        def along_y(self):
            self.take(2, 4)
            self.start(6, 4, y, lambda step: {"fsdp": index_of((y + step) % 4, z, x, c)}, 4)

        def along_z(self):
            self.take(6, 4)
            self.start(10, 2, z, lambda step: {"fsdp": index_of(y, 1 - z, x, c)}, 7)

        def across(self):
            self.take(10, 2)
            self.start(12, 2, t, lambda step: {"tp": other}, 8)

        def finish(self):
            layer = self.layer
            mine = smalls[layer]
            self.take(12, 2)
            both = smalls[layer]
            row = lax.broadcasted_iota(jnp.int32, both.shape, 0)
            lane = lax.broadcasted_iota(jnp.int32, both.shape, 1)
            shared = (row == 0) | (row == 8) | ((row == 9) & (lane < PAIR))
            small_ref[layer] = jnp.where(shared, both, mine)
            for copy in self.copies:
                copy.wait_send()

    reduce_1 = Reduce(w1, core1, la1, lb1, pa1, pb1, rsem.at[0], 1792, COLS)
    reduce_o0 = Reduce(wo0, coreo, lao, lbo, pao, pbo, rsem.at[1], 512, OUT)
    reduce_z0 = Reduce(wz0, core0, la0, lb0, pa0, pb0, rsem.at[2], 1280, IN_COLS)
    smalls_1, smalls_0 = Smalls(1), Smalls(0)

    backward_gate(1)
    inner_1 = send_rows(2)
    backward_wo(1)
    backward_ssd(1, inner_1, 2)
    backward_conv(1)
    backward_in(1, 2, pl.ds(0, ROWS))
    backward_wz(1)
    reduce_1.core()
    smalls_1.core()
    wait_mix(2, pl.ds(0, ROWS))

    @pl.loop(0, 4)
    def _(step):
        rows = tile(step, 64)
        grad[rows, :] = next_grad(1, 2, rows)

    reduce_1.line()
    smalls_1.along_x()
    wait_mix(1, peer_rows)
    act_ref[...] = (hid[1, own_rows, :] + mixed_rows(1, own_rows)).astype(BF16)

    backward_gate(0)
    inner_0 = send_rows(3)
    backward_wo(0)
    reduce_o0.core()
    backward_ssd(0, inner_0, 3)
    smalls_1.along_y()
    reduce_1.plane()
    reduce_o0.line()
    backward_conv(0)
    smalls_1.along_z()
    backward_in(0, 3, peer_rows)
    reduce_o0.plane()
    reduce_1.finish(gw_ref.at[1])
    bc_s[1] = gw_ref[1, :, pl.ds(ZX, PAIR)]
    bc_1 = send(bc_s.at[1], bc_r.at[1], tsem, 6, tp=other)
    smalls_1.across()
    backward_wz(0)
    reduce_z0.core()
    smalls_0.core()
    wait_mix(3, peer_rows)
    gin_ref[...] = next_grad(0, 3, own_rows)
    reduce_z0.line()
    smalls_0.along_x()
    smalls_1.finish()
    reduce_o0.finish(gw_ref.at[0, :, pl.ds(IN_COLS, OUT)])
    smalls_0.along_y()
    reduce_z0.plane()
    smalls_0.along_z()
    reduce_z0.finish(gw_ref.at[0, :, pl.ds(0, IN_COLS)])
    bc_s[0] = gw_ref[0, :, pl.ds(ZX, PAIR)]
    bc_0 = send(bc_s.at[0], bc_r.at[0], tsem, 7, tp=other)
    smalls_0.across()
    for layer, copy in ((1, bc_1), (0, bc_0)):
        copy.wait_recv()
        gw_ref[layer, :, pl.ds(ZX, PAIR)] = bc_s[layer] + bc_r[layer]
        copy.wait_send()
    smalls_0.finish()
    for copy in (send_x, send_cot, squares_0, squares_1, inner_1, inner_0):
        copy.wait_send()


def reduce_scratch(width, half):
    return [
        pltpu.VMEM((4, 2, 4, 16, width), BF16),
        pltpu.VMEM((3, 2, 4, 16, half), BF16),
        pltpu.VMEM((3, 4, 2, 16, width - half), BF16),
        pltpu.VMEM((7, 16, half), BF16),
        pltpu.VMEM((7, 16, width - half), BF16),
    ]


def whole_step(x_in, cotangent, own, lengths, vec, conv, head):
    scratch = [
        pltpu.VMEM((4, 2, 4, 2, 16, IN_COLS), BF16),
        pltpu.VMEM((4, 2, 4, 2, 16, OUT), BF16),
        pltpu.VMEM((4, 2, 4, 2, 16, COLS), BF16),
        pltpu.VMEM((2, ROWS, WIDTH), F32),
        pltpu.VMEM((2, WIDTH, ROWS), BF16),
        pltpu.VMEM((2, ROWS, ZX + PAIR), BF16),
        pltpu.VMEM((2, ROWS, SIGNAL), BF16),
        pltpu.VMEM((2, ROWS, INNER_OWN), F32),
        pltpu.VMEM((ROWS, INNER_OWN), BF16),
        pltpu.VMEM((2, ROWS, 128), F32),
        pltpu.VMEM((2, ROWS, 128), F32),
        pltpu.VMEM((2, 128, ROWS), F32),
        pltpu.VMEM((2, ROWS, 128), F32),
        pltpu.VMEM((2, ROWS, 128), F32),
        pltpu.VMEM((2, ROWS, 128), F32),
        pltpu.VMEM((ROWS, WIDTH), BF16),
        pltpu.VMEM((ROWS, WIDTH), BF16),
        pltpu.VMEM((ROWS, WIDTH), BF16),
        pltpu.VMEM((ROWS, WIDTH), BF16),
        pltpu.VMEM((WIDTH, ROWS), BF16),
        pltpu.VMEM((ROWS, WIDTH), F32),
        pltpu.VMEM((ROWS, INNER_OWN), F32),
        pltpu.VMEM((ROWS, SIGNAL), F32),
        pltpu.VMEM((ROWS, IN_COLS), BF16),
        pltpu.VMEM((ROWS, ROWS), F32),
        pltpu.VMEM((ROWS, ROWS), F32),
        pltpu.VMEM((ROWS, ROWS), F32),
        pltpu.VMEM((3, ROWS, 128), F32),
        pltpu.VMEM((ROWS, 128), F32),
        pltpu.VMEM((ROWS, 128), F32),
        pltpu.VMEM((ROWS, 128), F32),
        pltpu.VMEM((ROWS, 128), F32),
        pltpu.VMEM((4, ROWS, WIDTH), BF16),
        pltpu.VMEM((4, ROWS, WIDTH), BF16),
        pltpu.VMEM((4, 8, ROWS), F32),
        pltpu.VMEM((4, 8, ROWS), F32),
        pltpu.VMEM((2, 16, 1024), F32),
        pltpu.VMEM((2, 14, 16, 1024), F32),
        pltpu.VMEM((2, 16, PAIR), F32),
        pltpu.VMEM((2, 16, PAIR), F32),
        *reduce_scratch(COLS, 1792),
        *reduce_scratch(IN_COLS, 1280),
        *reduce_scratch(OUT, 512),
        pltpu.SemaphoreType.DMA((3, 2, GATHER_COPIES)),
        pltpu.SemaphoreType.DMA((3, 2, REDUCE_COPIES)),
        pltpu.SemaphoreType.DMA((2, 24)),
        pltpu.SemaphoreType.DMA((2, 2, 9)),
        pltpu.SemaphoreType.DMA((3,)),
    ]
    vmem = pl.BlockSpec(memory_space=pltpu.VMEM)
    return pl.pallas_call(
        body,
        out_shape=(
            jax.ShapeDtypeStruct((128, WIDTH), BF16),
            jax.ShapeDtypeStruct((128, WIDTH), F32),
            jax.ShapeDtypeStruct((2, 16, COLS), F32),
            jax.ShapeDtypeStruct((2, 16, 1024), F32),
        ),
        in_specs=[vmem, vmem, vmem, pl.BlockSpec(memory_space=pltpu.SMEM), vmem, vmem, vmem],
        out_specs=(vmem, vmem, vmem, vmem),
        scratch_shapes=scratch,
        compiler_params=pltpu.CompilerParams(
            collective_id=0, has_side_effects=True, vmem_limit_bytes=60 << 20
        ),
        name="whole_step",
    )(x_in, cotangent, own, lengths, vec, conv, head)


def shards(
    x_in, cotangent, seq_lengths, gain_in, w_zx, w_bc, w_dt, conv_x, conv_bc,
    bias_x, bias_bc, dt_bias, a_log, skip, gain_gate, w_out,
):
    def wide(part, width):
        return jnp.pad(part, ((0, 0), (0, 0), (0, width - part.shape[-1])))

    own = jnp.concatenate(
        [w_zx.reshape(2, 16, ZX), w_bc, wide(w_dt, DT), jnp.swapaxes(w_out, 1, 2)], axis=2
    )
    vec = jnp.stack([gain_in, gain_gate, jnp.repeat(skip, 64, axis=1)], axis=1)
    vec = jnp.pad(vec, ((0, 0), (0, 5), (0, 0))).astype(F32)
    conv = jnp.concatenate(
        [
            jnp.concatenate([conv_x, conv_bc], axis=2),
            jnp.concatenate([bias_x, bias_bc], axis=1)[:, None, :],
        ],
        axis=1,
    )
    conv = jnp.pad(conv, ((0, 0), (0, 3), (0, 0))).astype(F32)
    head = wide(jnp.stack([dt_bias, a_log], axis=1), 128)
    head = jnp.pad(head, ((0, 0), (0, 6), (0, 0))).astype(F32)
    act_out, grad_in, grad_w, small = whole_step(
        x_in, cotangent, own, seq_lengths, vec, conv, head
    )
    return (
        act_out,
        grad_in,
        small[:, 0],
        grad_w[:, :, :ZX].reshape(2, 16, 2, INNER_OWN),
        grad_w[:, :, ZX : ZX + PAIR],
        grad_w[:, :, ZX + PAIR : ZX + PAIR + HEADS_OWN],
        small[:, 4:8],
        small[:, 8].reshape(2, 4, PAIR),
        small[:, 3],
        small[:, 9, :PAIR],
        small[:, 9, 256 : 256 + HEADS_OWN],
        small[:, 9, 384 : 384 + HEADS_OWN],
        small[:, 2].reshape(2, HEADS_OWN, 64).sum(axis=2),
        small[:, 1],
        jnp.swapaxes(grad_w[:, :, IN_COLS:], 1, 2),
    )


def solution(mesh):
    placed = (
        P(("fsdp", "tp"), None),
        P(("fsdp", "tp"), None),
        P("fsdp", None),
        P(),
        P(None, "fsdp", None, "tp"),
        P(None, "fsdp", None),
        P(None, "fsdp", "tp"),
        P(None, None, "tp"),
        P(),
        P(None, "tp"),
        P(),
        P(None, "tp"),
        P(None, "tp"),
        P(None, "tp"),
        P(None, "tp"),
        P(None, "tp", "fsdp"),
    )
    return jax.shard_map(
        shards,
        mesh=mesh,
        in_specs=placed,
        out_specs=(
            P(("fsdp", "tp"), None),
            P(("fsdp", "tp"), None),
            P(),
            P(None, "fsdp", None, "tp"),
            P(None, "fsdp", None),
            P(None, "fsdp", "tp"),
            P(None, None, "tp"),
            P(),
            P(None, "tp"),
            P(),
            P(None, "tp"),
            P(None, "tp"),
            P(None, "tp"),
            P(None, "tp"),
            P(None, "tp", "fsdp"),
        ),
        check_vma=False,
    )
```

```python
import jax
import jax.numpy as jnp
from jax import lax
from jax.experimental import pallas as pl
from jax.experimental.pallas import tpu as pltpu
from jax.sharding import PartitionSpec as P

MESH = pl.DeviceIdType.MESH
INNER = 2048
EPS = 1e-05


def place():
    index = lax.axis_index("fsdp")
    return index // 16, (index // 8) % 2, (index // 2) % 4, index % 2


def index_of(y, z, x, c):
    return ((y * 2 + z) * 4 + x) * 2 + c


PLANE_ZX = [(dz, dx) for dz in range(2) for dx in range(4) if (dz, dx) != (0, 0)]
PLANE_YZ = [(dy, dz) for dy in range(4) for dz in range(2) if (dy, dz) != (0, 0)]


def peers_of():
    y, z, x, c = place()
    found = [index_of(y, (z + dz) % 2, (x + dx) % 4, c) for dz, dx in PLANE_ZX]
    found += [index_of((y + dy) % 4, (z + dz) % 2, x, c) for dy, dz in PLANE_YZ if dy != 0]
    found.append(index_of(y, z, x, 1 - c))
    return found


def greet_all(with_tp):
    barrier = pltpu.get_barrier_semaphore()
    peers = peers_of()
    for peer in peers:
        pl.semaphore_signal(barrier, inc=1, device_id={"fsdp": peer}, device_id_type=MESH)
    count = len(peers)
    if with_tp:
        other = 1 - lax.axis_index("tp")
        pl.semaphore_signal(barrier, inc=1, device_id={"tp": other}, device_id_type=MESH)
        count += 1
    pl.semaphore_wait(barrier, count)


def send(src, dst, sems, slot, **where):
    copy = pltpu.make_async_remote_copy(
        src_ref=src,
        dst_ref=dst,
        send_sem=sems.at[0, slot],
        recv_sem=sems.at[1, slot],
        device_id=where,
        device_id_type=MESH,
    )
    copy.start()
    return copy


GATHER_COPIES = 30


class Gather:
    def __init__(self, whole, sems, first, half, end):
        self.whole, self.sems = whole, sems
        self.cols = (pl.ds(first, half - first), pl.ds(half, end - half))
        self.started = []

    def plane(self):
        y, z, x, c = place()
        cols_a, cols_b = self.cols
        self.first = []
        for slot, (dz, dx) in enumerate(PLANE_ZX):
            ref = self.whole.at[y, z, x, c, :, cols_a]
            self.first.append(
                send(ref, ref, self.sems, slot, fsdp=index_of(y, (z + dz) % 2, (x + dx) % 4, c))
            )
        for slot, (dy, dz) in enumerate(PLANE_YZ):
            ref = self.whole.at[y, z, x, c, :, cols_b]
            self.first.append(
                send(ref, ref, self.sems, 7 + slot, fsdp=index_of((y + dy) % 4, (z + dz) % 2, x, c))
            )

    def line(self):
        y, z, x, c = place()
        cols_a, cols_b = self.cols
        for copy in self.first:
            copy.wait_recv()
        self.second = []
        for slot, step in enumerate((1, 3)):
            ref = self.whole.at[y, :, :, c, :, cols_a]
            self.second.append(
                send(ref, ref, self.sems, 14 + slot, fsdp=index_of((y + step) % 4, z, x, c))
            )
            ref = self.whole.at[:, :, x, c, :, cols_b]
            self.second.append(
                send(ref, ref, self.sems, 16 + slot, fsdp=index_of(y, z, (x + step) % 4, c))
            )
        self.third = []
        self.hand_over(0)

    def hand_over(self, step):
        y, z, x, c = place()
        cols_a, cols_b = self.cols
        ref = self.whole.at[(y - step + 4) % 4, :, :, c, :, cols_a]
        self.third.append(send(ref, ref, self.sems, 22 + step, fsdp=index_of(y, z, x, 1 - c)))
        ref = self.whole.at[:, :, (x - step + 4) % 4, c, :, cols_b]
        self.third.append(send(ref, ref, self.sems, 26 + step, fsdp=index_of(y, z, x, 1 - c)))

    def relay(self):
        y, z, x, c = place()
        cols_a, cols_b = self.cols
        self.fourth = []
        for slot, step in enumerate((1, 3)):
            self.second[2 * slot].wait_recv()
            ref = self.whole.at[(y - step + 4) % 4, slot, :, c, :, cols_a]
            self.fourth.append(
                send(ref, ref, self.sems, 18 + slot, fsdp=index_of((y + step) % 4, z, x, c))
            )
            self.second[2 * slot + 1].wait_recv()
            ref = self.whole.at[:, slot, (x - step + 4) % 4, c, :, cols_b]
            self.fourth.append(
                send(ref, ref, self.sems, 20 + slot, fsdp=index_of(y, z, (x + step) % 4, c))
            )
        self.hand_over(1)
        self.hand_over(3)

    def core(self):
        for copy in self.fourth:
            copy.wait_recv()
        self.hand_over(2)

    def finish(self):
        for copy in self.third:
            copy.wait_recv()
        for copy in self.first + self.second + self.third + self.fourth:
            copy.wait_send()


REDUCE_COPIES = 27


class Reduce:
    def __init__(
        self, grad, from_core, from_line_a, from_line_b, from_plane_a, from_plane_b, relay_a, relay_b, sems, half, end
    ):
        self.grad, self.from_core, self.sems = grad, from_core, sems
        self.line_a, self.line_b = from_line_a, from_line_b
        self.plane_a, self.plane_b = from_plane_a, from_plane_b
        self.relay_a, self.relay_b = relay_a, relay_b
        self.cols = (pl.ds(0, half), pl.ds(half, end - half))

    def core(self):
        y, z, x, c = place()
        self.copies = [
            send(
                self.grad.at[:, :, :, 1 - c],
                self.from_core,
                self.sems,
                0,
                fsdp=index_of(y, z, x, 1 - c),
            )
        ]

    def line(self):
        y, z, x, c = place()
        cols_a, cols_b = self.cols
        self.copies[0].wait_recv()

        @pl.loop(0, 32)
        def _(block):
            iy, iz, ix = block // 8, (block // 4) % 2, block % 4
            mine = self.grad[iy, iz, ix, c].astype(jnp.float32)
            theirs = self.from_core[iy, iz, ix].astype(jnp.float32)
            self.from_core[iy, iz, ix] = (mine + theirs).astype(jnp.bfloat16)

        self.relays, self.second = [], []
        for slot, step in enumerate((1, 3)):
            to, far = (y + step) % 4, (y + 2) % 4
            where = index_of(to, z, x, c)
            self.relays.append(
                send(self.from_core.at[far, slot, :, :, cols_a], self.relay_a.at[slot], self.sems, 1 + slot, fsdp=where)
            )
            self.second.append(
                send(
                    self.from_core.at[to, 1 - slot, :, :, cols_a],
                    self.line_a.at[slot, 1 - slot],
                    self.sems,
                    3 + slot,
                    fsdp=where,
                )
            )
            to, far = (x + step) % 4, (x + 2) % 4
            where = index_of(y, z, to, c)
            self.relays.append(
                send(self.from_core.at[:, slot, far, :, cols_b], self.relay_b.at[slot], self.sems, 5 + slot, fsdp=where)
            )
            self.second.append(
                send(
                    self.from_core.at[:, 1 - slot, to, :, cols_b],
                    self.line_b.at[slot, :, 1 - slot],
                    self.sems,
                    7 + slot,
                    fsdp=where,
                )
            )

    def relay(self):
        y, z, x, c = place()
        cols_a, cols_b = self.cols
        for copy in self.relays:
            copy.wait_recv()
        for slot, step in enumerate((1, 3)):
            to_y, to_x = (y + step) % 4, (x + step) % 4

            @pl.loop(0, 4)
            def _(block):
                mine = self.from_core[to_y, slot, block, :, cols_a].astype(jnp.float32)
                mine = mine + self.relay_a[slot, block].astype(jnp.float32)
                self.from_core[to_y, slot, block, :, cols_a] = mine.astype(jnp.bfloat16)
                mine = self.from_core[block, slot, to_x, :, cols_b].astype(jnp.float32)
                mine = mine + self.relay_b[slot, block].astype(jnp.float32)
                self.from_core[block, slot, to_x, :, cols_b] = mine.astype(jnp.bfloat16)

            self.second.append(
                send(
                    self.from_core.at[to_y, slot, :, :, cols_a],
                    self.line_a.at[slot, slot],
                    self.sems,
                    9 + slot,
                    fsdp=index_of(to_y, z, x, c),
                )
            )
            self.second.append(
                send(
                    self.from_core.at[:, slot, to_x, :, cols_b],
                    self.line_b.at[slot, :, slot],
                    self.sems,
                    11 + slot,
                    fsdp=index_of(y, z, to_x, c),
                )
            )

    def plane(self):
        y, z, x, c = place()
        cols_a, cols_b = self.cols
        for copy in self.second:
            copy.wait_recv()

        @pl.loop(0, 8)
        def _(block):
            iz, ix = block // 4, block % 4
            total = self.from_core[y, iz, ix, :, cols_a].astype(jnp.float32)
            for step in range(2):
                total = total + self.line_a[step, iz, ix].astype(jnp.float32)
            self.line_a[0, iz, ix] = total.astype(jnp.bfloat16)
            iy, iz = block // 2, block % 2
            total = self.from_core[iy, iz, x, :, cols_b].astype(jnp.float32)
            for step in range(2):
                total = total + self.line_b[step, iy, iz].astype(jnp.float32)
            self.line_b[0, iy, iz] = total.astype(jnp.bfloat16)

        self.third = []
        for slot, (dz, dx) in enumerate(PLANE_ZX):
            tz, tx = (z + dz) % 2, (x + dx) % 4
            self.third.append(
                send(
                    self.line_a.at[0, tz, tx],
                    self.plane_a.at[slot],
                    self.sems,
                    13 + slot,
                    fsdp=index_of(y, tz, tx, c),
                )
            )
        for slot, (dy, dz) in enumerate(PLANE_YZ):
            ty, tz = (y + dy) % 4, (z + dz) % 2
            self.third.append(
                send(
                    self.line_b.at[0, ty, tz],
                    self.plane_b.at[slot],
                    self.sems,
                    20 + slot,
                    fsdp=index_of(ty, tz, x, c),
                )
            )

    def finish(self, out):
        y, z, x, c = place()
        cols_a, cols_b = self.cols
        for copy in self.third:
            copy.wait_recv()
        total = self.line_a[0, z, x].astype(jnp.float32)
        for slot in range(7):
            total = total + self.plane_a[slot].astype(jnp.float32)
        out[:, cols_a] = total
        total = self.line_b[0, y, z].astype(jnp.float32)
        for slot in range(7):
            total = total + self.plane_b[slot].astype(jnp.float32)
        out[:, cols_b] = total
        for copy in self.copies + self.relays + self.second + self.third:
            copy.wait_send()


ROWS, WIDTH, INNER_OWN, STATE, HEADS_OWN = 256, 1024, 1024, 128, 16
ZX, PAIR, DT, OUT = 2048, 256, 128, 1024
SIGNAL = INNER_OWN + PAIR
XS = SIGNAL + DT
PARTS = (XS, INNER_OWN, OUT)
HALVES = (768, 512, 512)
F32, BF16 = jnp.float32, jnp.bfloat16
NN = (((1,), (0,)), ((), ()))
NT = (((1,), (1,)), ((), ()))
TN = (((0,), (0,)), ((), ()))


def dot(a, b, dims=NN):
    return lax.dot_general(a, b, dims, preferred_element_type=F32)


def exact_dot(a, b, dims=NN):
    return lax.dot_general(
        a, b, dims, preferred_element_type=F32, precision=lax.Precision.HIGHEST
    )


def tile(index, width):
    return pl.ds(pl.multiple_of(index * width, width), width)


def twice(part):
    return jnp.concatenate([part, part], axis=1)


def column(part, head):
    lane = lax.broadcasted_iota(jnp.int32, part.shape, 1)
    return jnp.sum(jnp.where(lane == head, part, 0.0), axis=1, keepdims=True)


def body(
    x_ref, cot_ref, own_ref, lens_ref, vec_ref, conv_ref, head_ref,
    act_ref, gin_ref, gx_ref, gg_ref, go_ref, small_ref,
    wx0, wg0, wo0, wx1, wg1, wo1,
    hid, norm_t, proj, vals, ssd, ngate, steps, cums, cums_t, scales, gscales, sig_dt,
    xs, cots, normed, cot_t, grad, dact, dproj, scores, dscores, mask, same, live, acc, dcum, dstep,
    mixs, mixr, row_s, row_r, smalls, slots, bc_s, bc_r,
    *rest,
):
    buffers, (gg0, gx0, gsem, rsem, tsem, ssem, lsem) = rest[:42], rest[42:]
    y, z, x, c = place()
    t = lax.axis_index("tp")
    other = 1 - t
    own_rows = pl.ds(pl.multiple_of(t * 128, 128), 128)
    peer_rows = pl.ds(pl.multiple_of(other * 128, 128), 128)

    def load_cols(ref, cols):
        part = ref[:, :, :, :, :, cols]
        return part.reshape(WIDTH, part.shape[-1])

    def store_cols(ref, cols, part):
        ref[:, :, :, :, :, cols] = part.astype(BF16).reshape(4, 2, 4, 2, 16, part.shape[-1])

    x_w, g_w, o_w = (wx0, wx1), (wg0, wg1), (wo0, wo1)
    whole = (wx0, wg0, wo0, wx1, wg1, wo1)
    gate_grads, signal_grads = (gg0, wg1), (gx0, wx1)
    all_grads = (gx0, gg0, wo0, wx1, wg1, wo1)

    keeps = []
    for slot, ref in enumerate(whole):
        first = sum(PARTS[: slot % 3])
        keeps.append(
            pltpu.make_async_copy(
                own_ref.at[slot // 3, :, pl.ds(first, PARTS[slot % 3])],
                ref.at[y, z, x, c],
                lsem.at[slot],
            )
        )
        keeps[-1].start()
    greet_all(True)
    gather_x0, gather_g0, gather_o0, gather_x1, gather_g1, gather_o1 = [
        Gather(ref, gsem.at[slot], 0, HALVES[slot % 3], PARTS[slot % 3])
        for slot, ref in enumerate(whole)
    ]
    keeps[0].wait()
    gather_x0.plane()
    for keep in keeps[1:]:
        keep.wait()
    xs[own_rows, :] = x_ref[...]
    cots[own_rows, :] = cot_ref[...]

    bounds = [lens_ref[0, 0]]
    for j in range(1, 4):
        bounds.append(bounds[-1] + lens_ref[0, j])

    def ids_at(pos):
        total = jnp.zeros(pos.shape, jnp.int32)
        for bound in bounds:
            total = total + (pos >= bound).astype(jnp.int32)
        return total

    pos = lax.broadcasted_iota(jnp.int32, (ROWS, 128), 0)
    ids = ids_at(pos)
    live[...] = (ids < 4).astype(F32)
    for back in range(1, 4):
        same[back - 1] = ((ids == ids_at(pos - back)) & (pos >= back)).astype(F32)
    at = lax.broadcasted_iota(jnp.int32, (ROWS, ROWS), 0)
    src = lax.broadcasted_iota(jnp.int32, (ROWS, ROWS), 1)
    mask[...] = jnp.where((ids_at(at) == ids_at(src)) & (src <= at), 0.0, -1e30)
    smalls[...] = jnp.zeros_like(smalls)

    def spread_rows(part):
        return jnp.broadcast_to(part[0:1, :], (128, ROWS)).T

    def send_rows(which):
        total = jnp.sum(acc[...], axis=1, keepdims=True)
        row_s[which] = jnp.broadcast_to(total, (ROWS, 128)).T[:8, :]
        return send(row_s.at[which], row_r.at[which], tsem, 2 + which, tp=other)

    def norm_layer(layer):
        @pl.loop(0, 4)
        def _(step):
            rows = tile(step, 64)
            part = hid[layer, rows, :]
            scale = lax.rsqrt(jnp.mean(part * part, axis=1, keepdims=True) + EPS)
            scales[layer, rows, :] = jnp.broadcast_to(scale, (64, 128))
            normed[rows, :] = (part * scale * vec_ref[layer, 0:1, :]).astype(BF16)

    def transposed(from_ref, to_ref):
        @pl.loop(0, 8)
        def _(step):
            cols = tile(step, 128)
            to_ref[cols, :] = from_ref[:, cols].astype(F32).T.astype(BF16)

    def conv_pre(layer, signal, cols):
        pre = conv_ref[layer, 4:5, cols] + conv_ref[layer, 3:4, cols] * signal
        shifted = []
        for back in range(1, 4):
            earlier = pltpu.roll(signal, back, 0) * twice(same[back - 1])
            shifted.append(earlier)
            pre = pre + conv_ref[layer, 3 - back : 4 - back, cols] * earlier
        return pre, shifted

    def shift_cols(step):
        return pl.ds(pl.multiple_of(INNER_OWN + step * 256, 256), 256)

    def project_gate(layer):
        @pl.loop(0, 4)
        def _(step):
            cols = tile(step, 256)
            proj[layer, :, cols] = dot(normed[...], load_cols(g_w[layer], cols)).astype(BF16)

    def project_signal(layer):
        @pl.loop(0, 5)
        def _(step):
            part = dot(normed[...], load_cols(x_w[layer], tile(step, 256)))
            proj[layer, :, shift_cols(step)] = part.astype(BF16)

    def forward_steps(layer):
        raw = dot(normed[...], load_cols(x_w[layer], pl.ds(SIGNAL, DT)))
        raw = raw.astype(BF16).astype(F32) + head_ref[layer, 0:1, :]
        sig_dt[layer] = jax.nn.sigmoid(raw)
        step_sizes = jnp.maximum(raw, 0.0) + jnp.log1p(jnp.exp(-jnp.abs(raw)))
        steps[layer] = step_sizes
        rate = -jnp.exp(head_ref[layer, 1:2, :])
        lower = (src <= at).astype(F32)
        summed = exact_dot(lower, step_sizes * rate)
        cums[layer] = summed
        cums_t[layer] = summed.T

    def forward_conv(layer):
        @pl.loop(0, 5)
        def _(step):
            signal = proj[layer, :, shift_cols(step)].astype(F32)
            pre, unused = conv_pre(layer, signal, tile(step, 256))
            vals[layer, :, tile(step, 256)] = (pre * jax.nn.sigmoid(pre)).astype(BF16)

    def set_scores(layer):
        b_mat = vals[layer, :, pl.ds(INNER_OWN, STATE)]
        c_mat = vals[layer, :, pl.ds(INNER_OWN + STATE, STATE)]
        scores[...] = dot(c_mat, b_mat, NT)

    def decays(layer, head):
        return jnp.exp(
            column(cums[layer], head) - cums_t[layer, pl.ds(head, 1), :] + mask[...]
        )

    def forward_ssd(layer):
        set_scores(layer)

        @pl.loop(0, 8)
        def _(step):
            cols = tile(step, 128)
            values = vals[layer, :, cols].astype(F32)
            upper = lax.broadcasted_iota(jnp.int32, (ROWS, 128), 1) >= 64
            total = vec_ref[layer, 2:3, cols] * values
            for half in range(2):
                head = 2 * step + half
                weights = (scores[...] * decays(layer, head)).astype(BF16)
                scaled = values * column(steps[layer], head)
                scaled = jnp.where(upper == (half == 1), scaled, 0.0).astype(BF16)
                total = total + dot(weights, scaled)
            ssd[layer, :, cols] = total

    def forward_gate(layer):
        acc[...] = jnp.zeros_like(acc)

        @pl.loop(0, 8)
        def _(step):
            cols = tile(step, 128)
            gate = proj[layer, :, cols].astype(F32)
            gated = ssd[layer, :, cols] * gate * jax.nn.sigmoid(gate)
            acc[...] += gated * gated
            ngate[:, cols] = (gated * vec_ref[layer, 1:2, cols]).astype(BF16)

    def mix_copy(which, step, rows):
        ref_s = mixs.at[which, rows, tile(step, 256)]
        ref_r = mixr.at[which, rows, tile(step, 256)]
        return pltpu.make_async_remote_copy(
            src_ref=ref_s,
            dst_ref=ref_r,
            send_sem=tsem.at[0, 8 + 4 * which + step],
            recv_sem=tsem.at[1, 8 + 4 * which + step],
            device_id={"tp": other},
            device_id_type=MESH,
        )

    def wait_mix(which, rows):
        @pl.loop(0, 4)
        def _(step):
            copy = mix_copy(which, step, rows)
            copy.wait_recv()
            copy.wait_send()

    def forward_out(layer, rows):
        @pl.loop(0, 4)
        def _(step):
            weight = o_w[layer][step].reshape(256, OUT)
            mixs[layer, :, tile(step, 256)] = dot(ngate[...], weight, NT).astype(BF16)
            mix_copy(layer, step, rows).start()

    def take_gate_scale(layer, copy):
        copy.wait_recv()
        total = row_s[layer] + row_r[layer]
        gscales[layer] = spread_rows(lax.rsqrt(total / INNER + EPS))

    def mixed_rows(layer, rows):
        part = mixs[layer, rows, :].astype(F32) + mixr[layer, rows, :].astype(F32)
        return part * (gscales[layer, rows, 0:1] * live[rows, 0:1])

    gather_x0.line()
    gather_g0.plane()
    send_x = send(x_ref, xs.at[own_rows], tsem, 0, tp=other)
    gather_o0.plane()
    gather_x0.relay()
    gather_g0.line()
    gather_x0.core()
    send_x.wait_recv()

    @pl.loop(0, 4)
    def _(step):
        rows = tile(step, 64)
        hid[0, rows, :] = xs[rows, :].astype(F32)

    norm_layer(0)
    gather_x0.finish()
    gather_o0.line()
    gather_x1.plane()
    gather_g1.plane()
    gather_o1.plane()
    project_signal(0)
    gather_g0.relay()
    forward_steps(0)
    forward_conv(0)
    gather_g0.core()
    gather_o0.relay()
    gather_x1.line()
    forward_ssd(0)
    gather_g0.finish()
    project_gate(0)
    forward_gate(0)
    squares_0 = send_rows(0)
    gather_o0.core()
    gather_x1.relay()
    gather_g1.line()
    gather_o0.finish()
    forward_out(0, pl.ds(0, ROWS))
    transposed(normed, norm_t.at[0])
    gather_x1.core()
    gather_g1.relay()
    gather_o1.line()
    take_gate_scale(0, squares_0)
    gather_x1.finish()
    wait_mix(0, pl.ds(0, ROWS))
    send_cot = send(cot_ref, cots.at[own_rows], tsem, 1, tp=other)

    @pl.loop(0, 4)
    def _(step):
        rows = tile(step, 64)
        hid[1, rows, :] = hid[0, rows, :] + mixed_rows(0, rows)

    norm_layer(1)
    project_signal(1)
    gather_g1.core()
    forward_steps(1)
    gather_o1.relay()
    forward_conv(1)
    transposed(normed, norm_t.at[1])
    forward_ssd(1)
    gather_o1.core()
    gather_g1.finish()
    project_gate(1)
    forward_gate(1)
    squares_1 = send_rows(1)
    gather_o1.finish()
    forward_out(1, peer_rows)
    send_cot.wait_recv()

    @pl.loop(0, 4)
    def _(step):
        rows = tile(step, 64)
        grad[rows, :] = cots[rows, :].astype(F32)

    take_gate_scale(1, squares_1)

    def backward_gate(layer):
        @pl.loop(0, 4)
        def _(step):
            rows = tile(step, 64)
            normed[rows, :] = (live[rows, 0:1] * grad[rows, :]).astype(BF16)

        transposed(normed, cot_t)
        acc[...] = jnp.zeros_like(acc)

        @pl.loop(0, 4)
        def _(step):
            cols = tile(step, 256)
            d_normed_gate = dot(normed[...], load_cols(o_w[layer], cols))
            gate = proj[layer, :, cols].astype(F32)
            gated = ssd[layer, :, cols] * gate * jax.nn.sigmoid(gate)
            normal = gated * twice(gscales[layer])
            gain = vec_ref[layer, 1:2, cols]
            ngate[:, cols] = (normal * gain).astype(BF16)
            smalls[layer, 1:2, cols] = jnp.sum(d_normed_gate * normal, axis=0, keepdims=True)
            weighted = d_normed_gate * gain
            dact[:, cols] = weighted
            inner = weighted * gated
            acc[...] += inner[:, :128] + inner[:, 128:]

    def backward_wo(layer):
        @pl.loop(0, 4)
        def _(step):
            part = dot(cot_t[tile(step, 256), :], ngate[...]).astype(BF16)
            o_w[layer][step] = part.reshape(2, 4, 2, 16, OUT)

    def backward_ssd(layer, copy, which):
        copy.wait_recv()
        inner = spread_rows(row_s[which] + row_r[which])
        gs = gscales[layer]
        acc[...] = gs * gs * gs * inner / INNER
        set_scores(layer)
        dscores[...] = jnp.zeros_like(dscores)
        dcum[...] = jnp.zeros_like(dcum)
        dstep[...] = jnp.zeros_like(dstep)

        @pl.loop(0, 8)
        def _(step):
            cols = tile(step, 128)
            lane = lax.broadcasted_iota(jnp.int32, (ROWS, 128), 1)
            upper = lane >= 64
            gate = proj[layer, :, cols].astype(F32)
            out = ssd[layer, :, cols]
            sigmoid = jax.nn.sigmoid(gate)
            silu = gate * sigmoid
            d_gated = gscales[layer] * dact[:, cols] - out * silu * acc[...]
            d_out = d_gated * silu
            dproj[:, cols] = (d_gated * out * sigmoid * (1.0 + gate * (1.0 - sigmoid))).astype(BF16)
            values = vals[layer, :, cols].astype(F32)
            size = jnp.where(
                upper, column(steps[layer], 2 * step + 1), column(steps[layer], 2 * step)
            )
            scaled = (values * size).astype(BF16)
            back = jnp.zeros((ROWS, 128), F32)
            for half in range(2):
                head = 2 * step + half
                decay = decays(layer, head)
                weights = (scores[...] * decay).astype(BF16)
                d_half = jnp.where(upper == (half == 1), d_out, 0.0).astype(BF16)
                dscores[...] += dot(d_half, scaled, NT) * decay
                back = back + dot(weights, d_half, TN)
            skip = vec_ref[layer, 2:3, cols]
            dact[:, cols] = skip * d_out + size * back
            smalls[layer, 2:3, cols] = jnp.sum(d_out * values, axis=0, keepdims=True)
            inside = out - skip * values
            turn = d_out.astype(BF16).astype(F32) * inside - scaled.astype(F32) * back
            size_turn = values * back
            for half in range(2):
                head = 2 * step + half
                mine = upper == (half == 1)
                dcum[...] += jnp.where(
                    lane == head,
                    jnp.sum(jnp.where(mine, turn, 0.0), axis=1, keepdims=True),
                    0.0,
                )
                dstep[...] += jnp.where(
                    lane == head,
                    jnp.sum(jnp.where(mine, size_turn, 0.0), axis=1, keepdims=True),
                    0.0,
                )

        rate = -jnp.exp(head_ref[layer, 1:2, :])
        later = (src >= at).astype(F32)
        d_log = exact_dot(later, dcum[...])
        d_raw = (dstep[...] + rate * d_log) * sig_dt[layer]
        smalls[layer, 9:10, pl.ds(256, 128)] = jnp.sum(d_raw, axis=0, keepdims=True)
        smalls[layer, 9:10, pl.ds(384, 128)] = rate * jnp.sum(
            steps[layer] * d_log, axis=0, keepdims=True
        )
        dproj[:, pl.ds(ZX + PAIR, DT)] = d_raw.astype(BF16)
        d_scores = dscores[...].astype(BF16)
        b_mat = vals[layer, :, pl.ds(INNER_OWN, STATE)]
        c_mat = vals[layer, :, pl.ds(INNER_OWN + STATE, STATE)]
        dact[:, pl.ds(INNER_OWN, STATE)] = dot(d_scores, c_mat, TN)
        dact[:, pl.ds(INNER_OWN + STATE, STATE)] = dot(d_scores, b_mat)

    def backward_conv(layer):
        def one(signal_cols, cols):
            signal = proj[layer, :, signal_cols].astype(F32)
            pre, shifted = conv_pre(layer, signal, cols)
            sigmoid = jax.nn.sigmoid(pre)
            d_pre = dact[:, cols] * sigmoid * (1.0 + pre * (1.0 - sigmoid))
            d_signal = conv_ref[layer, 3:4, cols] * d_pre
            d_taps = [jnp.sum(d_pre * signal, axis=0, keepdims=True)]
            for back in range(1, 4):
                d_signal = d_signal + conv_ref[layer, 3 - back : 4 - back, cols] * pltpu.roll(
                    d_pre * twice(same[back - 1]), ROWS - back, 0
                )
                d_taps.append(jnp.sum(d_pre * shifted[back - 1], axis=0, keepdims=True))
            dproj[:, signal_cols] = d_signal.astype(BF16)
            return jnp.sum(d_pre, axis=0, keepdims=True), d_taps

        @pl.loop(0, 4)
        def _(step):
            cols = tile(step, 256)
            d_bias, d_taps = one(shift_cols(step), cols)
            smalls[layer, 3:4, cols] = d_bias
            for back in range(4):
                smalls[layer, 7 - back : 8 - back, cols] = d_taps[back]

        d_bias, d_taps = one(pl.ds(ZX, PAIR), pl.ds(INNER_OWN, PAIR))
        smalls[layer, 9:10, pl.ds(0, PAIR)] = d_bias
        for back in range(4):
            smalls[layer, 8:9, pl.ds((3 - back) * PAIR, PAIR)] = d_taps[back]

    def backward_in(layer, which, rows):
        @pl.loop(0, 4)
        def _(step):
            cols = tile(step, 256)
            part = dot(dproj[:, :INNER_OWN], g_w[layer][step].reshape(256, INNER_OWN), NT)
            part = part + dot(dproj[:, INNER_OWN:], x_w[layer][step].reshape(256, XS), NT)
            mixs[which, :, cols] = part.astype(BF16)
            mix_copy(which, step, rows).start()
            smalls[layer, 0:1, cols] = jnp.sum(
                part * hid[layer, :, cols] * twice(scales[layer]), axis=0, keepdims=True
            )

    def backward_wg(layer):
        @pl.loop(0, 4)
        def _(step):
            cols = tile(step, 256)
            store_cols(gate_grads[layer], cols, dot(norm_t[layer], dproj[:, cols]))

    def backward_wx(layer):
        @pl.loop(0, 5)
        def _(step):
            part = dot(norm_t[layer], dproj[:, shift_cols(step)])
            store_cols(signal_grads[layer], tile(step, 256), part)

        part = dot(norm_t[layer], dproj[:, pl.ds(ZX + PAIR, DT)])
        store_cols(signal_grads[layer], pl.ds(SIGNAL, DT), part)

    def next_grad(layer, which, rows):
        part = mixs[which, rows, :].astype(F32) + mixr[which, rows, :].astype(F32)
        part = part * vec_ref[layer, 0:1, :]
        before = hid[layer, rows, :]
        scale = scales[layer, rows, 0:1]
        inner = jnp.sum(part * before, axis=1, keepdims=True)
        return grad[rows, :] + scale * part - before * (scale * scale * scale * inner / WIDTH)

    class Smalls:
        def __init__(self, layer):
            self.layer = layer
            self.copies = []

        def start(self, first, count, mine, where, base):
            layer = self.layer
            slots[layer, first + mine] = smalls[layer]
            ref = slots.at[layer, first + mine]
            for step in range(1, count):
                self.copies.append(send(ref, ref, ssem.at[layer], base + step - 1, **where(step)))
            self.pending = self.copies[len(self.copies) - count + 1 :]

        def take(self, first, count):
            layer = self.layer
            for copy in self.pending:
                copy.wait_recv()
            total = slots[layer, first]
            for step in range(1, count):
                total = total + slots[layer, first + step]
            smalls[layer] = total

        def core(self):
            self.start(0, 2, c, lambda step: {"fsdp": index_of(y, z, x, 1 - c)}, 0)

        def along_x(self):
            self.take(0, 2)
            self.start(2, 4, x, lambda step: {"fsdp": index_of(y, z, (x + step) % 4, c)}, 1)

        def along_y(self):
            self.take(2, 4)
            self.start(6, 4, y, lambda step: {"fsdp": index_of((y + step) % 4, z, x, c)}, 4)

        def along_z(self):
            self.take(6, 4)
            self.start(10, 2, z, lambda step: {"fsdp": index_of(y, 1 - z, x, c)}, 7)

        def across(self):
            self.take(10, 2)
            self.start(12, 2, t, lambda step: {"tp": other}, 8)

        def finish(self):
            layer = self.layer
            mine = smalls[layer]
            self.take(12, 2)
            both = smalls[layer]
            row = lax.broadcasted_iota(jnp.int32, both.shape, 0)
            lane = lax.broadcasted_iota(jnp.int32, both.shape, 1)
            shared = (row == 0) | (row == 8) | ((row == 9) & (lane < PAIR))
            small_ref[layer] = jnp.where(shared, both, mine)
            for copy in self.copies:
                copy.wait_send()

    reduce_x0, reduce_g0, reduce_o0, reduce_x1, reduce_g1, reduce_o1 = [
        Reduce(ref, *buffers[7 * slot : 7 * slot + 7], rsem.at[slot], HALVES[slot % 3], PARTS[slot % 3])
        for slot, ref in enumerate(all_grads)
    ]
    smalls_1, smalls_0 = Smalls(1), Smalls(0)

    def send_pair(layer):
        bc_s[layer] = gx_ref[layer, :, pl.ds(INNER_OWN, PAIR)]
        return send(bc_s.at[layer], bc_r.at[layer], tsem, 6 + layer, tp=other)

    def take_pair(layer, copy):
        copy.wait_recv()
        gx_ref[layer, :, pl.ds(INNER_OWN, PAIR)] = bc_s[layer] + bc_r[layer]
        copy.wait_send()

    backward_gate(1)
    inner_1 = send_rows(2)
    backward_wo(1)
    reduce_o1.core()
    backward_ssd(1, inner_1, 2)
    reduce_o1.line()
    backward_conv(1)
    backward_in(1, 2, pl.ds(0, ROWS))
    backward_wg(1)
    reduce_g1.core()
    backward_wx(1)
    reduce_x1.core()
    reduce_o1.relay()
    reduce_g1.line()
    reduce_x1.line()
    wait_mix(2, pl.ds(0, ROWS))

    @pl.loop(0, 4)
    def _(step):
        rows = tile(step, 64)
        grad[rows, :] = next_grad(1, 2, rows)

    smalls_1.core()
    backward_gate(0)
    inner_0 = send_rows(3)
    reduce_g1.relay()
    backward_wo(0)
    reduce_o0.core()
    reduce_o1.plane()
    smalls_1.along_x()
    wait_mix(1, peer_rows)
    act_ref[...] = (hid[1, own_rows, :] + mixed_rows(1, own_rows)).astype(BF16)
    reduce_x1.relay()
    backward_ssd(0, inner_0, 3)
    reduce_o0.line()
    reduce_g1.plane()
    reduce_x1.plane()
    smalls_1.along_y()
    backward_wg(0)
    reduce_g0.core()
    backward_conv(0)
    backward_wx(0)
    reduce_x0.core()
    reduce_o0.relay()
    reduce_g0.line()
    backward_in(0, 3, peer_rows)
    smalls_0.core()
    reduce_x0.line()
    reduce_o1.finish(go_ref.at[1])
    reduce_g0.relay()
    smalls_1.along_z()
    smalls_0.along_x()
    reduce_o0.plane()
    reduce_g1.finish(gg_ref.at[1])
    reduce_x1.finish(gx_ref.at[1])
    pair_1 = send_pair(1)
    reduce_x0.relay()
    reduce_g0.plane()
    smalls_0.along_y()
    smalls_1.across()
    wait_mix(3, peer_rows)
    gin_ref[...] = next_grad(0, 3, own_rows)
    reduce_o0.finish(go_ref.at[0])
    reduce_x0.plane()
    smalls_0.along_z()
    take_pair(1, pair_1)
    smalls_1.finish()
    reduce_g0.finish(gg_ref.at[0])
    smalls_0.across()
    reduce_x0.finish(gx_ref.at[0])
    pair_0 = send_pair(0)
    smalls_0.finish()
    take_pair(0, pair_0)
    for copy in (send_x, send_cot, squares_0, squares_1, inner_1, inner_0):
        copy.wait_send()


def reduce_scratch(width, half):
    return [
        pltpu.VMEM((4, 2, 4, 16, width), BF16),
        pltpu.VMEM((2, 2, 4, 16, half), BF16),
        pltpu.VMEM((2, 4, 2, 16, width - half), BF16),
        pltpu.VMEM((7, 16, half), BF16),
        pltpu.VMEM((7, 16, width - half), BF16),
        pltpu.VMEM((2, 4, 16, half), BF16),
        pltpu.VMEM((2, 4, 16, width - half), BF16),
    ]


def whole_step(x_in, cotangent, own, lengths, vec, conv, head):
    scratch = [
        *[pltpu.VMEM((4, 2, 4, 2, 16, width), BF16) for width in PARTS + PARTS],
        pltpu.VMEM((2, ROWS, WIDTH), F32),
        pltpu.VMEM((2, WIDTH, ROWS), BF16),
        pltpu.VMEM((2, ROWS, ZX + PAIR), BF16),
        pltpu.VMEM((2, ROWS, SIGNAL), BF16),
        pltpu.VMEM((2, ROWS, INNER_OWN), F32),
        pltpu.VMEM((ROWS, INNER_OWN), BF16),
        pltpu.VMEM((2, ROWS, 128), F32),
        pltpu.VMEM((2, ROWS, 128), F32),
        pltpu.VMEM((2, 128, ROWS), F32),
        pltpu.VMEM((2, ROWS, 128), F32),
        pltpu.VMEM((2, ROWS, 128), F32),
        pltpu.VMEM((2, ROWS, 128), F32),
        pltpu.VMEM((ROWS, WIDTH), BF16),
        pltpu.VMEM((ROWS, WIDTH), BF16),
        pltpu.VMEM((ROWS, WIDTH), BF16),
        pltpu.VMEM((WIDTH, ROWS), BF16),
        pltpu.VMEM((ROWS, WIDTH), F32),
        pltpu.VMEM((ROWS, SIGNAL), F32),
        pltpu.VMEM((ROWS, INNER_OWN + XS), BF16),
        pltpu.VMEM((ROWS, ROWS), F32),
        pltpu.VMEM((ROWS, ROWS), F32),
        pltpu.VMEM((ROWS, ROWS), F32),
        pltpu.VMEM((3, ROWS, 128), F32),
        pltpu.VMEM((ROWS, 128), F32),
        pltpu.VMEM((ROWS, 128), F32),
        pltpu.VMEM((ROWS, 128), F32),
        pltpu.VMEM((ROWS, 128), F32),
        pltpu.VMEM((4, ROWS, WIDTH), BF16),
        pltpu.VMEM((4, ROWS, WIDTH), BF16),
        pltpu.VMEM((4, 8, ROWS), F32),
        pltpu.VMEM((4, 8, ROWS), F32),
        pltpu.VMEM((2, 16, 1024), F32),
        pltpu.VMEM((2, 14, 16, 1024), F32),
        pltpu.VMEM((2, 16, PAIR), F32),
        pltpu.VMEM((2, 16, PAIR), F32),
        *[
            buffer
            for width, half in zip(PARTS + PARTS, HALVES + HALVES)
            for buffer in reduce_scratch(width, half)
        ],
        pltpu.VMEM((4, 2, 4, 2, 16, INNER_OWN), BF16),
        pltpu.VMEM((4, 2, 4, 2, 16, XS), BF16),
        pltpu.SemaphoreType.DMA((6, 2, GATHER_COPIES)),
        pltpu.SemaphoreType.DMA((6, 2, REDUCE_COPIES)),
        pltpu.SemaphoreType.DMA((2, 24)),
        pltpu.SemaphoreType.DMA((2, 2, 9)),
        pltpu.SemaphoreType.DMA((6,)),
    ]
    vmem = pl.BlockSpec(memory_space=pltpu.VMEM)
    return pl.pallas_call(
        body,
        out_shape=(
            jax.ShapeDtypeStruct((128, WIDTH), BF16),
            jax.ShapeDtypeStruct((128, WIDTH), F32),
            jax.ShapeDtypeStruct((2, 16, XS), F32),
            jax.ShapeDtypeStruct((2, 16, INNER_OWN), F32),
            jax.ShapeDtypeStruct((2, 16, OUT), F32),
            jax.ShapeDtypeStruct((2, 16, 1024), F32),
        ),
        in_specs=[vmem, vmem, vmem, pl.BlockSpec(memory_space=pltpu.SMEM), vmem, vmem, vmem],
        out_specs=(vmem,) * 6,
        scratch_shapes=scratch,
        compiler_params=pltpu.CompilerParams(
            collective_id=0, has_side_effects=True, vmem_limit_bytes=60 << 20
        ),
        name="whole_step",
    )(x_in, cotangent, own, lengths, vec, conv, head)


def finish_kernel(
    act_ref, gin_ref, gx_ref, gg_ref, go_ref, small_ref,
    act_out, grad_in, gain_in, w_zx, w_bc, w_dt, conv_x, conv_bc,
    bias_x, bias_bc, dt_bias, a_log, skip, gain_gate, w_out,
):
    w_out[...] = go_ref[...]
    act_out[...] = act_ref[...]
    grad_in[...] = gin_ref[...]
    w_bc[...] = gx_ref[:, :, INNER_OWN:SIGNAL]
    w_dt[...] = gx_ref[:, :, SIGNAL : SIGNAL + HEADS_OWN]
    channel = lax.broadcasted_iota(jnp.int32, (INNER_OWN, 128), 0) // 64
    head = lax.broadcasted_iota(jnp.int32, (INNER_OWN, 128), 1)
    members = (channel == head).astype(F32)
    for layer in range(2):
        for row in range(16):
            w_zx[layer, row, 0:1, :] = gg_ref[layer, row : row + 1, :]
            w_zx[layer, row, 1:2, :] = gx_ref[layer, row : row + 1, :INNER_OWN]
        one = slice(layer, layer + 1)
        gain_in[one, :] = small_ref[layer, 0:1, :]
        gain_gate[one, :] = small_ref[layer, 1:2, :]
        by_head = exact_dot(small_ref[layer], members)
        skip[one, :] = by_head[2:3, :HEADS_OWN]
        bias_x[one, :] = small_ref[layer, 3:4, :]
        conv_x[layer] = small_ref[layer, 4:8, :]
        for tap in range(4):
            conv_bc[layer, tap : tap + 1, :] = small_ref[layer, 8:9, tap * PAIR : (tap + 1) * PAIR]
        bias_bc[one, :] = small_ref[layer, 9:10, :PAIR]
        dt_bias[one, :] = small_ref[layer, 9:10, 256 : 256 + HEADS_OWN]
        a_log[one, :] = small_ref[layer, 9:10, 384 : 384 + HEADS_OWN]


def finish_step(*parts):
    shapes = [
        ((128, WIDTH), BF16), ((128, WIDTH), F32), ((2, WIDTH), F32), ((2, 16, 2, INNER_OWN), F32),
        ((2, 16, PAIR), F32), ((2, 16, HEADS_OWN), F32), ((2, 4, INNER_OWN), F32), ((2, 4, PAIR), F32),
        ((2, INNER_OWN), F32), ((2, PAIR), F32), ((2, HEADS_OWN), F32), ((2, HEADS_OWN), F32),
        ((2, HEADS_OWN), F32), ((2, INNER_OWN), F32), ((2, 16, INNER_OWN), F32),
    ]
    vmem = pl.BlockSpec(memory_space=pltpu.VMEM)
    return pl.pallas_call(
        finish_kernel,
        out_shape=[jax.ShapeDtypeStruct(*shape) for shape in shapes],
        in_specs=[vmem] * 6,
        out_specs=[vmem] * 15,
        compiler_params=pltpu.CompilerParams(vmem_limit_bytes=60 << 20),
        name="finish_step",
    )(*parts)


def shards(
    x_in, cotangent, seq_lengths, gain_in, w_zx, w_bc, w_dt, conv_x, conv_bc,
    bias_x, bias_bc, dt_bias, a_log, skip, gain_gate, w_out,
):
    def wide(part, width):
        return jnp.pad(part, ((0, 0), (0, 0), (0, width - part.shape[-1])))

    own = jnp.concatenate(
        [w_zx[:, :, 1], w_bc, wide(w_dt, DT), w_zx[:, :, 0], jnp.swapaxes(w_out, 1, 2)], axis=2
    )
    vec = jnp.stack([gain_in, gain_gate, jnp.repeat(skip, 64, axis=1)], axis=1)
    vec = jnp.pad(vec, ((0, 0), (0, 5), (0, 0))).astype(F32)
    conv = jnp.concatenate(
        [
            jnp.concatenate([conv_x, conv_bc], axis=2),
            jnp.concatenate([bias_x, bias_bc], axis=1)[:, None, :],
        ],
        axis=1,
    )
    conv = jnp.pad(conv, ((0, 0), (0, 3), (0, 0))).astype(F32)
    head = wide(jnp.stack([dt_bias, a_log], axis=1), 128)
    head = jnp.pad(head, ((0, 0), (0, 6), (0, 0))).astype(F32)
    parts = whole_step(x_in, cotangent, own, seq_lengths, vec, conv, head)
    done = finish_step(*parts)
    return (*done[:-1], jnp.swapaxes(done[-1], 1, 2))


def solution(mesh):
    placed = (
        P(("fsdp", "tp"), None),
        P(("fsdp", "tp"), None),
        P("fsdp", None),
        P(),
        P(None, "fsdp", None, "tp"),
        P(None, "fsdp", None),
        P(None, "fsdp", "tp"),
        P(None, None, "tp"),
        P(),
        P(None, "tp"),
        P(),
        P(None, "tp"),
        P(None, "tp"),
        P(None, "tp"),
        P(None, "tp"),
        P(None, "tp", "fsdp"),
    )
    return jax.shard_map(
        shards,
        mesh=mesh,
        in_specs=placed,
        out_specs=(
            P(("fsdp", "tp"), None),
            P(("fsdp", "tp"), None),
            P(),
            P(None, "fsdp", None, "tp"),
            P(None, "fsdp", None),
            P(None, "fsdp", "tp"),
            P(None, None, "tp"),
            P(),
            P(None, "tp"),
            P(),
            P(None, "tp"),
            P(None, "tp"),
            P(None, "tp"),
            P(None, "tp"),
            P(None, "tp", "fsdp"),
        ),
        check_vma=False,
    )
```

```python
import jax
import jax.numpy as jnp
from jax import lax
from jax.experimental import pallas as pl
from jax.experimental.pallas import tpu as pltpu
from jax.sharding import PartitionSpec as P

MESH = pl.DeviceIdType.MESH
INNER = 2048
EPS = 1e-05


def place():
    index = lax.axis_index("fsdp")
    return index // 16, (index // 8) % 2, (index // 2) % 4, index % 2


def index_of(y, z, x, c):
    return ((y * 2 + z) * 4 + x) * 2 + c


PLANE_ZX = [(dz, dx) for dz in range(2) for dx in range(4) if (dz, dx) != (0, 0)]
PLANE_YZ = [(dy, dz) for dy in range(4) for dz in range(2) if (dy, dz) != (0, 0)]


def peers_of():
    y, z, x, c = place()
    found = [index_of(y, (z + dz) % 2, (x + dx) % 4, c) for dz, dx in PLANE_ZX]
    found += [index_of((y + dy) % 4, (z + dz) % 2, x, c) for dy, dz in PLANE_YZ if dy != 0]
    found.append(index_of(y, z, x, 1 - c))
    return found


def greet_all(with_tp):
    barrier = pltpu.get_barrier_semaphore()
    peers = peers_of()
    for peer in peers:
        pl.semaphore_signal(barrier, inc=1, device_id={"fsdp": peer}, device_id_type=MESH)
    count = len(peers)
    if with_tp:
        other = 1 - lax.axis_index("tp")
        pl.semaphore_signal(barrier, inc=1, device_id={"tp": other}, device_id_type=MESH)
        count += 1
    pl.semaphore_wait(barrier, count)


def send(src, dst, sems, slot, **where):
    copy = pltpu.make_async_remote_copy(
        src_ref=src,
        dst_ref=dst,
        send_sem=sems.at[0, slot],
        recv_sem=sems.at[1, slot],
        device_id=where,
        device_id_type=MESH,
    )
    copy.start()
    return copy


GATHER_COPIES = 30


class Gather:
    def __init__(self, whole, sems, first, half, end):
        self.whole, self.sems = whole, sems
        self.cols = (pl.ds(first, half - first), pl.ds(half, end - half))
        self.started = []

    def pair(self):
        y, z, x, c = place()
        ref = self.whole.at[y, z, x, c]
        self.pairs = [send(ref, ref, self.sems, 0, fsdp=index_of(y, 1 - z, x, c))]

    def spread(self):
        y, z, x, c = place()
        cols_a, cols_b = self.cols
        self.pairs[0].wait_recv()
        self.first = []
        for step in range(1, 4):
            ref = self.whole.at[y, :, x, c, :, cols_a]
            self.first.append(
                send(ref, ref, self.sems, step, fsdp=index_of(y, z, (x + step) % 4, c))
            )
            ref = self.whole.at[y, :, x, c, :, cols_b]
            self.first.append(
                send(ref, ref, self.sems, 3 + step, fsdp=index_of((y + step) % 4, z, x, c))
            )

    def plane(self):
        y, z, x, c = place()
        cols_a, cols_b = self.cols
        self.pairs, self.first = [], []
        for slot, (dz, dx) in enumerate(PLANE_ZX):
            ref = self.whole.at[y, z, x, c, :, cols_a]
            self.first.append(
                send(ref, ref, self.sems, slot, fsdp=index_of(y, (z + dz) % 2, (x + dx) % 4, c))
            )
        for slot, (dy, dz) in enumerate(PLANE_YZ):
            ref = self.whole.at[y, z, x, c, :, cols_b]
            self.first.append(
                send(ref, ref, self.sems, 7 + slot, fsdp=index_of((y + dy) % 4, (z + dz) % 2, x, c))
            )

    def line(self):
        y, z, x, c = place()
        cols_a, cols_b = self.cols
        for copy in self.first:
            copy.wait_recv()
        self.second = []
        for slot, step in enumerate((1, 3)):
            ref = self.whole.at[y, :, :, c, :, cols_a]
            self.second.append(
                send(ref, ref, self.sems, 14 + slot, fsdp=index_of((y + step) % 4, z, x, c))
            )
            ref = self.whole.at[:, :, x, c, :, cols_b]
            self.second.append(
                send(ref, ref, self.sems, 16 + slot, fsdp=index_of(y, z, (x + step) % 4, c))
            )
        self.third = []
        self.hand_over(0)

    def hand_over(self, step):
        y, z, x, c = place()
        cols_a, cols_b = self.cols
        ref = self.whole.at[(y - step + 4) % 4, :, :, c, :, cols_a]
        self.third.append(send(ref, ref, self.sems, 22 + step, fsdp=index_of(y, z, x, 1 - c)))
        ref = self.whole.at[:, :, (x - step + 4) % 4, c, :, cols_b]
        self.third.append(send(ref, ref, self.sems, 26 + step, fsdp=index_of(y, z, x, 1 - c)))

    def relay(self):
        y, z, x, c = place()
        cols_a, cols_b = self.cols
        self.fourth = []
        for slot, step in enumerate((1, 3)):
            self.second[2 * slot].wait_recv()
            ref = self.whole.at[(y - step + 4) % 4, slot, :, c, :, cols_a]
            self.fourth.append(
                send(ref, ref, self.sems, 18 + slot, fsdp=index_of((y + step) % 4, z, x, c))
            )
            self.second[2 * slot + 1].wait_recv()
            ref = self.whole.at[:, slot, (x - step + 4) % 4, c, :, cols_b]
            self.fourth.append(
                send(ref, ref, self.sems, 20 + slot, fsdp=index_of(y, z, (x + step) % 4, c))
            )
        self.hand_over(1)
        self.hand_over(3)

    def core(self):
        for copy in self.fourth:
            copy.wait_recv()
        self.hand_over(2)

    def finish(self):
        for copy in self.third:
            copy.wait_recv()
        for copy in self.pairs + self.first + self.second + self.third + self.fourth:
            copy.wait_send()


REDUCE_COPIES = 27


class Reduce:
    def __init__(
        self, grad, from_core, from_line_a, from_line_b, from_plane_a, from_plane_b, relay_a, relay_b, sems, half, end
    ):
        self.grad, self.from_core, self.sems = grad, from_core, sems
        self.line_a, self.line_b = from_line_a, from_line_b
        self.plane_a, self.plane_b = from_plane_a, from_plane_b
        self.relay_a, self.relay_b = relay_a, relay_b
        self.cols = (pl.ds(0, half), pl.ds(half, end - half))

    def core(self):
        y, z, x, c = place()
        self.copies = [
            send(
                self.grad.at[:, :, :, 1 - c],
                self.from_core,
                self.sems,
                0,
                fsdp=index_of(y, z, x, 1 - c),
            )
        ]

    def line(self):
        y, z, x, c = place()
        cols_a, cols_b = self.cols
        self.copies[0].wait_recv()

        @pl.loop(0, 32)
        def _(block):
            iy, iz, ix = block // 8, (block // 4) % 2, block % 4
            mine = self.grad[iy, iz, ix, c].astype(jnp.float32)
            theirs = self.from_core[iy, iz, ix].astype(jnp.float32)
            self.from_core[iy, iz, ix] = (mine + theirs).astype(jnp.bfloat16)

        self.relays, self.second = [], []
        for slot, step in enumerate((1, 3)):
            to, far = (y + step) % 4, (y + 2) % 4
            where = index_of(to, z, x, c)
            self.relays.append(
                send(self.from_core.at[far, slot, :, :, cols_a], self.relay_a.at[slot], self.sems, 1 + slot, fsdp=where)
            )
            self.second.append(
                send(
                    self.from_core.at[to, 1 - slot, :, :, cols_a],
                    self.line_a.at[slot, 1 - slot],
                    self.sems,
                    3 + slot,
                    fsdp=where,
                )
            )
            to, far = (x + step) % 4, (x + 2) % 4
            where = index_of(y, z, to, c)
            self.relays.append(
                send(self.from_core.at[:, slot, far, :, cols_b], self.relay_b.at[slot], self.sems, 5 + slot, fsdp=where)
            )
            self.second.append(
                send(
                    self.from_core.at[:, 1 - slot, to, :, cols_b],
                    self.line_b.at[slot, :, 1 - slot],
                    self.sems,
                    7 + slot,
                    fsdp=where,
                )
            )

    def relay(self):
        y, z, x, c = place()
        cols_a, cols_b = self.cols
        for copy in self.relays:
            copy.wait_recv()
        for slot, step in enumerate((1, 3)):
            to_y, to_x = (y + step) % 4, (x + step) % 4

            @pl.loop(0, 4)
            def _(block):
                mine = self.from_core[to_y, slot, block, :, cols_a].astype(jnp.float32)
                mine = mine + self.relay_a[slot, block].astype(jnp.float32)
                self.from_core[to_y, slot, block, :, cols_a] = mine.astype(jnp.bfloat16)
                mine = self.from_core[block, slot, to_x, :, cols_b].astype(jnp.float32)
                mine = mine + self.relay_b[slot, block].astype(jnp.float32)
                self.from_core[block, slot, to_x, :, cols_b] = mine.astype(jnp.bfloat16)

            self.second.append(
                send(
                    self.from_core.at[to_y, slot, :, :, cols_a],
                    self.line_a.at[slot, slot],
                    self.sems,
                    9 + slot,
                    fsdp=index_of(to_y, z, x, c),
                )
            )
            self.second.append(
                send(
                    self.from_core.at[:, slot, to_x, :, cols_b],
                    self.line_b.at[slot, :, slot],
                    self.sems,
                    11 + slot,
                    fsdp=index_of(y, z, to_x, c),
                )
            )

    def plane(self):
        y, z, x, c = place()
        cols_a, cols_b = self.cols
        for copy in self.second:
            copy.wait_recv()

        @pl.loop(0, 8)
        def _(block):
            iz, ix = block // 4, block % 4
            total = self.from_core[y, iz, ix, :, cols_a].astype(jnp.float32)
            for step in range(2):
                total = total + self.line_a[step, iz, ix].astype(jnp.float32)
            self.line_a[0, iz, ix] = total.astype(jnp.bfloat16)
            iy, iz = block // 2, block % 2
            total = self.from_core[iy, iz, x, :, cols_b].astype(jnp.float32)
            for step in range(2):
                total = total + self.line_b[step, iy, iz].astype(jnp.float32)
            self.line_b[0, iy, iz] = total.astype(jnp.bfloat16)

        self.third = []
        for slot, (dz, dx) in enumerate(PLANE_ZX):
            tz, tx = (z + dz) % 2, (x + dx) % 4
            self.third.append(
                send(
                    self.line_a.at[0, tz, tx],
                    self.plane_a.at[slot],
                    self.sems,
                    13 + slot,
                    fsdp=index_of(y, tz, tx, c),
                )
            )
        for slot, (dy, dz) in enumerate(PLANE_YZ):
            ty, tz = (y + dy) % 4, (z + dz) % 2
            self.third.append(
                send(
                    self.line_b.at[0, ty, tz],
                    self.plane_b.at[slot],
                    self.sems,
                    20 + slot,
                    fsdp=index_of(ty, tz, x, c),
                )
            )

    def finish(self, out):
        y, z, x, c = place()
        cols_a, cols_b = self.cols
        for copy in self.third:
            copy.wait_recv()
        total = self.line_a[0, z, x].astype(jnp.float32)
        for slot in range(7):
            total = total + self.plane_a[slot].astype(jnp.float32)
        out[:, cols_a] = total
        total = self.line_b[0, y, z].astype(jnp.float32)
        for slot in range(7):
            total = total + self.plane_b[slot].astype(jnp.float32)
        out[:, cols_b] = total
        for copy in self.copies + self.relays + self.second + self.third:
            copy.wait_send()


ROWS, WIDTH, INNER_OWN, STATE, HEADS_OWN = 256, 1024, 1024, 128, 16
ZX, PAIR, DT, OUT = 2048, 256, 128, 1024
SIGNAL = INNER_OWN + PAIR
XS = SIGNAL + DT
PARTS = (XS, INNER_OWN, OUT)
HALVES = (768, 512, 512)
F32, BF16 = jnp.float32, jnp.bfloat16
NN = (((1,), (0,)), ((), ()))
NT = (((1,), (1,)), ((), ()))
TN = (((0,), (0,)), ((), ()))


def dot(a, b, dims=NN):
    return lax.dot_general(a, b, dims, preferred_element_type=F32)


def exact_dot(a, b, dims=NN):
    return lax.dot_general(
        a, b, dims, preferred_element_type=F32, precision=lax.Precision.HIGHEST
    )


def tile(index, width):
    return pl.ds(pl.multiple_of(index * width, width), width)


def twice(part):
    return jnp.concatenate([part, part], axis=1)


def three_parts(value):
    high = value.astype(BF16)
    rest = value - high.astype(F32)
    middle = rest.astype(BF16)
    return high, middle, (rest - middle.astype(F32)).astype(BF16)


def parts_by_lane(value):
    lane = lax.broadcasted_iota(jnp.int32, value.shape, 1)
    terms = [part.astype(F32) for part in three_parts(jnp.where(lane < 16, value, 0.0))]
    return (terms[0] + pltpu.roll(terms[1], 16, 1) + pltpu.roll(terms[2], 32, 1)).astype(BF16)


def picked(parts, heads):
    row = lax.broadcasted_iota(jnp.int32, heads.shape, 0)
    return dot(parts, jnp.where(((row & 15) == heads) & (row < 48), 1.0, 0.0).astype(BF16))


def body(
    x_ref, cot_ref, own_ref, lens_ref, vec_ref, conv_ref, head_ref,
    act_ref, gin_ref, gx_ref, gg_ref, go_ref, small_ref,
    wx0, wg0, wo0, wx1, wg1, wo1,
    hid, norm_t, proj, vals, ssd, ngate, steps, step_parts, cum_parts, cums_t, scales, gscales, sig_dt,
    xs, cots, normed, cot_t, grad, dact, dproj, scores, dscores, mask, same, live, acc, dcum, dstep,
    mixs, mixr, row_s, row_r, smalls, slots, bc_s, bc_r,
    *rest,
):
    buffers, (gg0, gx0, gsem, rsem, tsem, ssem, lsem) = rest[:42], rest[42:]
    y, z, x, c = place()
    t = lax.axis_index("tp")
    other = 1 - t
    own_rows = pl.ds(pl.multiple_of(t * 128, 128), 128)
    peer_rows = pl.ds(pl.multiple_of(other * 128, 128), 128)

    def load_cols(ref, cols):
        part = ref[:, :, :, :, :, cols]
        return part.reshape(WIDTH, part.shape[-1])

    def store_cols(ref, cols, part):
        ref[:, :, :, :, :, cols] = part.astype(BF16).reshape(4, 2, 4, 2, 16, part.shape[-1])

    x_w, g_w, o_w = (wx0, wx1), (wg0, wg1), (wo0, wo1)
    whole = (wx0, wg0, wo0, wx1, wg1, wo1)
    gate_grads, signal_grads = (gg0, wg1), (gx0, wx1)
    all_grads = (gx0, gg0, wo0, wx1, wg1, wo1)

    keeps = []
    for slot, ref in enumerate(whole):
        first = sum(PARTS[: slot % 3])
        keeps.append(
            pltpu.make_async_copy(
                own_ref.at[slot // 3, :, pl.ds(first, PARTS[slot % 3])],
                ref.at[y, z, x, c],
                lsem.at[slot],
            )
        )
        keeps[-1].start()
    greet_all(True)
    gather_x0, gather_g0, gather_o0, gather_x1, gather_g1, gather_o1 = [
        Gather(ref, gsem.at[slot], 0, HALVES[slot % 3], PARTS[slot % 3])
        for slot, ref in enumerate(whole)
    ]
    keeps[0].wait()
    gather_x0.plane()
    for keep in keeps[1:]:
        keep.wait()
    gather_g0.pair()
    gather_o0.pair()
    xs[own_rows, :] = x_ref[...]
    cots[own_rows, :] = cot_ref[...]

    bounds = [lens_ref[0, 0]]
    for j in range(1, 4):
        bounds.append(bounds[-1] + lens_ref[0, j])

    def ids_at(pos):
        total = jnp.zeros(pos.shape, jnp.int32)
        for bound in bounds:
            total = total + (pos >= bound).astype(jnp.int32)
        return total

    pos = lax.broadcasted_iota(jnp.int32, (ROWS, 128), 0)
    ids = ids_at(pos)
    live[...] = (ids < 4).astype(F32)
    for back in range(1, 4):
        same[back - 1] = ((ids == ids_at(pos - back)) & (pos >= back)).astype(F32)
    at = lax.broadcasted_iota(jnp.int32, (ROWS, ROWS), 0)
    src = lax.broadcasted_iota(jnp.int32, (ROWS, ROWS), 1)
    mask[...] = jnp.where((ids_at(at) == ids_at(src)) & (src <= at), 0.0, -1e30)
    smalls[...] = jnp.zeros_like(smalls)

    def spread_rows(part):
        return jnp.broadcast_to(part[0:1, :], (128, ROWS)).T

    def send_rows(which):
        total = jnp.sum(acc[...], axis=1, keepdims=True)
        row_s[which] = jnp.broadcast_to(total, (ROWS, 128)).T[:8, :]
        return send(row_s.at[which], row_r.at[which], tsem, 2 + which, tp=other)

    def norm_layer(layer):
        @pl.loop(0, 4)
        def _(step):
            rows = tile(step, 64)
            part = hid[layer, rows, :]
            scale = lax.rsqrt(jnp.mean(part * part, axis=1, keepdims=True) + EPS)
            scales[layer, rows, :] = jnp.broadcast_to(scale, (64, 128))
            normed[rows, :] = (part * scale * vec_ref[layer, 0:1, :]).astype(BF16)

    def transposed(from_ref, to_ref):
        @pl.loop(0, 8)
        def _(step):
            cols = tile(step, 128)
            to_ref[cols, :] = from_ref[:, cols].astype(F32).T.astype(BF16)

    def conv_pre(layer, signal, cols):
        pre = conv_ref[layer, 4:5, cols] + conv_ref[layer, 3:4, cols] * signal
        shifted = []
        for back in range(1, 4):
            earlier = pltpu.roll(signal, back, 0) * twice(same[back - 1])
            shifted.append(earlier)
            pre = pre + conv_ref[layer, 3 - back : 4 - back, cols] * earlier
        return pre, shifted

    def shift_cols(step):
        return pl.ds(pl.multiple_of(INNER_OWN + step * 256, 256), 256)

    def project_gate(layer):
        @pl.loop(0, 4)
        def _(step):
            cols = tile(step, 256)
            proj[layer, :, cols] = dot(normed[...], load_cols(g_w[layer], cols)).astype(BF16)

    def project_signal(layer):
        @pl.loop(0, 5)
        def _(step):
            part = dot(normed[...], load_cols(x_w[layer], tile(step, 256)))
            proj[layer, :, shift_cols(step)] = part.astype(BF16)

    def forward_steps(layer):
        raw = dot(normed[...], load_cols(x_w[layer], pl.ds(SIGNAL, DT)))
        raw = raw.astype(BF16).astype(F32) + head_ref[layer, 0:1, :]
        sig_dt[layer] = jax.nn.sigmoid(raw)
        step_sizes = jnp.maximum(raw, 0.0) + jnp.log1p(jnp.exp(-jnp.abs(raw)))
        steps[layer] = step_sizes
        rate = -jnp.exp(head_ref[layer, 1:2, :])
        lower = (src <= at).astype(F32)
        summed = exact_dot(lower, step_sizes * rate)
        cum_parts[layer] = parts_by_lane(summed)
        step_parts[layer] = parts_by_lane(step_sizes)
        cums_t[layer] = summed.T

    def forward_conv(layer):
        @pl.loop(0, 5)
        def _(step):
            signal = proj[layer, :, shift_cols(step)].astype(F32)
            pre, unused = conv_pre(layer, signal, tile(step, 256))
            vals[layer, :, tile(step, 256)] = (pre * jax.nn.sigmoid(pre)).astype(BF16)

    def set_scores(layer):
        b_mat = vals[layer, :, pl.ds(INNER_OWN, STATE)]
        c_mat = vals[layer, :, pl.ds(INNER_OWN + STATE, STATE)]
        scores[...] = dot(c_mat, b_mat, NT)

    def decays(layer, head):
        heads = jnp.full((128, ROWS), head, jnp.int32)
        return jnp.exp(
            picked(cum_parts[layer], heads) - cums_t[layer, pl.ds(head, 1), :] + mask[...]
        )

    def pair_heads(step):
        return 2 * step + lax.broadcasted_iota(jnp.int32, (128, 128), 1) // 64

    def forward_ssd(layer):
        set_scores(layer)

        @pl.loop(0, 8)
        def _(step):
            cols = tile(step, 128)
            values = vals[layer, :, cols].astype(F32)
            upper = lax.broadcasted_iota(jnp.int32, (ROWS, 128), 1) >= 64
            total = vec_ref[layer, 2:3, cols] * values
            scaled = values * picked(step_parts[layer], pair_heads(step))
            for half in range(2):
                weights = (scores[...] * decays(layer, 2 * step + half)).astype(BF16)
                mine = jnp.where(upper == (half == 1), scaled, 0.0).astype(BF16)
                total = total + dot(weights, mine)
            ssd[layer, :, cols] = total

    def forward_gate(layer):
        acc[...] = jnp.zeros_like(acc)

        @pl.loop(0, 8)
        def _(step):
            cols = tile(step, 128)
            gate = proj[layer, :, cols].astype(F32)
            gated = ssd[layer, :, cols] * gate * jax.nn.sigmoid(gate)
            acc[...] += gated * gated
            ngate[:, cols] = (gated * vec_ref[layer, 1:2, cols]).astype(BF16)

    def mix_copy(which, step, rows):
        ref_s = mixs.at[which, rows, tile(step, 256)]
        ref_r = mixr.at[which, rows, tile(step, 256)]
        return pltpu.make_async_remote_copy(
            src_ref=ref_s,
            dst_ref=ref_r,
            send_sem=tsem.at[0, 8 + 4 * which + step],
            recv_sem=tsem.at[1, 8 + 4 * which + step],
            device_id={"tp": other},
            device_id_type=MESH,
        )

    def wait_mix(which, rows):
        @pl.loop(0, 4)
        def _(step):
            copy = mix_copy(which, step, rows)
            copy.wait_recv()
            copy.wait_send()

    def forward_out(layer, rows):
        @pl.loop(0, 4)
        def _(step):
            weight = o_w[layer][step].reshape(256, OUT)
            mixs[layer, :, tile(step, 256)] = dot(ngate[...], weight, NT).astype(BF16)
            mix_copy(layer, step, rows).start()

    def take_gate_scale(layer, copy):
        copy.wait_recv()
        total = row_s[layer] + row_r[layer]
        gscales[layer] = spread_rows(lax.rsqrt(total / INNER + EPS))

    def mixed_rows(layer, rows):
        part = mixs[layer, rows, :].astype(F32) + mixr[layer, rows, :].astype(F32)
        return part * (gscales[layer, rows, 0:1] * live[rows, 0:1])

    gather_x0.line()
    gather_g0.spread()
    gather_o0.spread()
    send_x = send(x_ref, xs.at[own_rows], tsem, 0, tp=other)
    gather_x0.relay()
    gather_g0.line()
    gather_x0.core()
    gather_o0.line()
    for job in (gather_x1, gather_g1, gather_o1):
        job.pair()
    send_x.wait_recv()

    @pl.loop(0, 4)
    def _(step):
        rows = tile(step, 64)
        hid[0, rows, :] = xs[rows, :].astype(F32)

    norm_layer(0)
    gather_x0.finish()
    gather_g0.relay()
    for job in (gather_x1, gather_g1, gather_o1):
        job.spread()
    project_signal(0)
    gather_g0.core()
    gather_o0.relay()
    forward_steps(0)
    forward_conv(0)
    gather_x1.line()
    gather_o0.core()
    forward_ssd(0)
    gather_g0.finish()
    project_gate(0)
    forward_gate(0)
    squares_0 = send_rows(0)
    gather_x1.relay()
    gather_g1.line()
    gather_o0.finish()
    forward_out(0, pl.ds(0, ROWS))
    transposed(normed, norm_t.at[0])
    gather_x1.core()
    gather_g1.relay()
    gather_o1.line()
    take_gate_scale(0, squares_0)
    gather_x1.finish()
    wait_mix(0, pl.ds(0, ROWS))
    send_cot = send(cot_ref, cots.at[own_rows], tsem, 1, tp=other)

    @pl.loop(0, 4)
    def _(step):
        rows = tile(step, 64)
        hid[1, rows, :] = hid[0, rows, :] + mixed_rows(0, rows)

    norm_layer(1)
    project_signal(1)
    gather_g1.core()
    forward_steps(1)
    gather_o1.relay()
    forward_conv(1)
    transposed(normed, norm_t.at[1])
    forward_ssd(1)
    gather_o1.core()
    gather_g1.finish()
    project_gate(1)
    forward_gate(1)
    squares_1 = send_rows(1)
    gather_o1.finish()
    forward_out(1, peer_rows)
    send_cot.wait_recv()

    @pl.loop(0, 4)
    def _(step):
        rows = tile(step, 64)
        grad[rows, :] = cots[rows, :].astype(F32)

    take_gate_scale(1, squares_1)

    def backward_gate(layer):
        @pl.loop(0, 4)
        def _(step):
            rows = tile(step, 64)
            normed[rows, :] = (live[rows, 0:1] * grad[rows, :]).astype(BF16)

        acc[...] = jnp.zeros_like(acc)

        @pl.loop(0, 4)
        def _(step):
            cols = tile(step, 256)
            d_normed_gate = dot(normed[...], load_cols(o_w[layer], cols))
            gate = proj[layer, :, cols].astype(F32)
            gated = ssd[layer, :, cols] * gate * jax.nn.sigmoid(gate)
            normal = gated * twice(gscales[layer])
            gain = vec_ref[layer, 1:2, cols]
            ngate[:, cols] = (normal * gain).astype(BF16)
            smalls[layer, 1:2, cols] = jnp.sum(d_normed_gate * normal, axis=0, keepdims=True)
            weighted = d_normed_gate * gain
            dact[:, cols] = weighted
            inner = weighted * gated
            acc[...] += inner[:, :128] + inner[:, 128:]

    def backward_wo(layer):
        transposed(normed, cot_t)

        @pl.loop(0, 4)
        def _(step):
            part = dot(cot_t[tile(step, 256), :], ngate[...]).astype(BF16)
            o_w[layer][step] = part.reshape(2, 4, 2, 16, OUT)

    def backward_ssd(layer, copy, which, between):
        copy.wait_recv()
        inner = spread_rows(row_s[which] + row_r[which])
        gs = gscales[layer]
        acc[...] = gs * gs * gs * inner / INNER
        set_scores(layer)
        dscores[...] = jnp.zeros_like(dscores)
        dcum[...] = jnp.zeros_like(dcum)
        dstep[...] = jnp.zeros_like(dstep)

        def one(step):
            cols = tile(step, 128)
            upper = lax.broadcasted_iota(jnp.int32, (ROWS, 128), 1) >= 64
            gate = proj[layer, :, cols].astype(F32)
            out = ssd[layer, :, cols]
            sigmoid = jax.nn.sigmoid(gate)
            silu = gate * sigmoid
            d_gated = gscales[layer] * dact[:, cols] - out * silu * acc[...]
            d_out = d_gated * silu
            dproj[:, cols] = (d_gated * out * sigmoid * (1.0 + gate * (1.0 - sigmoid))).astype(BF16)
            values = vals[layer, :, cols].astype(F32)
            size = picked(step_parts[layer], pair_heads(step))
            scaled = (values * size).astype(BF16)
            back = jnp.zeros((ROWS, 128), F32)
            for half in range(2):
                head = 2 * step + half
                decay = decays(layer, head)
                weights = (scores[...] * decay).astype(BF16)
                d_half = jnp.where(upper == (half == 1), d_out, 0.0).astype(BF16)
                dscores[...] += dot(d_half, scaled, NT) * decay
                back = back + dot(weights, d_half, TN)
            skip = vec_ref[layer, 2:3, cols]
            dact[:, cols] = skip * d_out + size * back
            smalls[layer, 2:3, cols] = jnp.sum(d_out * values, axis=0, keepdims=True)
            inside = out - skip * values
            turn = d_out.astype(BF16).astype(F32) * inside - scaled.astype(F32) * back
            size_turn = values * back
            lane = lax.broadcasted_iota(jnp.int32, (128, 128), 0)
            to = lax.broadcasted_iota(jnp.int32, (128, 128), 1)
            members = jnp.where(to == 2 * step + lane // 64, 1.0, 0.0).astype(BF16)
            for part in three_parts(turn):
                dcum[...] += dot(part, members)
            for part in three_parts(size_turn)[:2]:
                dstep[...] += dot(part, members)

        pl.loop(0, 4)(one)
        between()
        pl.loop(4, 8)(one)
        rate = -jnp.exp(head_ref[layer, 1:2, :])
        later = (src >= at).astype(F32)
        d_log = exact_dot(later, dcum[...])
        d_raw = (dstep[...] + rate * d_log) * sig_dt[layer]
        smalls[layer, 9:10, pl.ds(256, 128)] = jnp.sum(d_raw, axis=0, keepdims=True)
        smalls[layer, 9:10, pl.ds(384, 128)] = rate * jnp.sum(
            steps[layer] * d_log, axis=0, keepdims=True
        )
        dproj[:, pl.ds(ZX + PAIR, DT)] = d_raw.astype(BF16)
        d_scores = dscores[...].astype(BF16)
        b_mat = vals[layer, :, pl.ds(INNER_OWN, STATE)]
        c_mat = vals[layer, :, pl.ds(INNER_OWN + STATE, STATE)]
        dact[:, pl.ds(INNER_OWN, STATE)] = dot(d_scores, c_mat, TN)
        dact[:, pl.ds(INNER_OWN + STATE, STATE)] = dot(d_scores, b_mat)

    def backward_conv(layer):
        def one(signal_cols, cols):
            signal = proj[layer, :, signal_cols].astype(F32)
            pre, shifted = conv_pre(layer, signal, cols)
            sigmoid = jax.nn.sigmoid(pre)
            d_pre = dact[:, cols] * sigmoid * (1.0 + pre * (1.0 - sigmoid))
            d_signal = conv_ref[layer, 3:4, cols] * d_pre
            d_taps = [jnp.sum(d_pre * signal, axis=0, keepdims=True)]
            for back in range(1, 4):
                d_signal = d_signal + conv_ref[layer, 3 - back : 4 - back, cols] * pltpu.roll(
                    d_pre * twice(same[back - 1]), ROWS - back, 0
                )
                d_taps.append(jnp.sum(d_pre * shifted[back - 1], axis=0, keepdims=True))
            dproj[:, signal_cols] = d_signal.astype(BF16)
            return jnp.sum(d_pre, axis=0, keepdims=True), d_taps

        @pl.loop(0, 4)
        def _(step):
            cols = tile(step, 256)
            d_bias, d_taps = one(shift_cols(step), cols)
            smalls[layer, 3:4, cols] = d_bias
            for back in range(4):
                smalls[layer, 7 - back : 8 - back, cols] = d_taps[back]

        d_bias, d_taps = one(pl.ds(ZX, PAIR), pl.ds(INNER_OWN, PAIR))
        smalls[layer, 9:10, pl.ds(0, PAIR)] = d_bias
        for back in range(4):
            smalls[layer, 8:9, pl.ds((3 - back) * PAIR, PAIR)] = d_taps[back]

    def backward_in(layer, which, rows):
        @pl.loop(0, 4)
        def _(step):
            cols = tile(step, 256)
            part = dot(dproj[:, :INNER_OWN], g_w[layer][step].reshape(256, INNER_OWN), NT)
            part = part + dot(dproj[:, INNER_OWN:], x_w[layer][step].reshape(256, XS), NT)
            mixs[which, :, cols] = part.astype(BF16)
            mix_copy(which, step, rows).start()
            smalls[layer, 0:1, cols] = jnp.sum(
                part * hid[layer, :, cols] * twice(scales[layer]), axis=0, keepdims=True
            )

    def backward_wg(layer):
        @pl.loop(0, 4)
        def _(step):
            cols = tile(step, 256)
            store_cols(gate_grads[layer], cols, dot(norm_t[layer], dproj[:, cols]))

    def backward_wx(layer):
        @pl.loop(0, 5)
        def _(step):
            part = dot(norm_t[layer], dproj[:, shift_cols(step)])
            store_cols(signal_grads[layer], tile(step, 256), part)

        part = dot(norm_t[layer], dproj[:, pl.ds(ZX + PAIR, DT)])
        store_cols(signal_grads[layer], pl.ds(SIGNAL, DT), part)

    def next_grad(layer, which, rows):
        part = mixs[which, rows, :].astype(F32) + mixr[which, rows, :].astype(F32)
        part = part * vec_ref[layer, 0:1, :]
        before = hid[layer, rows, :]
        scale = scales[layer, rows, 0:1]
        inner = jnp.sum(part * before, axis=1, keepdims=True)
        return grad[rows, :] + scale * part - before * (scale * scale * scale * inner / WIDTH)

    class Smalls:
        def __init__(self, layer):
            self.layer = layer
            self.copies = []

        def start(self, first, count, mine, where, base):
            layer = self.layer
            slots[layer, first + mine] = smalls[layer]
            ref = slots.at[layer, first + mine]
            for step in range(1, count):
                self.copies.append(send(ref, ref, ssem.at[layer], base + step - 1, **where(step)))
            self.pending = self.copies[len(self.copies) - count + 1 :]

        def take(self, first, count):
            layer = self.layer
            for copy in self.pending:
                copy.wait_recv()
            total = slots[layer, first]
            for step in range(1, count):
                total = total + slots[layer, first + step]
            smalls[layer] = total

        def core(self):
            self.start(0, 2, c, lambda step: {"fsdp": index_of(y, z, x, 1 - c)}, 0)

        def along_x(self):
            self.take(0, 2)
            self.start(2, 4, x, lambda step: {"fsdp": index_of(y, z, (x + step) % 4, c)}, 1)

        def along_y(self):
            self.take(2, 4)
            self.start(6, 4, y, lambda step: {"fsdp": index_of((y + step) % 4, z, x, c)}, 4)

        def along_z(self):
            self.take(6, 4)
            self.start(10, 2, z, lambda step: {"fsdp": index_of(y, 1 - z, x, c)}, 7)

        def across(self):
            self.take(10, 2)
            self.start(12, 2, t, lambda step: {"tp": other}, 8)

        def finish(self):
            layer = self.layer
            mine = smalls[layer]
            self.take(12, 2)
            both = smalls[layer]
            row = lax.broadcasted_iota(jnp.int32, both.shape, 0)
            lane = lax.broadcasted_iota(jnp.int32, both.shape, 1)
            shared = (row == 0) | (row == 8) | ((row == 9) & (lane < PAIR))
            small_ref[layer] = jnp.where(shared, both, mine)
            for copy in self.copies:
                copy.wait_send()

    reduce_x0, reduce_g0, reduce_o0, reduce_x1, reduce_g1, reduce_o1 = [
        Reduce(ref, *buffers[7 * slot : 7 * slot + 7], rsem.at[slot], HALVES[slot % 3], PARTS[slot % 3])
        for slot, ref in enumerate(all_grads)
    ]
    smalls_1, smalls_0 = Smalls(1), Smalls(0)

    def send_pair(layer):
        bc_s[layer] = gx_ref[layer, :, pl.ds(INNER_OWN, PAIR)]
        return send(bc_s.at[layer], bc_r.at[layer], tsem, 6 + layer, tp=other)

    def take_pair(layer, copy):
        copy.wait_recv()
        gx_ref[layer, :, pl.ds(INNER_OWN, PAIR)] = bc_s[layer] + bc_r[layer]
        copy.wait_send()

    backward_gate(1)
    inner_1 = send_rows(2)
    backward_wo(1)
    reduce_o1.core()
    backward_ssd(1, inner_1, 2, lambda: None)
    reduce_o1.line()
    backward_conv(1)
    backward_in(1, 2, pl.ds(0, ROWS))
    backward_wg(1)
    reduce_g1.core()
    backward_wx(1)
    reduce_x1.core()
    reduce_o1.relay()
    reduce_g1.line()
    reduce_x1.line()
    wait_mix(2, pl.ds(0, ROWS))

    @pl.loop(0, 4)
    def _(step):
        rows = tile(step, 64)
        grad[rows, :] = next_grad(1, 2, rows)

    smalls_1.core()
    backward_gate(0)
    inner_0 = send_rows(3)
    reduce_g1.relay()
    backward_wo(0)
    reduce_o0.core()
    reduce_o1.plane()
    smalls_1.along_x()
    wait_mix(1, peer_rows)
    act_ref[...] = (hid[1, own_rows, :] + mixed_rows(1, own_rows)).astype(BF16)
    reduce_x1.relay()
    backward_ssd(0, inner_0, 3, lambda: None)
    reduce_o0.line()
    reduce_g1.plane()
    reduce_x1.plane()
    smalls_1.along_y()
    backward_wg(0)
    reduce_g0.core()
    backward_conv(0)
    backward_wx(0)
    reduce_x0.core()
    reduce_o0.relay()
    reduce_g0.line()
    backward_in(0, 3, peer_rows)
    smalls_0.core()
    reduce_x0.line()
    reduce_o1.finish(go_ref.at[1])
    reduce_g0.relay()
    smalls_1.along_z()
    smalls_0.along_x()
    reduce_o0.plane()
    reduce_g1.finish(gg_ref.at[1])
    reduce_x1.finish(gx_ref.at[1])
    pair_1 = send_pair(1)
    reduce_x0.relay()
    reduce_g0.plane()
    smalls_0.along_y()
    smalls_1.across()
    wait_mix(3, peer_rows)
    gin_ref[...] = next_grad(0, 3, own_rows)
    reduce_o0.finish(go_ref.at[0])
    reduce_x0.plane()
    smalls_0.along_z()
    take_pair(1, pair_1)
    smalls_1.finish()
    reduce_g0.finish(gg_ref.at[0])
    smalls_0.across()
    reduce_x0.finish(gx_ref.at[0])
    pair_0 = send_pair(0)
    smalls_0.finish()
    take_pair(0, pair_0)
    for copy in (send_x, send_cot, squares_0, squares_1, inner_1, inner_0):
        copy.wait_send()


def reduce_scratch(width, half):
    return [
        pltpu.VMEM((4, 2, 4, 16, width), BF16),
        pltpu.VMEM((2, 2, 4, 16, half), BF16),
        pltpu.VMEM((2, 4, 2, 16, width - half), BF16),
        pltpu.VMEM((7, 16, half), BF16),
        pltpu.VMEM((7, 16, width - half), BF16),
        pltpu.VMEM((2, 4, 16, half), BF16),
        pltpu.VMEM((2, 4, 16, width - half), BF16),
    ]


def whole_step(x_in, cotangent, own, lengths, vec, conv, head):
    scratch = [
        *[pltpu.VMEM((4, 2, 4, 2, 16, width), BF16) for width in PARTS + PARTS],
        pltpu.VMEM((2, ROWS, WIDTH), F32),
        pltpu.VMEM((2, WIDTH, ROWS), BF16),
        pltpu.VMEM((2, ROWS, ZX + PAIR), BF16),
        pltpu.VMEM((2, ROWS, SIGNAL), BF16),
        pltpu.VMEM((2, ROWS, INNER_OWN), F32),
        pltpu.VMEM((ROWS, INNER_OWN), BF16),
        pltpu.VMEM((2, ROWS, 128), F32),
        pltpu.VMEM((2, ROWS, 128), BF16),
        pltpu.VMEM((2, ROWS, 128), BF16),
        pltpu.VMEM((2, 128, ROWS), F32),
        pltpu.VMEM((2, ROWS, 128), F32),
        pltpu.VMEM((2, ROWS, 128), F32),
        pltpu.VMEM((2, ROWS, 128), F32),
        pltpu.VMEM((ROWS, WIDTH), BF16),
        pltpu.VMEM((ROWS, WIDTH), BF16),
        pltpu.VMEM((ROWS, WIDTH), BF16),
        pltpu.VMEM((WIDTH, ROWS), BF16),
        pltpu.VMEM((ROWS, WIDTH), F32),
        pltpu.VMEM((ROWS, SIGNAL), F32),
        pltpu.VMEM((ROWS, INNER_OWN + XS), BF16),
        pltpu.VMEM((ROWS, ROWS), F32),
        pltpu.VMEM((ROWS, ROWS), F32),
        pltpu.VMEM((ROWS, ROWS), F32),
        pltpu.VMEM((3, ROWS, 128), F32),
        pltpu.VMEM((ROWS, 128), F32),
        pltpu.VMEM((ROWS, 128), F32),
        pltpu.VMEM((ROWS, 128), F32),
        pltpu.VMEM((ROWS, 128), F32),
        pltpu.VMEM((4, ROWS, WIDTH), BF16),
        pltpu.VMEM((4, ROWS, WIDTH), BF16),
        pltpu.VMEM((4, 8, ROWS), F32),
        pltpu.VMEM((4, 8, ROWS), F32),
        pltpu.VMEM((2, 16, 1024), F32),
        pltpu.VMEM((2, 14, 16, 1024), F32),
        pltpu.VMEM((2, 16, PAIR), F32),
        pltpu.VMEM((2, 16, PAIR), F32),
        *[
            buffer
            for width, half in zip(PARTS + PARTS, HALVES + HALVES)
            for buffer in reduce_scratch(width, half)
        ],
        pltpu.VMEM((4, 2, 4, 2, 16, INNER_OWN), BF16),
        pltpu.VMEM((4, 2, 4, 2, 16, XS), BF16),
        pltpu.SemaphoreType.DMA((6, 2, GATHER_COPIES)),
        pltpu.SemaphoreType.DMA((6, 2, REDUCE_COPIES)),
        pltpu.SemaphoreType.DMA((2, 24)),
        pltpu.SemaphoreType.DMA((2, 2, 9)),
        pltpu.SemaphoreType.DMA((6,)),
    ]
    vmem = pl.BlockSpec(memory_space=pltpu.VMEM)
    return pl.pallas_call(
        body,
        out_shape=(
            jax.ShapeDtypeStruct((128, WIDTH), BF16),
            jax.ShapeDtypeStruct((128, WIDTH), F32),
            jax.ShapeDtypeStruct((2, 16, XS), F32),
            jax.ShapeDtypeStruct((2, 16, INNER_OWN), F32),
            jax.ShapeDtypeStruct((2, 16, OUT), F32),
            jax.ShapeDtypeStruct((2, 16, 1024), F32),
        ),
        in_specs=[vmem, vmem, vmem, pl.BlockSpec(memory_space=pltpu.SMEM), vmem, vmem, vmem],
        out_specs=(vmem,) * 6,
        scratch_shapes=scratch,
        compiler_params=pltpu.CompilerParams(
            collective_id=0, has_side_effects=True, vmem_limit_bytes=60 << 20
        ),
        name="whole_step",
    )(x_in, cotangent, own, lengths, vec, conv, head)


def finish_kernel(
    act_ref, gin_ref, gx_ref, gg_ref, go_ref, small_ref,
    act_out, grad_in, gain_in, w_zx, w_bc, w_dt, conv_x, conv_bc,
    bias_x, bias_bc, dt_bias, a_log, skip, gain_gate, w_out,
):
    w_out[...] = go_ref[...]
    act_out[...] = act_ref[...]
    grad_in[...] = gin_ref[...]
    w_bc[...] = gx_ref[:, :, INNER_OWN:SIGNAL]
    w_dt[...] = gx_ref[:, :, SIGNAL : SIGNAL + HEADS_OWN]
    channel = lax.broadcasted_iota(jnp.int32, (INNER_OWN, 128), 0) // 64
    head = lax.broadcasted_iota(jnp.int32, (INNER_OWN, 128), 1)
    members = (channel == head).astype(F32)
    for layer in range(2):
        for row in range(16):
            w_zx[layer, row, 0:1, :] = gg_ref[layer, row : row + 1, :]
            w_zx[layer, row, 1:2, :] = gx_ref[layer, row : row + 1, :INNER_OWN]
        one = slice(layer, layer + 1)
        gain_in[one, :] = small_ref[layer, 0:1, :]
        gain_gate[one, :] = small_ref[layer, 1:2, :]
        by_head = exact_dot(small_ref[layer], members)
        skip[one, :] = by_head[2:3, :HEADS_OWN]
        bias_x[one, :] = small_ref[layer, 3:4, :]
        conv_x[layer] = small_ref[layer, 4:8, :]
        for tap in range(4):
            conv_bc[layer, tap : tap + 1, :] = small_ref[layer, 8:9, tap * PAIR : (tap + 1) * PAIR]
        bias_bc[one, :] = small_ref[layer, 9:10, :PAIR]
        dt_bias[one, :] = small_ref[layer, 9:10, 256 : 256 + HEADS_OWN]
        a_log[one, :] = small_ref[layer, 9:10, 384 : 384 + HEADS_OWN]


def finish_step(*parts):
    shapes = [
        ((128, WIDTH), BF16), ((128, WIDTH), F32), ((2, WIDTH), F32), ((2, 16, 2, INNER_OWN), F32),
        ((2, 16, PAIR), F32), ((2, 16, HEADS_OWN), F32), ((2, 4, INNER_OWN), F32), ((2, 4, PAIR), F32),
        ((2, INNER_OWN), F32), ((2, PAIR), F32), ((2, HEADS_OWN), F32), ((2, HEADS_OWN), F32),
        ((2, HEADS_OWN), F32), ((2, INNER_OWN), F32), ((2, 16, INNER_OWN), F32),
    ]
    vmem = pl.BlockSpec(memory_space=pltpu.VMEM)
    return pl.pallas_call(
        finish_kernel,
        out_shape=[jax.ShapeDtypeStruct(*shape) for shape in shapes],
        in_specs=[vmem] * 6,
        out_specs=[vmem] * 15,
        compiler_params=pltpu.CompilerParams(vmem_limit_bytes=60 << 20),
        name="finish_step",
    )(*parts)


def pack_kernel(
    gain_in, w_zx, w_bc, w_dt, conv_x, conv_bc, bias_x, bias_bc, dt_bias, a_log, skip, gain_gate, w_out,
    own, vec, conv, head,
):
    heads = lax.broadcasted_iota(jnp.int32, (HEADS_OWN, INNER_OWN), 0)
    channel = lax.broadcasted_iota(jnp.int32, (HEADS_OWN, INNER_OWN), 1)
    members = jnp.where(heads == channel // 64, 1.0, 0.0)
    skips = exact_dot(skip[...].astype(F32), members)
    gains, gates = gain_in[...].astype(F32), gain_gate[...].astype(F32)
    shift_x, shift_bc = bias_x[...].astype(F32), bias_bc[...].astype(F32)
    sizes, rates = dt_bias[...].astype(F32), a_log[...].astype(F32)
    own[...] = jnp.zeros_like(own)
    vec[...] = jnp.zeros_like(vec)
    conv[...] = jnp.zeros_like(conv)
    head[...] = jnp.zeros_like(head)
    gate_at, out_at = XS, XS + INNER_OWN
    for layer in range(2):
        one = slice(layer, layer + 1)
        rows = [w_zx[layer, row].astype(F32) for row in range(16)]
        own[layer, :, :INNER_OWN] = jnp.concatenate([row[1:2] for row in rows], axis=0).astype(BF16)
        own[layer, :, INNER_OWN:SIGNAL] = w_bc[layer]
        own[layer, :, SIGNAL : SIGNAL + HEADS_OWN] = w_dt[layer]
        own[layer, :, gate_at:out_at] = jnp.concatenate([row[0:1] for row in rows], axis=0).astype(BF16)
        own[layer, :, out_at:] = w_out[layer]
        vec[layer, 0:1, :] = gains[one]
        vec[layer, 1:2, :] = gates[one]
        vec[layer, 2:3, :] = skips[one]
        conv[layer, 0:4, :INNER_OWN] = conv_x[layer].astype(F32)
        conv[layer, 0:4, INNER_OWN:] = conv_bc[layer].astype(F32)
        conv[layer, 4:5, :INNER_OWN] = shift_x[one]
        conv[layer, 4:5, INNER_OWN:] = shift_bc[one]
        head[layer, 0:1, :HEADS_OWN] = sizes[one]
        head[layer, 1:2, :HEADS_OWN] = rates[one]


def pack_step(*params):
    vmem = pl.BlockSpec(memory_space=pltpu.VMEM)
    return pl.pallas_call(
        pack_kernel,
        out_shape=[
            jax.ShapeDtypeStruct((2, 16, XS + INNER_OWN + OUT), BF16),
            jax.ShapeDtypeStruct((2, 8, WIDTH), F32),
            jax.ShapeDtypeStruct((2, 8, SIGNAL), F32),
            jax.ShapeDtypeStruct((2, 8, 128), F32),
        ],
        in_specs=[vmem] * 13,
        out_specs=[vmem] * 4,
        compiler_params=pltpu.CompilerParams(vmem_limit_bytes=60 << 20),
        name="pack_step",
    )(*params)


def shards(
    x_in, cotangent, seq_lengths, gain_in, w_zx, w_bc, w_dt, conv_x, conv_bc,
    bias_x, bias_bc, dt_bias, a_log, skip, gain_gate, w_out,
):
    own, vec, conv, head = pack_step(
        gain_in, w_zx, w_bc, w_dt, conv_x, conv_bc, bias_x, bias_bc,
        dt_bias, a_log, skip, gain_gate, jnp.swapaxes(w_out, 1, 2),
    )
    parts = whole_step(x_in, cotangent, own, seq_lengths, vec, conv, head)
    done = finish_step(*parts)
    return (*done[:-1], jnp.swapaxes(done[-1], 1, 2))


def solution(mesh):
    placed = (
        P(("fsdp", "tp"), None),
        P(("fsdp", "tp"), None),
        P("fsdp", None),
        P(),
        P(None, "fsdp", None, "tp"),
        P(None, "fsdp", None),
        P(None, "fsdp", "tp"),
        P(None, None, "tp"),
        P(),
        P(None, "tp"),
        P(),
        P(None, "tp"),
        P(None, "tp"),
        P(None, "tp"),
        P(None, "tp"),
        P(None, "tp", "fsdp"),
    )
    return jax.shard_map(
        shards,
        mesh=mesh,
        in_specs=placed,
        out_specs=(
            P(("fsdp", "tp"), None),
            P(("fsdp", "tp"), None),
            P(),
            P(None, "fsdp", None, "tp"),
            P(None, "fsdp", None),
            P(None, "fsdp", "tp"),
            P(None, None, "tp"),
            P(),
            P(None, "tp"),
            P(),
            P(None, "tp"),
            P(None, "tp"),
            P(None, "tp"),
            P(None, "tp"),
            P(None, "tp", "fsdp"),
        ),
        check_vma=False,
    )
```

```python
import jax
import jax.numpy as jnp
from jax import lax
from jax.experimental import pallas as pl
from jax.experimental.pallas import tpu as pltpu
from jax.sharding import PartitionSpec as P

MESH = pl.DeviceIdType.MESH
INNER = 2048
EPS = 1e-05


def place():
    index = lax.axis_index("fsdp")
    return index // 16, (index // 8) % 2, (index // 2) % 4, index % 2


def index_of(y, z, x, c):
    return ((y * 2 + z) * 4 + x) * 2 + c


PLANE_ZX = [(dz, dx) for dz in range(2) for dx in range(4) if (dz, dx) != (0, 0)]
PLANE_YZ = [(dy, dz) for dy in range(4) for dz in range(2) if (dy, dz) != (0, 0)]


def peers_of():
    y, z, x, c = place()
    found = [index_of(y, (z + dz) % 2, (x + dx) % 4, c) for dz, dx in PLANE_ZX]
    found += [index_of((y + dy) % 4, (z + dz) % 2, x, c) for dy, dz in PLANE_YZ if dy != 0]
    found.append(index_of(y, z, x, 1 - c))
    return found


def greet_all(with_tp):
    barrier = pltpu.get_barrier_semaphore()
    peers = peers_of()
    for peer in peers:
        pl.semaphore_signal(barrier, inc=1, device_id={"fsdp": peer}, device_id_type=MESH)
    count = len(peers)
    if with_tp:
        other = 1 - lax.axis_index("tp")
        pl.semaphore_signal(barrier, inc=1, device_id={"tp": other}, device_id_type=MESH)
        count += 1
    pl.semaphore_wait(barrier, count)


def send(src, dst, sems, slot, **where):
    copy = pltpu.make_async_remote_copy(
        src_ref=src,
        dst_ref=dst,
        send_sem=sems.at[0, slot],
        recv_sem=sems.at[1, slot],
        device_id=where,
        device_id_type=MESH,
    )
    copy.start()
    return copy


GATHER_COPIES = 30


class Gather:
    def __init__(self, whole, sems, first, half, end):
        self.whole, self.sems = whole, sems
        self.cols = (pl.ds(first, half - first), pl.ds(half, end - half))
        self.started = []

    def pair(self):
        y, z, x, c = place()
        ref = self.whole.at[y, z, x, c]
        self.pairs = [send(ref, ref, self.sems, 0, fsdp=index_of(y, 1 - z, x, c))]

    def spread(self):
        y, z, x, c = place()
        cols_a, cols_b = self.cols
        self.pairs[0].wait_recv()
        self.first = []
        for step in range(1, 4):
            ref = self.whole.at[y, :, x, c, :, cols_a]
            self.first.append(
                send(ref, ref, self.sems, step, fsdp=index_of(y, z, (x + step) % 4, c))
            )
            ref = self.whole.at[y, :, x, c, :, cols_b]
            self.first.append(
                send(ref, ref, self.sems, 3 + step, fsdp=index_of((y + step) % 4, z, x, c))
            )

    def plane(self):
        y, z, x, c = place()
        cols_a, cols_b = self.cols
        self.pairs, self.first = [], []
        for slot, (dz, dx) in enumerate(PLANE_ZX):
            ref = self.whole.at[y, z, x, c, :, cols_a]
            self.first.append(
                send(ref, ref, self.sems, slot, fsdp=index_of(y, (z + dz) % 2, (x + dx) % 4, c))
            )
        for slot, (dy, dz) in enumerate(PLANE_YZ):
            ref = self.whole.at[y, z, x, c, :, cols_b]
            self.first.append(
                send(ref, ref, self.sems, 7 + slot, fsdp=index_of((y + dy) % 4, (z + dz) % 2, x, c))
            )

    def line(self):
        y, z, x, c = place()
        cols_a, cols_b = self.cols
        for copy in self.first:
            copy.wait_recv()
        self.second = []
        for slot, step in enumerate((1, 3)):
            ref = self.whole.at[y, :, :, c, :, cols_a]
            self.second.append(
                send(ref, ref, self.sems, 14 + slot, fsdp=index_of((y + step) % 4, z, x, c))
            )
            ref = self.whole.at[:, :, x, c, :, cols_b]
            self.second.append(
                send(ref, ref, self.sems, 16 + slot, fsdp=index_of(y, z, (x + step) % 4, c))
            )
        self.third = []
        self.hand_over(0)

    def hand_over(self, step):
        y, z, x, c = place()
        cols_a, cols_b = self.cols
        ref = self.whole.at[(y - step + 4) % 4, :, :, c, :, cols_a]
        self.third.append(send(ref, ref, self.sems, 22 + step, fsdp=index_of(y, z, x, 1 - c)))
        ref = self.whole.at[:, :, (x - step + 4) % 4, c, :, cols_b]
        self.third.append(send(ref, ref, self.sems, 26 + step, fsdp=index_of(y, z, x, 1 - c)))

    def relay(self):
        y, z, x, c = place()
        cols_a, cols_b = self.cols
        self.fourth = []
        for slot, step in enumerate((1, 3)):
            self.second[2 * slot].wait_recv()
            ref = self.whole.at[(y - step + 4) % 4, slot, :, c, :, cols_a]
            self.fourth.append(
                send(ref, ref, self.sems, 18 + slot, fsdp=index_of((y + step) % 4, z, x, c))
            )
            self.second[2 * slot + 1].wait_recv()
            ref = self.whole.at[:, slot, (x - step + 4) % 4, c, :, cols_b]
            self.fourth.append(
                send(ref, ref, self.sems, 20 + slot, fsdp=index_of(y, z, (x + step) % 4, c))
            )
        self.hand_over(1)
        self.hand_over(3)

    def core(self):
        for copy in self.fourth:
            copy.wait_recv()
        self.hand_over(2)

    def finish(self):
        for copy in self.third:
            copy.wait_recv()
        for copy in self.pairs + self.first + self.second + self.third + self.fourth:
            copy.wait_send()


REDUCE_COPIES = 27


class Reduce:
    def __init__(
        self, grad, from_core, from_line_a, from_line_b, from_plane_a, from_plane_b, relay_a, relay_b, sems, half, end
    ):
        self.grad, self.from_core, self.sems = grad, from_core, sems
        self.line_a, self.line_b = from_line_a, from_line_b
        self.plane_a, self.plane_b = from_plane_a, from_plane_b
        self.relay_a, self.relay_b = relay_a, relay_b
        self.cols = (pl.ds(0, half), pl.ds(half, end - half))

    def core(self):
        y, z, x, c = place()
        self.copies = [
            send(
                self.grad.at[:, :, :, 1 - c],
                self.from_core,
                self.sems,
                0,
                fsdp=index_of(y, z, x, 1 - c),
            )
        ]

    def line(self):
        y, z, x, c = place()
        cols_a, cols_b = self.cols
        self.copies[0].wait_recv()

        @pl.loop(0, 32)
        def _(block):
            iy, iz, ix = block // 8, (block // 4) % 2, block % 4
            mine = self.grad[iy, iz, ix, c].astype(jnp.float32)
            theirs = self.from_core[iy, iz, ix].astype(jnp.float32)
            self.from_core[iy, iz, ix] = (mine + theirs).astype(jnp.bfloat16)

        self.relays, self.second = [], []
        for slot, step in enumerate((1, 3)):
            to, far = (y + step) % 4, (y + 2) % 4
            where = index_of(to, z, x, c)
            self.relays.append(
                send(self.from_core.at[far, slot, :, :, cols_a], self.relay_a.at[slot], self.sems, 1 + slot, fsdp=where)
            )
            self.second.append(
                send(
                    self.from_core.at[to, 1 - slot, :, :, cols_a],
                    self.line_a.at[slot, 1 - slot],
                    self.sems,
                    3 + slot,
                    fsdp=where,
                )
            )
            to, far = (x + step) % 4, (x + 2) % 4
            where = index_of(y, z, to, c)
            self.relays.append(
                send(self.from_core.at[:, slot, far, :, cols_b], self.relay_b.at[slot], self.sems, 5 + slot, fsdp=where)
            )
            self.second.append(
                send(
                    self.from_core.at[:, 1 - slot, to, :, cols_b],
                    self.line_b.at[slot, :, 1 - slot],
                    self.sems,
                    7 + slot,
                    fsdp=where,
                )
            )

    def relay(self):
        y, z, x, c = place()
        cols_a, cols_b = self.cols
        for copy in self.relays:
            copy.wait_recv()
        for slot, step in enumerate((1, 3)):
            to_y, to_x = (y + step) % 4, (x + step) % 4

            @pl.loop(0, 4)
            def _(block):
                mine = self.from_core[to_y, slot, block, :, cols_a].astype(jnp.float32)
                mine = mine + self.relay_a[slot, block].astype(jnp.float32)
                self.from_core[to_y, slot, block, :, cols_a] = mine.astype(jnp.bfloat16)
                mine = self.from_core[block, slot, to_x, :, cols_b].astype(jnp.float32)
                mine = mine + self.relay_b[slot, block].astype(jnp.float32)
                self.from_core[block, slot, to_x, :, cols_b] = mine.astype(jnp.bfloat16)

            self.second.append(
                send(
                    self.from_core.at[to_y, slot, :, :, cols_a],
                    self.line_a.at[slot, slot],
                    self.sems,
                    9 + slot,
                    fsdp=index_of(to_y, z, x, c),
                )
            )
            self.second.append(
                send(
                    self.from_core.at[:, slot, to_x, :, cols_b],
                    self.line_b.at[slot, :, slot],
                    self.sems,
                    11 + slot,
                    fsdp=index_of(y, z, to_x, c),
                )
            )

    def plane(self):
        y, z, x, c = place()
        cols_a, cols_b = self.cols
        for copy in self.second:
            copy.wait_recv()

        @pl.loop(0, 8)
        def _(block):
            iz, ix = block // 4, block % 4
            total = self.from_core[y, iz, ix, :, cols_a].astype(jnp.float32)
            for step in range(2):
                total = total + self.line_a[step, iz, ix].astype(jnp.float32)
            self.line_a[0, iz, ix] = total.astype(jnp.bfloat16)
            iy, iz = block // 2, block % 2
            total = self.from_core[iy, iz, x, :, cols_b].astype(jnp.float32)
            for step in range(2):
                total = total + self.line_b[step, iy, iz].astype(jnp.float32)
            self.line_b[0, iy, iz] = total.astype(jnp.bfloat16)

        self.third = []
        for slot, (dz, dx) in enumerate(PLANE_ZX):
            tz, tx = (z + dz) % 2, (x + dx) % 4
            self.third.append(
                send(
                    self.line_a.at[0, tz, tx],
                    self.plane_a.at[slot],
                    self.sems,
                    13 + slot,
                    fsdp=index_of(y, tz, tx, c),
                )
            )
        for slot, (dy, dz) in enumerate(PLANE_YZ):
            ty, tz = (y + dy) % 4, (z + dz) % 2
            self.third.append(
                send(
                    self.line_b.at[0, ty, tz],
                    self.plane_b.at[slot],
                    self.sems,
                    20 + slot,
                    fsdp=index_of(ty, tz, x, c),
                )
            )

    def finish(self, out):
        y, z, x, c = place()
        cols_a, cols_b = self.cols
        for copy in self.third:
            copy.wait_recv()
        total = self.line_a[0, z, x].astype(jnp.float32)
        for slot in range(7):
            total = total + self.plane_a[slot].astype(jnp.float32)
        out[:, cols_a] = total
        total = self.line_b[0, y, z].astype(jnp.float32)
        for slot in range(7):
            total = total + self.plane_b[slot].astype(jnp.float32)
        out[:, cols_b] = total
        for copy in self.copies + self.relays + self.second + self.third:
            copy.wait_send()


ROWS, WIDTH, INNER_OWN, STATE, HEADS_OWN = 256, 1024, 1024, 128, 16
ZX, PAIR, DT, OUT = 2048, 256, 128, 1024
SIGNAL = INNER_OWN + PAIR
XS = SIGNAL + DT
PARTS = (XS, INNER_OWN, OUT)
HALVES = (768, 512, 512)
F32, BF16 = jnp.float32, jnp.bfloat16
NN = (((1,), (0,)), ((), ()))
NT = (((1,), (1,)), ((), ()))
TN = (((0,), (0,)), ((), ()))


def dot(a, b, dims=NN):
    return lax.dot_general(a, b, dims, preferred_element_type=F32)


def exact_dot(a, b, dims=NN):
    return lax.dot_general(
        a, b, dims, preferred_element_type=F32, precision=lax.Precision.HIGHEST
    )


def tile(index, width):
    return pl.ds(pl.multiple_of(index * width, width), width)


def twice(part):
    return jnp.concatenate([part, part], axis=1)


def three_parts(value):
    high = value.astype(BF16)
    rest = value - high.astype(F32)
    middle = rest.astype(BF16)
    return high, middle, (rest - middle.astype(F32)).astype(BF16)


def parts_by_lane(value):
    lane = lax.broadcasted_iota(jnp.int32, value.shape, 1)
    terms = [part.astype(F32) for part in three_parts(jnp.where(lane < 16, value, 0.0))]
    return (terms[0] + pltpu.roll(terms[1], 16, 1) + pltpu.roll(terms[2], 32, 1)).astype(BF16)


def picked(parts, heads):
    row = lax.broadcasted_iota(jnp.int32, heads.shape, 0)
    return dot(parts, jnp.where(((row & 15) == heads) & (row < 48), 1.0, 0.0).astype(BF16))


def body(
    x_ref, cot_ref, own_ref, lens_ref, vec_ref, conv_ref, head_ref,
    act_ref, gin_ref, gx_ref, gg_ref, go_ref, small_ref,
    wx0, wg0, wo0, wx1, wg1, wo1,
    hid, norm_t, proj, vals, ssd, ngate, steps, step_parts, cum_parts, cums_t, scales, gscales, sig_dt,
    xs, cots, normed, cot_t, grad, dact, dproj, scores, dscores, mask, same, live, acc, dcum, dstep,
    mixs, mixr, row_s, row_r, smalls, slots, bc_s, bc_r,
    *rest,
):
    buffers, (gg0, gx0, gsem, rsem, tsem, ssem, lsem) = rest[:42], rest[42:]
    y, z, x, c = place()
    t = lax.axis_index("tp")
    other = 1 - t
    own_rows = pl.ds(pl.multiple_of(t * 128, 128), 128)
    peer_rows = pl.ds(pl.multiple_of(other * 128, 128), 128)

    def load_cols(ref, cols):
        part = ref[:, :, :, :, :, cols]
        return part.reshape(WIDTH, part.shape[-1])

    def store_cols(ref, cols, part):
        ref[:, :, :, :, :, cols] = part.astype(BF16).reshape(4, 2, 4, 2, 16, part.shape[-1])

    x_w, g_w, o_w = (wx0, wx1), (wg0, wg1), (wo0, wo1)
    whole = (wx0, wg0, wo0, wx1, wg1, wo1)
    gate_grads, signal_grads = (gg0, wg1), (gx0, wx1)
    all_grads = (gx0, gg0, wo0, wx1, wg1, wo1)

    keeps = []
    for slot, ref in enumerate(whole):
        first = sum(PARTS[: slot % 3])
        keeps.append(
            pltpu.make_async_copy(
                own_ref.at[slot // 3, :, pl.ds(first, PARTS[slot % 3])],
                ref.at[y, z, x, c],
                lsem.at[slot],
            )
        )
        keeps[-1].start()
    greet_all(True)
    gather_x0, gather_g0, gather_o0, gather_x1, gather_g1, gather_o1 = [
        Gather(ref, gsem.at[slot], 0, HALVES[slot % 3], PARTS[slot % 3])
        for slot, ref in enumerate(whole)
    ]
    keeps[0].wait()
    gather_x0.plane()
    for keep in keeps[1:]:
        keep.wait()
    gather_g0.pair()
    gather_o0.pair()
    xs[own_rows, :] = x_ref[...]
    cots[own_rows, :] = cot_ref[...]

    bounds = [lens_ref[0, 0]]
    for j in range(1, 4):
        bounds.append(bounds[-1] + lens_ref[0, j])

    def ids_at(pos):
        total = jnp.zeros(pos.shape, jnp.int32)
        for bound in bounds:
            total = total + (pos >= bound).astype(jnp.int32)
        return total

    pos = lax.broadcasted_iota(jnp.int32, (ROWS, 128), 0)
    ids = ids_at(pos)
    live[...] = (ids < 4).astype(F32)
    for back in range(1, 4):
        same[back - 1] = ((ids == ids_at(pos - back)) & (pos >= back)).astype(F32)
    at = lax.broadcasted_iota(jnp.int32, (ROWS, ROWS), 0)
    src = lax.broadcasted_iota(jnp.int32, (ROWS, ROWS), 1)
    mask[...] = jnp.where((ids_at(at) == ids_at(src)) & (src <= at), 0.0, -1e30)
    smalls[...] = jnp.zeros_like(smalls)

    def spread_rows(part):
        return jnp.broadcast_to(part[0:1, :], (128, ROWS)).T

    def send_rows(which):
        total = jnp.sum(acc[...], axis=1, keepdims=True)
        row_s[which] = jnp.broadcast_to(total, (ROWS, 128)).T[:8, :]
        return send(row_s.at[which], row_r.at[which], tsem, 2 + which, tp=other)

    def norm_layer(layer):
        @pl.loop(0, 4)
        def _(step):
            rows = tile(step, 64)
            part = hid[layer, rows, :]
            scale = lax.rsqrt(jnp.mean(part * part, axis=1, keepdims=True) + EPS)
            scales[layer, rows, :] = jnp.broadcast_to(scale, (64, 128))
            normed[rows, :] = (part * scale * vec_ref[layer, 0:1, :]).astype(BF16)

    def transposed(from_ref, to_ref):
        @pl.loop(0, 8)
        def _(step):
            cols = tile(step, 128)
            to_ref[cols, :] = from_ref[:, cols].astype(F32).T.astype(BF16)

    def conv_pre(layer, signal, cols):
        pre = conv_ref[layer, 4:5, cols] + conv_ref[layer, 3:4, cols] * signal
        shifted = []
        for back in range(1, 4):
            earlier = pltpu.roll(signal, back, 0) * twice(same[back - 1])
            shifted.append(earlier)
            pre = pre + conv_ref[layer, 3 - back : 4 - back, cols] * earlier
        return pre, shifted

    def shift_cols(step):
        return pl.ds(pl.multiple_of(INNER_OWN + step * 256, 256), 256)

    def project_gate(layer):
        @pl.loop(0, 4)
        def _(step):
            cols = tile(step, 256)
            proj[layer, :, cols] = dot(normed[...], load_cols(g_w[layer], cols)).astype(BF16)

    def project_signal(layer):
        @pl.loop(0, 5)
        def _(step):
            part = dot(normed[...], load_cols(x_w[layer], tile(step, 256)))
            proj[layer, :, shift_cols(step)] = part.astype(BF16)

    def forward_steps(layer):
        raw = dot(normed[...], load_cols(x_w[layer], pl.ds(SIGNAL, DT)))
        raw = raw.astype(BF16).astype(F32) + head_ref[layer, 0:1, :]
        sig_dt[layer] = jax.nn.sigmoid(raw)
        step_sizes = jnp.maximum(raw, 0.0) + jnp.log1p(jnp.exp(-jnp.abs(raw)))
        steps[layer] = step_sizes
        rate = -jnp.exp(head_ref[layer, 1:2, :])
        lower = (src <= at).astype(F32)
        summed = exact_dot(lower, step_sizes * rate)
        cum_parts[layer] = parts_by_lane(summed)
        step_parts[layer] = parts_by_lane(step_sizes)
        cums_t[layer] = summed.T

    def forward_conv(layer):
        @pl.loop(0, 5)
        def _(step):
            signal = proj[layer, :, shift_cols(step)].astype(F32)
            pre, unused = conv_pre(layer, signal, tile(step, 256))
            vals[layer, :, tile(step, 256)] = (pre * jax.nn.sigmoid(pre)).astype(BF16)

    def set_scores(layer):
        b_mat = vals[layer, :, pl.ds(INNER_OWN, STATE)]
        c_mat = vals[layer, :, pl.ds(INNER_OWN + STATE, STATE)]
        scores[...] = dot(c_mat, b_mat, NT)

    def decays(layer, head):
        heads = jnp.full((128, ROWS), head, jnp.int32)
        return jnp.exp(
            picked(cum_parts[layer], heads) - cums_t[layer, pl.ds(head, 1), :] + mask[...]
        )

    def pair_heads(step):
        return 2 * step + lax.broadcasted_iota(jnp.int32, (128, 128), 1) // 64

    def forward_ssd(layer):
        set_scores(layer)

        @pl.loop(0, 8)
        def _(step):
            cols = tile(step, 128)
            values = vals[layer, :, cols].astype(F32)
            upper = lax.broadcasted_iota(jnp.int32, (ROWS, 128), 1) >= 64
            total = vec_ref[layer, 2:3, cols] * values
            scaled = values * picked(step_parts[layer], pair_heads(step))
            for half in range(2):
                weights = (scores[...] * decays(layer, 2 * step + half)).astype(BF16)
                mine = jnp.where(upper == (half == 1), scaled, 0.0).astype(BF16)
                total = total + dot(weights, mine)
            ssd[layer, :, cols] = total

    def forward_gate(layer):
        acc[...] = jnp.zeros_like(acc)

        @pl.loop(0, 8)
        def _(step):
            cols = tile(step, 128)
            gate = proj[layer, :, cols].astype(F32)
            gated = ssd[layer, :, cols] * gate * jax.nn.sigmoid(gate)
            acc[...] += gated * gated
            ngate[:, cols] = (gated * vec_ref[layer, 1:2, cols]).astype(BF16)

    def mix_copy(which, step, rows):
        ref_s = mixs.at[which, rows, tile(step, 256)]
        ref_r = mixr.at[which, rows, tile(step, 256)]
        return pltpu.make_async_remote_copy(
            src_ref=ref_s,
            dst_ref=ref_r,
            send_sem=tsem.at[0, 8 + 4 * which + step],
            recv_sem=tsem.at[1, 8 + 4 * which + step],
            device_id={"tp": other},
            device_id_type=MESH,
        )

    def wait_mix(which, rows):
        @pl.loop(0, 4)
        def _(step):
            copy = mix_copy(which, step, rows)
            copy.wait_recv()
            copy.wait_send()

    def forward_out(layer, rows):
        @pl.loop(0, 4)
        def _(step):
            weight = o_w[layer][step].reshape(256, OUT)
            mixs[layer, :, tile(step, 256)] = dot(ngate[...], weight, NT).astype(BF16)
            mix_copy(layer, step, rows).start()

    def take_gate_scale(layer, copy):
        copy.wait_recv()
        total = row_s[layer] + row_r[layer]
        gscales[layer] = spread_rows(lax.rsqrt(total / INNER + EPS))

    def mixed_rows(layer, rows):
        part = mixs[layer, rows, :].astype(F32) + mixr[layer, rows, :].astype(F32)
        return part * (gscales[layer, rows, 0:1] * live[rows, 0:1])

    gather_x0.line()
    gather_g0.spread()
    gather_o0.spread()
    send_x = send(x_ref, xs.at[own_rows], tsem, 0, tp=other)
    gather_x0.relay()
    gather_g0.line()
    gather_x0.core()
    gather_o0.line()
    for job in (gather_x1, gather_g1, gather_o1):
        job.pair()
    send_x.wait_recv()

    @pl.loop(0, 4)
    def _(step):
        rows = tile(step, 64)
        hid[0, rows, :] = xs[rows, :].astype(F32)

    norm_layer(0)
    gather_x0.finish()
    gather_g0.relay()
    for job in (gather_x1, gather_g1, gather_o1):
        job.spread()
    project_signal(0)
    gather_g0.core()
    gather_o0.relay()
    forward_steps(0)
    forward_conv(0)
    gather_x1.line()
    gather_o0.core()
    forward_ssd(0)
    gather_g0.finish()
    project_gate(0)
    forward_gate(0)
    squares_0 = send_rows(0)
    gather_x1.relay()
    gather_g1.line()
    gather_o0.finish()
    forward_out(0, pl.ds(0, ROWS))
    transposed(normed, norm_t.at[0])
    gather_x1.core()
    gather_g1.relay()
    gather_o1.line()
    take_gate_scale(0, squares_0)
    gather_x1.finish()
    wait_mix(0, pl.ds(0, ROWS))
    send_cot = send(cot_ref, cots.at[own_rows], tsem, 1, tp=other)

    @pl.loop(0, 4)
    def _(step):
        rows = tile(step, 64)
        hid[1, rows, :] = hid[0, rows, :] + mixed_rows(0, rows)

    norm_layer(1)
    project_signal(1)
    gather_g1.core()
    forward_steps(1)
    gather_o1.relay()
    forward_conv(1)
    forward_ssd(1)
    gather_o1.core()
    gather_g1.finish()
    project_gate(1)
    forward_gate(1)
    squares_1 = send_rows(1)
    gather_o1.finish()
    forward_out(1, peer_rows)
    transposed(normed, norm_t.at[1])
    send_cot.wait_recv()

    @pl.loop(0, 4)
    def _(step):
        rows = tile(step, 64)
        grad[rows, :] = cots[rows, :].astype(F32)

    take_gate_scale(1, squares_1)

    def backward_gate(layer):
        @pl.loop(0, 4)
        def _(step):
            rows = tile(step, 64)
            normed[rows, :] = (live[rows, 0:1] * grad[rows, :]).astype(BF16)

        acc[...] = jnp.zeros_like(acc)

        @pl.loop(0, 4)
        def _(step):
            cols = tile(step, 256)
            d_normed_gate = dot(normed[...], load_cols(o_w[layer], cols))
            gate = proj[layer, :, cols].astype(F32)
            gated = ssd[layer, :, cols] * gate * jax.nn.sigmoid(gate)
            normal = gated * twice(gscales[layer])
            gain = vec_ref[layer, 1:2, cols]
            ngate[:, cols] = (normal * gain).astype(BF16)
            smalls[layer, 1:2, cols] = jnp.sum(d_normed_gate * normal, axis=0, keepdims=True)
            weighted = d_normed_gate * gain
            dact[:, cols] = weighted
            inner = weighted * gated
            acc[...] += inner[:, :128] + inner[:, 128:]

    def backward_wo(layer):
        transposed(normed, cot_t)

        @pl.loop(0, 4)
        def _(step):
            part = dot(cot_t[tile(step, 256), :], ngate[...]).astype(BF16)
            o_w[layer][step] = part.reshape(2, 4, 2, 16, OUT)

    def backward_ssd(layer, copy, which, between):
        copy.wait_recv()
        inner = spread_rows(row_s[which] + row_r[which])
        gs = gscales[layer]
        acc[...] = gs * gs * gs * inner / INNER
        set_scores(layer)
        dscores[...] = jnp.zeros_like(dscores)
        dcum[...] = jnp.zeros_like(dcum)
        dstep[...] = jnp.zeros_like(dstep)

        def one(step):
            cols = tile(step, 128)
            upper = lax.broadcasted_iota(jnp.int32, (ROWS, 128), 1) >= 64
            gate = proj[layer, :, cols].astype(F32)
            out = ssd[layer, :, cols]
            sigmoid = jax.nn.sigmoid(gate)
            silu = gate * sigmoid
            d_gated = gscales[layer] * dact[:, cols] - out * silu * acc[...]
            d_out = d_gated * silu
            dproj[:, cols] = (d_gated * out * sigmoid * (1.0 + gate * (1.0 - sigmoid))).astype(BF16)
            values = vals[layer, :, cols].astype(F32)
            size = picked(step_parts[layer], pair_heads(step))
            scaled = (values * size).astype(BF16)
            back = jnp.zeros((ROWS, 128), F32)
            for half in range(2):
                head = 2 * step + half
                decay = decays(layer, head)
                weights = (scores[...] * decay).astype(BF16)
                d_half = jnp.where(upper == (half == 1), d_out, 0.0).astype(BF16)
                dscores[...] += dot(d_half, scaled, NT) * decay
                back = back + dot(weights, d_half, TN)
            skip = vec_ref[layer, 2:3, cols]
            dact[:, cols] = skip * d_out + size * back
            smalls[layer, 2:3, cols] = jnp.sum(d_out * values, axis=0, keepdims=True)
            inside = out - skip * values
            turn = d_out.astype(BF16).astype(F32) * inside - scaled.astype(F32) * back
            size_turn = values * back
            lane = lax.broadcasted_iota(jnp.int32, (128, 128), 0)
            to = lax.broadcasted_iota(jnp.int32, (128, 128), 1)
            members = jnp.where(to == 2 * step + lane // 64, 1.0, 0.0).astype(BF16)
            for part in three_parts(turn):
                dcum[...] += dot(part, members)
            for part in three_parts(size_turn)[:2]:
                dstep[...] += dot(part, members)

        pl.loop(0, 4)(one)
        between()
        pl.loop(4, 8)(one)
        rate = -jnp.exp(head_ref[layer, 1:2, :])
        later = (src >= at).astype(F32)
        d_log = exact_dot(later, dcum[...])
        d_raw = (dstep[...] + rate * d_log) * sig_dt[layer]
        smalls[layer, 9:10, pl.ds(256, 128)] = jnp.sum(d_raw, axis=0, keepdims=True)
        smalls[layer, 9:10, pl.ds(384, 128)] = rate * jnp.sum(
            steps[layer] * d_log, axis=0, keepdims=True
        )
        dproj[:, pl.ds(ZX + PAIR, DT)] = d_raw.astype(BF16)
        d_scores = dscores[...].astype(BF16)
        b_mat = vals[layer, :, pl.ds(INNER_OWN, STATE)]
        c_mat = vals[layer, :, pl.ds(INNER_OWN + STATE, STATE)]
        dact[:, pl.ds(INNER_OWN, STATE)] = dot(d_scores, c_mat, TN)
        dact[:, pl.ds(INNER_OWN + STATE, STATE)] = dot(d_scores, b_mat)

    def backward_conv(layer):
        def one(signal_cols, cols):
            signal = proj[layer, :, signal_cols].astype(F32)
            pre, shifted = conv_pre(layer, signal, cols)
            sigmoid = jax.nn.sigmoid(pre)
            d_pre = dact[:, cols] * sigmoid * (1.0 + pre * (1.0 - sigmoid))
            d_signal = conv_ref[layer, 3:4, cols] * d_pre
            d_taps = [jnp.sum(d_pre * signal, axis=0, keepdims=True)]
            for back in range(1, 4):
                d_signal = d_signal + conv_ref[layer, 3 - back : 4 - back, cols] * pltpu.roll(
                    d_pre * twice(same[back - 1]), ROWS - back, 0
                )
                d_taps.append(jnp.sum(d_pre * shifted[back - 1], axis=0, keepdims=True))
            dproj[:, signal_cols] = d_signal.astype(BF16)
            return jnp.sum(d_pre, axis=0, keepdims=True), d_taps

        @pl.loop(0, 4)
        def _(step):
            cols = tile(step, 256)
            d_bias, d_taps = one(shift_cols(step), cols)
            smalls[layer, 3:4, cols] = d_bias
            for back in range(4):
                smalls[layer, 7 - back : 8 - back, cols] = d_taps[back]

        d_bias, d_taps = one(pl.ds(ZX, PAIR), pl.ds(INNER_OWN, PAIR))
        smalls[layer, 9:10, pl.ds(0, PAIR)] = d_bias
        for back in range(4):
            smalls[layer, 8:9, pl.ds((3 - back) * PAIR, PAIR)] = d_taps[back]

    def backward_in(layer, which, rows):
        @pl.loop(0, 4)
        def _(step):
            cols = tile(step, 256)
            part = dot(dproj[:, :INNER_OWN], g_w[layer][step].reshape(256, INNER_OWN), NT)
            part = part + dot(dproj[:, INNER_OWN:], x_w[layer][step].reshape(256, XS), NT)
            mixs[which, :, cols] = part.astype(BF16)
            mix_copy(which, step, rows).start()
            smalls[layer, 0:1, cols] = jnp.sum(
                part * hid[layer, :, cols] * twice(scales[layer]), axis=0, keepdims=True
            )

    def backward_wg(layer):
        @pl.loop(0, 4)
        def _(step):
            cols = tile(step, 256)
            store_cols(gate_grads[layer], cols, dot(norm_t[layer], dproj[:, cols]))

    def backward_wx(layer):
        @pl.loop(0, 5)
        def _(step):
            part = dot(norm_t[layer], dproj[:, shift_cols(step)])
            store_cols(signal_grads[layer], tile(step, 256), part)

        part = dot(norm_t[layer], dproj[:, pl.ds(ZX + PAIR, DT)])
        store_cols(signal_grads[layer], pl.ds(SIGNAL, DT), part)

    def next_grad(layer, which, rows):
        part = mixs[which, rows, :].astype(F32) + mixr[which, rows, :].astype(F32)
        part = part * vec_ref[layer, 0:1, :]
        before = hid[layer, rows, :]
        scale = scales[layer, rows, 0:1]
        inner = jnp.sum(part * before, axis=1, keepdims=True)
        return grad[rows, :] + scale * part - before * (scale * scale * scale * inner / WIDTH)

    class Smalls:
        def __init__(self, layer):
            self.layer = layer
            self.copies = []

        def start(self, first, count, mine, where, base):
            layer = self.layer
            slots[layer, first + mine] = smalls[layer]
            ref = slots.at[layer, first + mine]
            for step in range(1, count):
                self.copies.append(send(ref, ref, ssem.at[layer], base + step - 1, **where(step)))
            self.pending = self.copies[len(self.copies) - count + 1 :]

        def take(self, first, count):
            layer = self.layer
            for copy in self.pending:
                copy.wait_recv()
            total = slots[layer, first]
            for step in range(1, count):
                total = total + slots[layer, first + step]
            smalls[layer] = total

        def core(self):
            self.start(0, 2, c, lambda step: {"fsdp": index_of(y, z, x, 1 - c)}, 0)

        def along_x(self):
            self.take(0, 2)
            self.start(2, 4, x, lambda step: {"fsdp": index_of(y, z, (x + step) % 4, c)}, 1)

        def along_y(self):
            self.take(2, 4)
            self.start(6, 4, y, lambda step: {"fsdp": index_of((y + step) % 4, z, x, c)}, 4)

        def along_z(self):
            self.take(6, 4)
            self.start(10, 2, z, lambda step: {"fsdp": index_of(y, 1 - z, x, c)}, 7)

        def across(self):
            self.take(10, 2)
            self.start(12, 2, t, lambda step: {"tp": other}, 8)

        def finish(self):
            layer = self.layer
            mine = smalls[layer]
            self.take(12, 2)
            both = smalls[layer]
            row = lax.broadcasted_iota(jnp.int32, both.shape, 0)
            lane = lax.broadcasted_iota(jnp.int32, both.shape, 1)
            shared = (row == 0) | (row == 8) | ((row == 9) & (lane < PAIR))
            small_ref[layer] = jnp.where(shared, both, mine)
            for copy in self.copies:
                copy.wait_send()

    reduce_x0, reduce_g0, reduce_o0, reduce_x1, reduce_g1, reduce_o1 = [
        Reduce(ref, *buffers[7 * slot : 7 * slot + 7], rsem.at[slot], HALVES[slot % 3], PARTS[slot % 3])
        for slot, ref in enumerate(all_grads)
    ]
    smalls_1, smalls_0 = Smalls(1), Smalls(0)

    def send_pair(layer):
        bc_s[layer] = gx_ref[layer, :, pl.ds(INNER_OWN, PAIR)]
        return send(bc_s.at[layer], bc_r.at[layer], tsem, 6 + layer, tp=other)

    def take_pair(layer, copy):
        copy.wait_recv()
        gx_ref[layer, :, pl.ds(INNER_OWN, PAIR)] = bc_s[layer] + bc_r[layer]
        copy.wait_send()

    backward_gate(1)
    inner_1 = send_rows(2)
    backward_wo(1)
    reduce_o1.core()
    backward_ssd(1, inner_1, 2, lambda: None)
    reduce_o1.line()
    backward_conv(1)
    backward_in(1, 2, pl.ds(0, ROWS))
    backward_wg(1)
    reduce_g1.core()
    backward_wx(1)
    reduce_x1.core()
    reduce_o1.relay()
    reduce_g1.line()
    reduce_x1.line()
    smalls_1.core()
    wait_mix(1, peer_rows)
    act_ref[...] = (hid[1, own_rows, :] + mixed_rows(1, own_rows)).astype(BF16)
    wait_mix(2, pl.ds(0, ROWS))

    @pl.loop(0, 4)
    def _(step):
        rows = tile(step, 64)
        grad[rows, :] = next_grad(1, 2, rows)

    backward_gate(0)
    inner_0 = send_rows(3)
    reduce_g1.relay()
    backward_wo(0)
    reduce_o0.core()
    reduce_o1.plane()
    smalls_1.along_x()
    reduce_x1.relay()
    backward_ssd(0, inner_0, 3, lambda: None)
    reduce_o0.line()
    reduce_g1.plane()
    reduce_x1.plane()
    smalls_1.along_y()
    backward_wg(0)
    reduce_g0.core()
    backward_conv(0)
    backward_wx(0)
    reduce_x0.core()
    reduce_o0.relay()
    reduce_g0.line()
    backward_in(0, 3, peer_rows)
    smalls_0.core()
    reduce_x0.line()
    reduce_o1.finish(go_ref.at[1])
    reduce_g0.relay()
    smalls_1.along_z()
    smalls_0.along_x()
    reduce_o0.plane()
    reduce_g1.finish(gg_ref.at[1])
    reduce_x1.finish(gx_ref.at[1])
    pair_1 = send_pair(1)
    reduce_x0.relay()
    reduce_g0.plane()
    smalls_0.along_y()
    smalls_1.across()
    wait_mix(3, peer_rows)
    gin_ref[...] = next_grad(0, 3, own_rows)
    reduce_o0.finish(go_ref.at[0])
    reduce_x0.plane()
    smalls_0.along_z()
    take_pair(1, pair_1)
    smalls_1.finish()
    reduce_g0.finish(gg_ref.at[0])
    smalls_0.across()
    reduce_x0.finish(gx_ref.at[0])
    pair_0 = send_pair(0)
    smalls_0.finish()
    take_pair(0, pair_0)
    for copy in (send_x, send_cot, squares_0, squares_1, inner_1, inner_0):
        copy.wait_send()


def reduce_scratch(width, half):
    return [
        pltpu.VMEM((4, 2, 4, 16, width), BF16),
        pltpu.VMEM((2, 2, 4, 16, half), BF16),
        pltpu.VMEM((2, 4, 2, 16, width - half), BF16),
        pltpu.VMEM((7, 16, half), BF16),
        pltpu.VMEM((7, 16, width - half), BF16),
        pltpu.VMEM((2, 4, 16, half), BF16),
        pltpu.VMEM((2, 4, 16, width - half), BF16),
    ]


def whole_step(x_in, cotangent, own, lengths, vec, conv, head):
    scratch = [
        *[pltpu.VMEM((4, 2, 4, 2, 16, width), BF16) for width in PARTS + PARTS],
        pltpu.VMEM((2, ROWS, WIDTH), F32),
        pltpu.VMEM((2, WIDTH, ROWS), BF16),
        pltpu.VMEM((2, ROWS, ZX + PAIR), BF16),
        pltpu.VMEM((2, ROWS, SIGNAL), BF16),
        pltpu.VMEM((2, ROWS, INNER_OWN), F32),
        pltpu.VMEM((ROWS, INNER_OWN), BF16),
        pltpu.VMEM((2, ROWS, 128), F32),
        pltpu.VMEM((2, ROWS, 128), BF16),
        pltpu.VMEM((2, ROWS, 128), BF16),
        pltpu.VMEM((2, 128, ROWS), F32),
        pltpu.VMEM((2, ROWS, 128), F32),
        pltpu.VMEM((2, ROWS, 128), F32),
        pltpu.VMEM((2, ROWS, 128), F32),
        pltpu.VMEM((ROWS, WIDTH), BF16),
        pltpu.VMEM((ROWS, WIDTH), BF16),
        pltpu.VMEM((ROWS, WIDTH), BF16),
        pltpu.VMEM((WIDTH, ROWS), BF16),
        pltpu.VMEM((ROWS, WIDTH), F32),
        pltpu.VMEM((ROWS, SIGNAL), F32),
        pltpu.VMEM((ROWS, INNER_OWN + XS), BF16),
        pltpu.VMEM((ROWS, ROWS), F32),
        pltpu.VMEM((ROWS, ROWS), F32),
        pltpu.VMEM((ROWS, ROWS), F32),
        pltpu.VMEM((3, ROWS, 128), F32),
        pltpu.VMEM((ROWS, 128), F32),
        pltpu.VMEM((ROWS, 128), F32),
        pltpu.VMEM((ROWS, 128), F32),
        pltpu.VMEM((ROWS, 128), F32),
        pltpu.VMEM((4, ROWS, WIDTH), BF16),
        pltpu.VMEM((4, ROWS, WIDTH), BF16),
        pltpu.VMEM((4, 8, ROWS), F32),
        pltpu.VMEM((4, 8, ROWS), F32),
        pltpu.VMEM((2, 16, 1024), F32),
        pltpu.VMEM((2, 14, 16, 1024), F32),
        pltpu.VMEM((2, 16, PAIR), F32),
        pltpu.VMEM((2, 16, PAIR), F32),
        *[
            buffer
            for width, half in zip(PARTS + PARTS, HALVES + HALVES)
            for buffer in reduce_scratch(width, half)
        ],
        pltpu.VMEM((4, 2, 4, 2, 16, INNER_OWN), BF16),
        pltpu.VMEM((4, 2, 4, 2, 16, XS), BF16),
        pltpu.SemaphoreType.DMA((6, 2, GATHER_COPIES)),
        pltpu.SemaphoreType.DMA((6, 2, REDUCE_COPIES)),
        pltpu.SemaphoreType.DMA((2, 24)),
        pltpu.SemaphoreType.DMA((2, 2, 9)),
        pltpu.SemaphoreType.DMA((6,)),
    ]
    vmem = pl.BlockSpec(memory_space=pltpu.VMEM)
    return pl.pallas_call(
        body,
        out_shape=(
            jax.ShapeDtypeStruct((128, WIDTH), BF16),
            jax.ShapeDtypeStruct((128, WIDTH), F32),
            jax.ShapeDtypeStruct((2, 16, XS), F32),
            jax.ShapeDtypeStruct((2, 16, INNER_OWN), F32),
            jax.ShapeDtypeStruct((2, 16, OUT), F32),
            jax.ShapeDtypeStruct((2, 16, 1024), F32),
        ),
        in_specs=[vmem, vmem, vmem, pl.BlockSpec(memory_space=pltpu.SMEM), vmem, vmem, vmem],
        out_specs=(vmem,) * 6,
        scratch_shapes=scratch,
        compiler_params=pltpu.CompilerParams(
            collective_id=0, has_side_effects=True, vmem_limit_bytes=60 << 20
        ),
        name="whole_step",
    )(x_in, cotangent, own, lengths, vec, conv, head)


def finish_kernel(
    act_ref, gin_ref, gx_ref, gg_ref, go_ref, small_ref,
    act_out, grad_in, gain_in, w_zx, w_bc, w_dt, conv_x, conv_bc,
    bias_x, bias_bc, dt_bias, a_log, skip, gain_gate, w_out,
):
    w_out[...] = go_ref[...]
    act_out[...] = act_ref[...]
    grad_in[...] = gin_ref[...]
    w_bc[...] = gx_ref[:, :, INNER_OWN:SIGNAL]
    w_dt[...] = gx_ref[:, :, SIGNAL : SIGNAL + HEADS_OWN]
    channel = lax.broadcasted_iota(jnp.int32, (INNER_OWN, 128), 0) // 64
    head = lax.broadcasted_iota(jnp.int32, (INNER_OWN, 128), 1)
    members = (channel == head).astype(F32)
    for layer in range(2):
        for row in range(16):
            w_zx[layer, row, 0:1, :] = gg_ref[layer, row : row + 1, :]
            w_zx[layer, row, 1:2, :] = gx_ref[layer, row : row + 1, :INNER_OWN]
        one = slice(layer, layer + 1)
        gain_in[one, :] = small_ref[layer, 0:1, :]
        gain_gate[one, :] = small_ref[layer, 1:2, :]
        by_head = exact_dot(small_ref[layer], members)
        skip[one, :] = by_head[2:3, :HEADS_OWN]
        bias_x[one, :] = small_ref[layer, 3:4, :]
        conv_x[layer] = small_ref[layer, 4:8, :]
        for tap in range(4):
            conv_bc[layer, tap : tap + 1, :] = small_ref[layer, 8:9, tap * PAIR : (tap + 1) * PAIR]
        bias_bc[one, :] = small_ref[layer, 9:10, :PAIR]
        dt_bias[one, :] = small_ref[layer, 9:10, 256 : 256 + HEADS_OWN]
        a_log[one, :] = small_ref[layer, 9:10, 384 : 384 + HEADS_OWN]


def finish_step(*parts):
    shapes = [
        ((128, WIDTH), BF16), ((128, WIDTH), F32), ((2, WIDTH), F32), ((2, 16, 2, INNER_OWN), F32),
        ((2, 16, PAIR), F32), ((2, 16, HEADS_OWN), F32), ((2, 4, INNER_OWN), F32), ((2, 4, PAIR), F32),
        ((2, INNER_OWN), F32), ((2, PAIR), F32), ((2, HEADS_OWN), F32), ((2, HEADS_OWN), F32),
        ((2, HEADS_OWN), F32), ((2, INNER_OWN), F32), ((2, 16, INNER_OWN), F32),
    ]
    vmem = pl.BlockSpec(memory_space=pltpu.VMEM)
    return pl.pallas_call(
        finish_kernel,
        out_shape=[jax.ShapeDtypeStruct(*shape) for shape in shapes],
        in_specs=[vmem] * 6,
        out_specs=[vmem] * 15,
        compiler_params=pltpu.CompilerParams(vmem_limit_bytes=60 << 20),
        name="finish_step",
    )(*parts)


def pack_kernel(
    gain_in, w_zx, w_bc, w_dt, conv_x, conv_bc, bias_x, bias_bc, dt_bias, a_log, skip, gain_gate, w_out,
    own, vec, conv, head,
):
    heads = lax.broadcasted_iota(jnp.int32, (HEADS_OWN, INNER_OWN), 0)
    channel = lax.broadcasted_iota(jnp.int32, (HEADS_OWN, INNER_OWN), 1)
    members = jnp.where(heads == channel // 64, 1.0, 0.0)
    skips = exact_dot(skip[...].astype(F32), members)
    gains, gates = gain_in[...].astype(F32), gain_gate[...].astype(F32)
    shift_x, shift_bc = bias_x[...].astype(F32), bias_bc[...].astype(F32)
    sizes, rates = dt_bias[...].astype(F32), a_log[...].astype(F32)
    own[...] = jnp.zeros_like(own)
    vec[...] = jnp.zeros_like(vec)
    conv[...] = jnp.zeros_like(conv)
    head[...] = jnp.zeros_like(head)
    gate_at, out_at = XS, XS + INNER_OWN
    for layer in range(2):
        one = slice(layer, layer + 1)
        rows = [w_zx[layer, row].astype(F32) for row in range(16)]
        own[layer, :, :INNER_OWN] = jnp.concatenate([row[1:2] for row in rows], axis=0).astype(BF16)
        own[layer, :, INNER_OWN:SIGNAL] = w_bc[layer]
        own[layer, :, SIGNAL : SIGNAL + HEADS_OWN] = w_dt[layer]
        own[layer, :, gate_at:out_at] = jnp.concatenate([row[0:1] for row in rows], axis=0).astype(BF16)
        own[layer, :, out_at:] = w_out[layer]
        vec[layer, 0:1, :] = gains[one]
        vec[layer, 1:2, :] = gates[one]
        vec[layer, 2:3, :] = skips[one]
        conv[layer, 0:4, :INNER_OWN] = conv_x[layer].astype(F32)
        conv[layer, 0:4, INNER_OWN:] = conv_bc[layer].astype(F32)
        conv[layer, 4:5, :INNER_OWN] = shift_x[one]
        conv[layer, 4:5, INNER_OWN:] = shift_bc[one]
        head[layer, 0:1, :HEADS_OWN] = sizes[one]
        head[layer, 1:2, :HEADS_OWN] = rates[one]


def pack_step(*params):
    vmem = pl.BlockSpec(memory_space=pltpu.VMEM)
    return pl.pallas_call(
        pack_kernel,
        out_shape=[
            jax.ShapeDtypeStruct((2, 16, XS + INNER_OWN + OUT), BF16),
            jax.ShapeDtypeStruct((2, 8, WIDTH), F32),
            jax.ShapeDtypeStruct((2, 8, SIGNAL), F32),
            jax.ShapeDtypeStruct((2, 8, 128), F32),
        ],
        in_specs=[vmem] * 13,
        out_specs=[vmem] * 4,
        compiler_params=pltpu.CompilerParams(vmem_limit_bytes=60 << 20),
        name="pack_step",
    )(*params)


def shards(
    x_in, cotangent, seq_lengths, gain_in, w_zx, w_bc, w_dt, conv_x, conv_bc,
    bias_x, bias_bc, dt_bias, a_log, skip, gain_gate, w_out,
):
    own, vec, conv, head = pack_step(
        gain_in, w_zx, w_bc, w_dt, conv_x, conv_bc, bias_x, bias_bc,
        dt_bias, a_log, skip, gain_gate, jnp.swapaxes(w_out, 1, 2),
    )
    parts = whole_step(x_in, cotangent, own, seq_lengths, vec, conv, head)
    done = finish_step(*parts)
    return (*done[:-1], jnp.swapaxes(done[-1], 1, 2))


def solution(mesh):
    placed = (
        P(("fsdp", "tp"), None),
        P(("fsdp", "tp"), None),
        P("fsdp", None),
        P(),
        P(None, "fsdp", None, "tp"),
        P(None, "fsdp", None),
        P(None, "fsdp", "tp"),
        P(None, None, "tp"),
        P(),
        P(None, "tp"),
        P(),
        P(None, "tp"),
        P(None, "tp"),
        P(None, "tp"),
        P(None, "tp"),
        P(None, "tp", "fsdp"),
    )
    return jax.shard_map(
        shards,
        mesh=mesh,
        in_specs=placed,
        out_specs=(
            P(("fsdp", "tp"), None),
            P(("fsdp", "tp"), None),
            P(),
            P(None, "fsdp", None, "tp"),
            P(None, "fsdp", None),
            P(None, "fsdp", "tp"),
            P(None, None, "tp"),
            P(),
            P(None, "tp"),
            P(),
            P(None, "tp"),
            P(None, "tp"),
            P(None, "tp"),
            P(None, "tp"),
            P(None, "tp", "fsdp"),
        ),
        check_vma=False,
    )
```
